32 devices in a mesh: section: 2 (over core), batch: 16 (over z, y, x).
Axes of the slice: x: 2, y: 2, z: 4, core: 2. Of those that a mesh axis runs over, the one named last changes fastest.
Arguments:
- inputs: bfloat16 [2, 16, 64, 768], P(None, 'batch'), may hold values from -6 to 6
- cotangent: bfloat16 [2, 16, 64, 768], P(None, 'batch'), may hold values from -6 to 6
- segments: int32 [2, 16, 64], P(None, 'batch'), may hold values from 0 to 3, never falling along the last dimension, each value on 1 to 32 neighbouring positions
- row_widths: int32 [2, 16, 4], P(None, 'batch'), may hold values from 4 to 16
- w_qkv: bfloat16 [2, 768, 2304], P('section'), may hold values from -0.21875 to 0.21875
- w_out: bfloat16 [2, 768, 768], P('section'), may hold values from -0.625 to 0.625
- w_fc1: bfloat16 [2, 768, 3072], P('section'), may hold values from -0.21875 to 0.21875
- w_fc2: bfloat16 [2, 3072, 768], P('section'), may hold values from -0.109375 to 0.109375
- norm_gains: float32 [2, 4, 768], P('section'), may hold values from 0.25 to 1.75
- bias_rows: float32 [2, 6, 768], P('section'), may hold values from -4 to 4
- fc1_bias: float32 [2, 3072], P('section'), may hold values from -4 to 4
- rel_table: float32 [2, 12, 729], P('section'), may hold values from -6 to 6
Outputs:
- activations: bfloat16 [2, 2, 16, 64, 768], P('section', None, 'batch')
- input_grads: float32 [2, 2, 16, 64, 768], P('section', None, 'batch')
- grad_qkv: float32 [2, 768, 2304], P('section', 'batch')
- grad_out: float32 [2, 768, 768], P('section', 'batch')
- grad_fc1: float32 [2, 768, 3072], P('section', 'batch')
- grad_fc2: float32 [2, 3072, 768], P('section', 'batch')
- grad_gains: float32 [2, 4, 768], P('section')
- grad_biases: float32 [2, 6, 768], P('section')
- grad_fc1_bias: float32 [2, 3072], P('section')
- grad_table: float32 [2, 12, 729], P('section')
The draws below stay inside these ranges and needn't reach their ends.
Inputs may be any that keep to these rules, and one draw needn't show every extreme that they name: `segments`: along a packed row the numbers never fall and each of the 4 images has 1 to 32 slots; every image number occurs in every row.
All inputs are finite; a program needn't handle non-finite values.
Results may differ from the reference program's by a relative error of at most 0.02.
Values may be sent and summed in bfloat16 or wider, within the bound.
A program may use at most 256 MiB of HBM per device.

```python
import math
import jax
import jax.numpy as jnp
import numpy as np
from jax import lax

D = 768
HEADS = 12
HEAD = 64
FF = 3072
ROW = 64
MICRO = 2
IMAGES = 4
REACH = 13
RELS = 729
N_BATCH = 16


def touch_ends(array, stream_key, smallest, top_value):
    extent = array.shape
    place = [jax.random.randint(jax.random.fold_in(stream_key, axis), (), 0, extent[axis]) for axis in range(len(extent))]
    array = array.at[tuple(place)].set(smallest)
    longest = extent.index(max(extent))
    place[longest] = (place[longest] + 1) % extent[longest]
    return array.at[tuple(place)].set(top_value)


def block_levels(stream_key, shape, pieces, least, top_value):
    def one(axis_at, shards_of):
        draws = jax.random.uniform(jax.random.fold_in(jax.random.fold_in(stream_key, 6), axis_at), (shards_of,), jnp.float32, least / len(pieces), top_value / len(pieces))
        return jnp.repeat(jnp.exp(draws), shape[axis_at] // shards_of).reshape((-1,) + (1,) * (len(shape) - axis_at - 1))

    level = one(*pieces[0])
    for cut in pieces[1:]:
        level = level * one(*cut)
    return level


def profile(amount, total, bound, skew):
    loads = [(1 << 20) // math.isqrt(grade ** skew) + 1 for grade in range(2, amount + 1)]
    spare, given = total - bound - (amount - 1), [1] * (amount - 1)
    while spare > 0:
        movable = [i for i in range(amount - 1) if given[i] < bound]
        pool, budget = sum([loads[i] for i in movable]), spare
        for i in movable:
            addition = min(bound - given[i], max(1, budget * loads[i] // pool), spare)
            given[i] = given[i] + addition
            spare = spare - addition
    return np.array([bound] + given)


def ragged_sizes(own_key, amount, total, most, skew):
    if amount == 2:
        one = jax.random.randint(own_key, (), max(1, total - most), min(most, total - 1) + 1)
        return jnp.stack([one, total - one])
    tallies = jnp.asarray(profile(amount, total, most, skew), jnp.int32)
    couples = (amount - 1) // 2
    source_of, taker = tallies[1:1 + 2 * couples:2], tallies[2:2 + 2 * couples:2]
    room = jnp.minimum(source_of - 1, most - taker)
    shifted = jax.random.randint(jax.random.fold_in(own_key, 1), (couples,), 0, 1 << 20) % (room + 1)
    tallies = tallies.at[1:1 + 2 * couples:2].set(source_of - shifted).at[2:2 + 2 * couples:2].set(taker + shifted)
    return tallies[jax.random.permutation(jax.random.fold_in(own_key, 2), amount)]


def bell_draw(rng, shape, spread, limit, pieces=(), kind=jnp.bfloat16):
    array = jax.random.normal(rng, shape, jnp.float32) * spread
    if len(pieces) > 0:
        array = block_levels(rng, shape, pieces, -0.22, 0.18) * array
    return jnp.clip(array, min=-limit, max=limit).astype(kind)


def setup_inputs(seed: int = 0) -> dict:
    keys = jax.random.split(jax.random.key(seed), 13)
    return {
        "inputs": bell_draw(keys[0], (MICRO, N_BATCH, ROW, D), 1.0, 6.0, ((1, 16),)),
        "cotangent": bell_draw(keys[1], (MICRO, N_BATCH, ROW, D), 1.0, 6.0, ((1, 16),)),
        "segments": jax.vmap(lambda own: jnp.searchsorted(jnp.cumsum(ragged_sizes(own, IMAGES, ROW, ROW // 2, 1)), jnp.arange(ROW), side="right"))(jax.random.split(keys[2], MICRO * N_BATCH)).reshape((MICRO, N_BATCH, ROW)).astype(jnp.int32),
        "row_widths": touch_ends(jax.random.randint(keys[3], (MICRO, N_BATCH, IMAGES), 4, 17), jax.random.fold_in(keys[3], 1), 4, 16).astype(jnp.int32),
        "w_qkv": bell_draw(keys[4], (2, D, 3 * D), D ** -0.5, 0.21875, ((0, 2),)),
        "w_out": bell_draw(keys[5], (2, D, D), (D // 8) ** -0.5, 0.625, ((0, 2),)),
        "w_fc1": bell_draw(keys[6], (2, D, FF), D ** -0.5, 0.21875, ((0, 2),)),
        "w_fc2": bell_draw(keys[7], (2, FF, D), FF ** -0.5, 0.109375, ((0, 2),)),
        "norm_gains": jnp.clip(1.0 + 0.15 * jax.random.normal(keys[8], (2, 4, D), jnp.float32), 0.25, 1.75),
        "bias_rows": bell_draw(keys[9], (2, 6, D), 0.3, 4.0, ((0, 2),), jnp.float32),
        "fc1_bias": bell_draw(keys[10], (2, FF), 0.3, 4.0, ((0, 2),), jnp.float32),
        "rel_table": bell_draw(keys[11], (2, HEADS, RELS), 1.0, 6.0, ((0, 2),), jnp.float32),
    }


@jax.custom_vjp
def low(v):
    return lax.optimization_barrier(v.astype(jnp.bfloat16)).astype(jnp.float32)

@jax.custom_vjp
def low_back(v):
    return v

def low_keep(v):
    return (low(v), None)

def low_pass(kept, grad):
    return (grad,)

def back_keep(v):
    return (v, None)

def back_low(kept, grad):
    return (low(grad),)
low.defvjp(low_keep, low_pass)
low_back.defvjp(back_keep, back_low)
NORM_EPS = 1e-06
PRECISE = lax.Precision.HIGHEST

def norm_rows(values_in, gain_row, shift_row):
    row_mean = lax.optimization_barrier(jnp.mean(values_in, axis=-1, keepdims=True))
    centered = values_in - row_mean
    variance = lax.optimization_barrier(jnp.mean(centered * centered, axis=-1, keepdims=True))
    return centered * lax.rsqrt(variance + NORM_EPS) * gain_row + shift_row

def geometry(segment_row, width_row):
    slot_ids = jnp.arange(segment_row.shape[0], dtype=jnp.int32)
    same_image = segment_row[:, None] == segment_row[None, :]
    before = lax.optimization_barrier(jnp.sum((segment_row[None, :] < segment_row[:, None]).astype(jnp.int32), axis=1))
    place_in = slot_ids - before
    one_hot = (segment_row[:, None] == jnp.arange(width_row.shape[0], dtype=jnp.int32)[None, :]).astype(jnp.int32)
    img_width = lax.optimization_barrier(jnp.sum(one_hot * width_row[None, :], axis=1))
    grid_row = place_in // img_width
    column = place_in % img_width
    row_step = jnp.clip(grid_row[:, None] - grid_row[None, :], -REACH, REACH) + REACH
    col_step = jnp.clip(column[:, None] - column[None, :], -REACH, REACH) + REACH
    rel_index = (row_step * (2 * REACH + 1) + col_step).astype(jnp.int32)
    return (same_image, rel_index)

def layer(layer_in, weights, same_image, rel_index):
    w_qkv, w_out, w_fc1, w_fc2, norm_gains, bias_rows, fc1_bias, pos_table = weights
    slot_count = layer_in.shape[0]
    normed = low(norm_rows(layer_in, norm_gains[0], bias_rows[0]))
    qkv_bias = jnp.concatenate([bias_rows[1], jnp.zeros_like(bias_rows[1]), bias_rows[2]])
    qkv_rows = low_back(low(jnp.dot(normed, w_qkv, precision=PRECISE) + qkv_bias))
    qkv_split = qkv_rows.reshape(slot_count, 3, HEADS, HEAD)
    queries, key_rows, values = (qkv_split[:, 0], qkv_split[:, 1], qkv_split[:, 2])
    raw_scores = low_back(jnp.einsum('qhd,khd->hqk', queries, key_rows, precision=PRECISE))
    pos_bias = jnp.take(pos_table, rel_index, axis=1)
    scores = jnp.where(same_image[None], raw_scores * 0.125 + pos_bias, -1e+30)
    row_max = lax.optimization_barrier(jnp.max(scores, axis=-1, keepdims=True))
    exp_scores = jnp.exp(scores - row_max)
    att_probs = exp_scores / lax.optimization_barrier(jnp.sum(exp_scores, axis=-1, keepdims=True))
    mixed_out = jnp.einsum('hqk,khd->qhd', low(att_probs), values, precision=PRECISE).reshape(slot_count, D)
    mixed_out = low_back(low(mixed_out))
    att_out = low_back(jnp.dot(mixed_out, w_out, precision=PRECISE) + bias_rows[3])
    middle = layer_in + norm_gains[1] * att_out
    second = low(norm_rows(middle, norm_gains[2], bias_rows[4]))
    hidden = low_back(jnp.dot(second, w_fc1, precision=PRECISE) + fc1_bias)
    active = low(jax.nn.gelu(hidden, approximate=False))
    branch = low_back(jnp.dot(active, w_fc2, precision=PRECISE) + bias_rows[5])
    return middle + norm_gains[3] * branch

def reference(inputs, cotangent, segments, row_widths, w_qkv, w_out, w_fc1, w_fc2, norm_gains, bias_rows, fc1_bias, rel_table):
    params = (w_qkv.astype(jnp.float32), w_out.astype(jnp.float32), w_fc1.astype(jnp.float32), w_fc2.astype(jnp.float32), norm_gains.astype(jnp.float32), bias_rows.astype(jnp.float32), fc1_bias.astype(jnp.float32), rel_table.astype(jnp.float32))
    row_total = MICRO * N_BATCH
    flat_inputs = inputs.reshape(row_total, ROW, D)
    flat_cot = cotangent.reshape(row_total, ROW, D)
    flat_seg = segments.reshape(row_total, ROW)
    flat_wid = row_widths.reshape(row_total, IMAGES)

    def one_row(totals, packed):
        row_in, row_cot, row_seg, row_wid = packed
        same_image, rel_index = geometry(row_seg, row_wid)

        def network(start, probe, weights):
            lower = tuple((item[0] for item in weights))
            upper = tuple((item[1] for item in weights))
            first_out = layer(start, lower, same_image, rel_index)
            handed = low_back(low(first_out)) + probe
            return (first_out, layer(handed, upper, same_image, rel_index))
        start = row_in.astype(jnp.float32)
        outputs, pullback = jax.vjp(network, start, jnp.zeros_like(start), params)
        first_out, last_out = outputs
        d_start, d_probe, d_params = pullback((jnp.zeros_like(first_out), row_cot.astype(jnp.float32)))
        totals = tuple((left_val + right_val for left_val, right_val in zip(totals, d_params)))
        return (totals, (first_out.astype(jnp.bfloat16), last_out.astype(jnp.bfloat16), d_start, d_probe))
    zero_grads = tuple((jnp.zeros(item.shape, jnp.float32) for item in params))
    totals, stacked = lax.scan(one_row, zero_grads, (flat_inputs, flat_cot, flat_seg, flat_wid))
    out_one, out_two, grad_one, grad_two = stacked
    full_shape = (MICRO, N_BATCH, ROW, D)
    activations = jnp.stack([out_one.reshape(full_shape), out_two.reshape(full_shape)])
    input_grads = jnp.stack([grad_one.reshape(full_shape), grad_two.reshape(full_shape)])
    return (activations, input_grads, totals[0], totals[1], totals[2], totals[3], totals[4], totals[5], totals[6], totals[7])
```

```python
import functools

import jax
import jax.numpy as jnp
from jax import lax
from jax.experimental import pallas as pl
from jax.experimental.pallas import tpu as pltpu
from jax.sharding import PartitionSpec as P

MESH = pl.DeviceIdType.MESH
F32 = jnp.float32
BF16 = jnp.bfloat16
REACH = 13
SPAN = 2 * REACH + 1
NORM_EPS = 1e-06
ROOT_HALF = 0.7071067811865476
INV_ROOT_TWO_PI = 0.3989422804014327
COLS = 256
GRID_ROWS = 8
GRID_COLS = 16
PITCH = 2 * GRID_COLS
WIDE = 2 * GRID_ROWS * PITCH
HALF = WIDE // 2


def nn(left, right):
    return lax.dot_general(left, right, (((1,), (0,)), ((), ())), preferred_element_type=F32)


def nt(left, right):
    return lax.dot_general(left, right, (((1,), (1,)), ((), ())), preferred_element_type=F32)


def tn(left, right):
    return lax.dot_general(left, right, (((0,), (0,)), ((), ())), preferred_element_type=F32)


def iota(shape, dim):
    return lax.broadcasted_iota(jnp.int32, shape, dim)


def two_parts(value):
    high = value.astype(BF16)
    return high, (value - high.astype(F32)).astype(BF16)


def norm_parts(values_in):
    row_mean = jnp.mean(values_in, axis=-1, keepdims=True)
    centered = values_in - row_mean
    inv_scale = lax.rsqrt(jnp.mean(centered * centered, axis=-1, keepdims=True) + NORM_EPS)
    return centered * inv_scale, inv_scale


def norm_back(upstream, normal_in, inv_scale):
    return inv_scale * (
        upstream
        - jnp.mean(upstream, axis=-1, keepdims=True)
        - normal_in * jnp.mean(upstream * normal_in, axis=-1, keepdims=True)
    )


def col_sum(value):
    return jnp.sum(value, axis=0, keepdims=True)


def chunk_loop(count, body):
    def step(index, carry):
        body(index)
        return carry

    lax.fori_loop(0, count, step, 0)


def cols_of(index, size=COLS):
    return pl.ds(pl.multiple_of(index * size, size), size)


def geometry(seg, wid, same, pick_q, pick_k, pick_kt, pick_qt):
    micro, slots = seg.shape
    tokens = micro * slots
    images = wid.shape[1]
    seg_f = seg[...].astype(F32)
    seg_row = jnp.concatenate(
        [seg_f[m : m + 1, :] + float(m * images) for m in range(micro)], axis=1
    )
    sub = iota((tokens, tokens), 0)
    lane = iota((tokens, tokens), 1)
    seg_col = jnp.sum(jnp.where(sub == lane, seg_row, 0.0), axis=1, keepdims=True)
    same[...] = (seg_col == seg_row).astype(F32)
    before_row = jnp.sum((seg_col < seg_row).astype(F32), axis=0, keepdims=True)
    before_col = jnp.sum((seg_row < seg_col).astype(F32), axis=1, keepdims=True)
    place_row = iota((1, tokens), 1).astype(F32) - before_row
    place_col = iota((tokens, 1), 0).astype(F32) - before_col
    width_row = jnp.zeros((1, tokens), F32)
    width_col = jnp.zeros((tokens, 1), F32)
    for m in range(micro):
        for image in range(images):
            width = wid[m, image].astype(F32)
            number = float(m * images + image)
            width_row = width_row + jnp.where(seg_row == number, width, 0.0)
            width_col = width_col + jnp.where(seg_col == number, width, 0.0)

    def grid(place, width):
        row = jnp.zeros_like(place)
        for k in range(1, GRID_ROWS):
            row = row + (place >= float(k) * width).astype(F32)
        return row, place - row * width

    row_r, col_r = grid(place_row, width_row)
    row_c, col_c = grid(place_col, width_col)
    cells = GRID_ROWS * GRID_COLS
    pick_q[...] = (iota((tokens, cells), 1).astype(F32) == row_c * GRID_COLS + col_c).astype(
        F32
    ).astype(BF16)
    pick_qt[...] = (
        iota((cells, tokens), 0).astype(F32) == row_r * GRID_COLS + (GRID_COLS - 1.0) - col_r
    ).astype(F32).astype(BF16)
    pick_k[...] = (iota((tokens, HALF), 1).astype(F32) == row_c * PITCH + col_c).astype(
        F32
    ).astype(BF16)
    pick_kt[...] = (iota((HALF, tokens), 0).astype(F32) == row_r * PITCH + col_r).astype(
        F32
    ).astype(BF16)


def spread_table(table, padded, spread, wide_table):
    heads, rels = table.shape
    padded[...] = jnp.zeros_like(padded)
    padded[0:heads, 0:rels] = table[...]
    shape = spread.shape
    where = iota((1, WIDE), 1)
    signed = jnp.where(where < HALF, where, where - WIDE)
    row_step = (signed + GRID_COLS + WIDE) // PITCH - WIDE // PITCH
    col_step = signed - row_step * PITCH
    entry = (REACH - row_step) * SPAN + jnp.clip(-col_step, -REACH, REACH) + REACH
    spread[...] = (iota(shape, 0) == entry).astype(F32).astype(BF16)
    high, low = two_parts(padded[...])
    vector = nn(high, spread[...]) + nn(low, spread[...])
    cells = GRID_ROWS * GRID_COLS
    for head in range(heads):
        line = jnp.broadcast_to(vector[head : head + 1, :], (GRID_COLS, WIDE))
        line = pltpu.roll(line, 0, 1, stride=1, stride_axis=0)
        for low_row in range(4):
            turned = line if low_row == 0 else pltpu.roll(line, low_row * PITCH, 1)
            for high_row in range(GRID_ROWS // 4):
                if high_row == 0:
                    part = turned[:, 0:HALF]
                else:
                    part = jnp.concatenate(
                        [turned[:, WIDE - 4 * PITCH : WIDE], turned[:, 0 : HALF - 4 * PITCH]], axis=1
                    )
                top = (high_row * 4 + low_row) * GRID_COLS
                part_high, part_low = two_parts(part)
                wide_table[top : top + GRID_COLS, head * HALF : (head + 1) * HALF] = part_high
                wide_table[
                    cells + top : cells + top + GRID_COLS, head * HALF : (head + 1) * HALF
                ] = part_low


def fold_table(head_grad):
    total = None
    for low_row in range(4):
        near = head_grad[low_row * GRID_COLS : (low_row + 1) * GRID_COLS, :]
        far = head_grad[(low_row + 4) * GRID_COLS : (low_row + 5) * GRID_COLS, :]
        step = 4 * PITCH
        laid = jnp.concatenate(
            [
                near[:, 0:step] + far[:, step : 2 * step],
                near[:, step : 2 * step],
                jnp.zeros((GRID_COLS, step), F32),
                far[:, 0:step],
            ],
            axis=1,
        )
        if low_row > 0:
            laid = pltpu.roll(laid, WIDE - low_row * PITCH, 1)
        total = laid if total is None else total + laid
    total = pltpu.roll(total, WIDE - (GRID_COLS - 1), 1, stride=1, stride_axis=0)
    return col_sum(total)


def block_kernel(
    inputs,
    cotangent,
    seg,
    wid,
    wqkv_in,
    wout_in,
    wfc1_in,
    wfc2_in,
    gains,
    biases,
    fc1_bias,
    table,
    activation,
    grad_in,
    at_small,
    at_active,
    b_all,
    small,
    wqkv,
    wout,
    wfc1,
    wfc2,
    arrived,
    leaving,
    stream,
    hat_one,
    hat_two,
    att_out,
    branch,
    d_middle,
    d_wide,
    normed,
    qkv,
    probs,
    bias,
    mixed,
    d_mixed,
    second,
    active,
    slope,
    same,
    pick_q,
    pick_k,
    pick_kt,
    pick_qt,
    padded,
    spread,
    wide_table,
    folded,
    scale_one,
    scale_two,
    weight_sem,
    send_sem,
    recv_sem,
):
    section = lax.axis_index("section")
    place = lax.axis_index("batch")
    other = (1 - section, place)
    width = inputs.shape[1]
    tokens = inputs.shape[0]
    ff = active.shape[1]
    heads = table.shape[0]
    pair = 2 * (width // heads)
    pairs = heads // 2
    parts = ff // width
    per_part = width // COLS

    loads = [
        pltpu.make_async_copy(source.at[0], target, weight_sem.at[index])
        for index, (source, target) in enumerate(
            [(wqkv_in, wqkv), (wout_in, wout), (wfc1_in, wfc1), (wfc2_in, wfc2)]
        )
    ]
    for load in loads:
        load.start()

    barrier = pltpu.get_barrier_semaphore()
    pl.semaphore_signal(barrier, inc=1, device_id=other, device_id_type=MESH)

    geometry(seg, wid, same, pick_q, pick_k, pick_kt, pick_qt)
    spread_table(table, padded, spread, wide_table)
    cells = GRID_ROWS * GRID_COLS

    def bias_of(head):
        where = cols_of(head, HALF)
        high = nn(pick_q[...], wide_table[0:cells, where]).astype(BF16)
        low = nn(pick_q[...], wide_table[cells : 2 * cells, where]).astype(BF16)
        bias[cols_of(head, tokens), :] = nn(high, pick_kt[...]) + nn(low, pick_kt[...])

    chunk_loop(heads, bias_of)

    pl.semaphore_wait(barrier, 1)

    def relay(source):
        return pltpu.make_async_remote_copy(
            src_ref=source,
            dst_ref=arrived,
            send_sem=send_sem,
            recv_sem=recv_sem,
            device_id=other,
            device_id_type=MESH,
        )

    @pl.when(section == 0)
    def _():
        stream[...] = inputs[...].astype(F32)

    @pl.when(section == 1)
    def _():
        relay(activation).wait_recv()
        stream[...] = arrived[...].astype(F32)

    hat, inv_scale = norm_parts(stream[...])
    hat_one[...] = hat
    scale_one[...] = inv_scale
    normed[...] = (hat * gains[0, 0:1, :] + biases[0, 0:1, :]).astype(BF16)
    loads[0].wait()
    for third in range(3):

        def project(index):
            out = nn(normed[...], wqkv[:, cols_of(third * per_part + index)])
            if third != 1:
                row = 1 if third == 0 else 2
                out = out + biases[0, row : row + 1, cols_of(index)]
            qkv[third, :, cols_of(index)] = out.astype(BF16)

        chunk_loop(per_part, project)

    lane = iota((1, pair), 1)
    low_lanes = (lane < pair // 2).astype(F32).astype(BF16)
    high_lanes = (lane >= pair // 2).astype(F32).astype(BF16)

    def stacked(value):
        return jnp.concatenate([value * low_lanes, value * high_lanes], axis=0)

    def side_by_side(value):
        return jnp.concatenate([value[0:tokens, :], value[tokens : 2 * tokens, :]], axis=1)

    for index in range(pairs):
        at = slice(index * pair, (index + 1) * pair)
        rows = slice(index * 2 * tokens, (index + 1) * 2 * tokens)
        raw = nt(stacked(qkv[0, :, at]), qkv[1, :, at])
        mask = jnp.concatenate([same[...], same[...]], axis=0) > 0.5
        scores = jnp.where(mask, raw * 0.125 + bias[rows, :], -1e30)
        exped = jnp.exp(scores - jnp.max(scores, axis=-1, keepdims=True))
        prob = exped / jnp.sum(exped, axis=-1, keepdims=True)
        probs[rows, :] = prob
        mixed[:, at] = nn(side_by_side(prob.astype(BF16)), stacked(qkv[2, :, at])).astype(BF16)

    loads[1].wait()

    def attend_out(index):
        at = cols_of(index)
        out = nn(mixed[...], wout[:, at]) + biases[0, 3:4, at]
        att_out[:, at] = out
        stream[:, at] = stream[:, at] + gains[0, 1:2, at] * out

    chunk_loop(per_part, attend_out)
    hat, inv_scale = norm_parts(stream[...])
    hat_two[...] = hat
    scale_two[...] = inv_scale
    second[...] = (hat * gains[0, 2:3, :] + biases[0, 4:5, :]).astype(BF16)
    loads[2].wait()

    def feed(index):
        at = cols_of(index)
        hidden = nn(second[...], wfc1[:, at]) + fc1_bias[0:1, at]
        cumul = 0.5 * (1.0 + lax.erf(hidden * ROOT_HALF))
        density = jnp.exp(-0.5 * hidden * hidden) * INV_ROOT_TWO_PI
        active[:, at] = (hidden * cumul).astype(BF16)
        slope[:, at] = cumul + hidden * density

    chunk_loop(ff // COLS, feed)
    loads[3].wait()

    def feed_out(index):
        at = cols_of(index)
        out = nn(active[...], wfc2[:, at]) + biases[0, 5:6, at]
        branch[:, at] = out
        activation[:, at] = (stream[:, at] + gains[0, 3:4, at] * out).astype(BF16)

    chunk_loop(per_part, feed_out)

    def turn():
        def turn_small(index):
            at = cols_of(index, 128)
            for number, source in enumerate((second, normed, mixed)):
                at_small[number, at, :] = source[:, at].T

        def turn_active(index):
            at = cols_of(index, 128)
            at_active[at, :] = active[:, at].T

        chunk_loop(width // 128, turn_small)
        chunk_loop(ff // 128, turn_active)

    @pl.when(section == 0)
    def _():
        relay(activation).start()
        turn()
        relay(activation).wait_send()
        relay(activation).wait_recv()
        stream[...] = arrived[...].astype(F32)

    @pl.when(section == 1)
    def _():
        stream[...] = cotangent[...].astype(F32)

    small[...] = jnp.zeros_like(small)
    upstream = stream[...]
    small[3:4, :] = col_sum(upstream * branch[...])
    d_branch = (gains[0, 3:4, :] * upstream).astype(BF16)
    b_all[parts + 4] = d_branch
    small[9:10, :] = col_sum(d_branch.astype(F32))

    def feed_back(index):
        at = cols_of(index)
        out = nt(b_all[parts + 4], wfc2[at, :])
        d_hidden = (out * slope[:, at]).astype(BF16)
        part = index // per_part
        inner = cols_of(index % per_part)
        b_all[part, :, inner] = d_hidden
        small[pl.ds(10 + part, 1), inner] = col_sum(d_hidden.astype(F32))

    chunk_loop(ff // COLS, feed_back)

    def second_back(index):
        at = cols_of(index)
        out = nt(b_all[0], wfc1[at, 0:width])
        for part in range(1, parts):
            out = out + nt(b_all[part], wfc1[at, part * width : (part + 1) * width])
        d_wide[:, at] = out

    chunk_loop(per_part, second_back)
    d_second = d_wide[...]
    small[2:3, :] = col_sum(d_second * hat_two[...])
    small[8:9, :] = col_sum(d_second)
    d_mid = stream[...] + norm_back(d_second * gains[0, 2:3, :], hat_two[...], scale_two[...])
    d_middle[...] = d_mid
    small[1:2, :] = col_sum(d_mid * att_out[...])
    d_att = (gains[0, 1:2, :] * d_mid).astype(BF16)
    b_all[parts + 3] = d_att
    small[7:8, :] = col_sum(d_att.astype(F32))

    def out_back(index):
        at = cols_of(index)
        d_mixed[:, at] = nt(b_all[parts + 3], wout[at, :]).astype(BF16)

    chunk_loop(per_part, out_back)

    folded[...] = jnp.zeros_like(folded)
    for index in range(pairs):
        at = slice(index * pair, (index + 1) * pair)
        rows = slice(index * 2 * tokens, (index + 1) * 2 * tokens)
        prob = probs[rows, :]
        d_mix = stacked(d_mixed[:, at])
        d_prob = nt(d_mix, qkv[2, :, at])
        b_all[parts + 2, :, at] = tn(prob.astype(BF16), d_mix).astype(BF16)
        d_scores = prob * (d_prob - jnp.sum(prob * d_prob, axis=-1, keepdims=True))
        d_raw = (0.125 * d_scores).astype(BF16)
        b_all[parts, :, at] = nn(side_by_side(d_raw), stacked(qkv[1, :, at])).astype(BF16)
        b_all[parts + 1, :, at] = tn(d_raw, stacked(qkv[0, :, at])).astype(BF16)
        high, low = two_parts(d_scores)
        high = nn(high, pick_k[...]).astype(BF16)
        low = nn(low, pick_k[...]).astype(BF16)
        for side in range(2):
            own = slice(side * tokens, (side + 1) * tokens)
            head_grad = nn(pick_qt[...], high[own, :]) + nn(pick_qt[...], low[own, :])
            folded[2 * index + side : 2 * index + side + 1, :] = fold_table(head_grad)

    small[5:6, :] = col_sum(b_all[parts].astype(F32))
    small[6:7, :] = col_sum(b_all[parts + 2].astype(F32))

    def normed_back(index):
        at = cols_of(index)
        out = nt(b_all[parts], wqkv[at, 0:width])
        for third in range(1, 3):
            out = out + nt(b_all[parts + third], wqkv[at, third * width : (third + 1) * width])
        d_wide[:, at] = out

    chunk_loop(per_part, normed_back)
    d_normed = d_wide[...]
    small[0:1, :] = col_sum(d_normed * hat_one[...])
    small[4:5, :] = col_sum(d_normed)
    d_in = d_middle[...] + norm_back(d_normed * gains[0, 0:1, :], hat_one[...], scale_one[...])
    grad_in[...] = d_in
    leaving[...] = d_in.astype(BF16)

    @pl.when(section == 1)
    def _():
        relay(leaving).start()
        turn()

    high, low = two_parts(folded[...])
    small[16:32, :] = nt(high, spread[...]) + nt(low, spread[...])

    @pl.when(section == 1)
    def _():
        relay(leaving).wait_send()


def run_block(inputs, cotangent, seg, wid, weights):
    w_qkv, w_out, w_fc1, w_fc2, gains, biases, fc1_bias, table = weights
    tokens, width = inputs.shape
    ff = w_fc1.shape[2]
    heads, rels = table.shape[1:]
    parts = ff // width
    cells = GRID_ROWS * GRID_COLS
    whole = pl.BlockSpec(memory_space=pltpu.VMEM)
    vm = pltpu.VMEM
    padded_rels = -(-rels // 256) * 256
    return pl.pallas_call(
        block_kernel,
        out_shape=(
            jax.ShapeDtypeStruct((tokens, width), BF16),
            jax.ShapeDtypeStruct((tokens, width), F32),
            jax.ShapeDtypeStruct((3, width, tokens), BF16),
            jax.ShapeDtypeStruct((ff, tokens), BF16),
            jax.ShapeDtypeStruct((parts + 5, tokens, width), BF16),
            jax.ShapeDtypeStruct((32, width), F32),
        ),
        in_specs=[whole, whole, whole, pl.BlockSpec(memory_space=pltpu.SMEM)]
        + [pl.BlockSpec(memory_space=pl.ANY)] * 4
        + [whole] * 4,
        out_specs=(whole,) * 6,
        scratch_shapes=[
            vm(w_qkv.shape[1:], BF16),
            vm(w_out.shape[1:], BF16),
            vm(w_fc1.shape[1:], BF16),
            vm(w_fc2.shape[1:], BF16),
            vm((tokens, width), BF16),
            vm((tokens, width), BF16),
        ]
        + [vm((tokens, width), F32)] * 7
        + [
            vm((tokens, width), BF16),
            vm((3, tokens, width), BF16),
            vm((heads * tokens, tokens), F32),
            vm((heads * tokens, tokens), F32),
            vm((tokens, width), BF16),
            vm((tokens, width), BF16),
            vm((tokens, width), BF16),
            vm((tokens, ff), BF16),
            vm((tokens, ff), F32),
            vm((tokens, tokens), F32),
            vm((tokens, cells), BF16),
            vm((tokens, HALF), BF16),
            vm((HALF, tokens), BF16),
            vm((cells, tokens), BF16),
            vm((16, padded_rels), F32),
            vm((padded_rels, WIDE), BF16),
            vm((2 * cells, heads * HALF), BF16),
            vm((16, WIDE), F32),
            vm((tokens, 1), F32),
            vm((tokens, 1), F32),
            pltpu.SemaphoreType.DMA((4,)),
            pltpu.SemaphoreType.DMA,
            pltpu.SemaphoreType.DMA,
        ],
        compiler_params=pltpu.CompilerParams(
            collective_id=0, has_side_effects=True, vmem_limit_bytes=56 * 2**20
        ),
        name="block",
    )(inputs, cotangent, seg, wid, w_qkv, w_out, w_fc1, w_fc2, gains, biases, fc1_bias, table[0])


UNIT_LEFT = (0, 0, 0, 0, 1, 1, 1, 2)


def share_kernel(
    at_small,
    at_active,
    b_all,
    small,
    g_qkv,
    g_out,
    g_fc1,
    g_fc2,
    g_gains,
    g_biases,
    g_fc1_bias,
    g_table,
    left,
    right,
    left_four,
    right_four,
    y_send,
    y_recv,
    totals,
    passing,
    inward,
    small_own,
    small_recv,
    own_sem,
    x_send_sem,
    x_recv_sem,
    y_send_sem,
    y_recv_sem,
    four_send_sem,
    four_recv_sem,
    z_send_sem,
    z_recv_sem,
    small_send_sem,
    small_recv_sem,
):
    section = lax.axis_index("section")
    place = lax.axis_index("batch")
    z = place // 4
    y = (place // 2) % 2
    x = place % 2
    x_peer = z * 4 + y * 2 + (1 - x)
    y_peer = z * 4 + (1 - y) * 2 + x
    xy_peer = z * 4 + (1 - y) * 2 + (1 - x)
    at_end = (z == 0) | (z == 3)
    lower = z < 2
    in_peer = jnp.where(lower, place + 4, place - 4)
    out_peer = jnp.where(z == 1, place - 4, place + 4)
    out_peer = jnp.where(at_end, place, out_peer)
    far_z = jnp.where(lower, z + 2, z - 2)
    far_peer = far_z * 4 + y * 2 + x
    pair_peer = jnp.where(z % 2 == 0, place + 4, place - 4)
    units = len(UNIT_LEFT)
    tokens = b_all.shape[1]
    rows = left.shape[3]
    width = right.shape[2]

    def remote(source, target, send, recv, peer):
        return pltpu.make_async_remote_copy(
            src_ref=source,
            dst_ref=target,
            send_sem=send,
            recv_sem=recv,
            device_id=(section, peer),
            device_id_type=MESH,
        )

    barrier = pltpu.get_barrier_semaphore()

    def greet(peer):
        pl.semaphore_signal(barrier, inc=1, device_id=(section, peer), device_id_type=MESH)

    for peer in (x_peer, y_peer, xy_peer, in_peer, far_peer):
        greet(peer)

    @pl.when(jnp.logical_not(at_end))
    def _():
        greet(out_peer)

    own = []
    for number in range(3):
        own.append(
            pltpu.make_async_copy(
                at_small.at[number, :, :, x],
                left.at[number, :, :, :, 0:tokens],
                own_sem.at[number],
            )
        )
    own.append(
        pltpu.make_async_copy(
            b_all.at[0:units], right.at[:, 0:tokens, :], own_sem.at[3]
        )
    )
    own.append(
        pltpu.make_async_copy(at_active.at[:, y, x], left_four.at[:, :, 0:tokens], own_sem.at[4])
    )
    own.append(
        pltpu.make_async_copy(b_all.at[units], right_four.at[0:tokens, :], own_sem.at[5])
    )
    for copy in own:
        copy.start()
    small_own[0] = small[...]

    @pl.when(at_end)
    def _():
        pl.semaphore_wait(barrier, 5)

    @pl.when(jnp.logical_not(at_end))
    def _():
        pl.semaphore_wait(barrier, 6)

    def send_four(slot, peer_y, peer_x, peer):
        lanes = slice(slot * tokens, (slot + 1) * tokens)
        return (
            remote(
                at_active.at[:, peer_y, peer_x],
                left_four.at[:, :, lanes],
                four_send_sem.at[0, slot],
                four_recv_sem.at[0, slot],
                peer,
            ),
            remote(
                b_all.at[units],
                right_four.at[lanes, :],
                four_send_sem.at[1, slot],
                four_recv_sem.at[1, slot],
                peer,
            ),
        )

    four = (
        send_four(1, y, 1 - x, x_peer)
        + send_four(2, 1 - y, x, y_peer)
        + send_four(3, 1 - y, 1 - x, xy_peer)
    )
    x_left = [
        remote(
            at_small.at[number, :, :, 1 - x],
            left.at[number, :, :, :, tokens : 2 * tokens],
            x_send_sem.at[units + number],
            x_recv_sem.at[units + number],
            x_peer,
        )
        for number in range(3)
    ]
    x_right = [
        remote(
            b_all.at[unit],
            right.at[unit, tokens : 2 * tokens, :],
            x_send_sem.at[unit],
            x_recv_sem.at[unit],
            x_peer,
        )
        for unit in range(units)
    ]
    small_peers = (x_peer, y_peer, pair_peer, far_peer)
    small_copy = [
        remote(
            small_own.at[step],
            small_recv.at[step],
            small_send_sem.at[step],
            small_recv_sem.at[step],
            small_peers[step],
        )
        for step in range(4)
    ]
    small_copy[0].start()
    x_left[0].start()
    x_right[0].start()
    for copy in four[2:4]:
        copy.start()
    x_right[1].start()
    for copy in four[4:6]:
        copy.start()
    x_right[2].start()
    x_right[3].start()
    for copy in four[0:2]:
        copy.start()
    x_left[1].start()
    for unit in (4, 5, 6):
        x_right[unit].start()
    x_left[2].start()
    x_right[7].start()

    y_copy = [
        remote(
            y_send.at[unit],
            y_recv.at[unit],
            y_send_sem.at[unit],
            y_recv_sem.at[unit],
            y_peer,
        )
        for unit in range(units)
    ]
    order = [0, 1, 2, 3, 8, 4, 9, 5, 10, 6, 11, 7]
    for copy in own:
        copy.wait()
    waited = set()

    def product(unit, side):
        lhs = left[UNIT_LEFT[unit], :, side].reshape(4 * rows, 2 * tokens)
        return nn(lhs, right[unit])

    def first(unit):
        if unit >= units:
            if not waited & {"four"}:
                waited.add("four")
                for copy in four:
                    copy.wait_recv()
            return
        if UNIT_LEFT[unit] not in waited:
            waited.add(UNIT_LEFT[unit])
            x_left[UNIT_LEFT[unit]].wait_recv()
        x_right[unit].wait_recv()
        y_send[unit] = product(unit, 1 - y).astype(BF16).reshape(4, rows, width)
        y_copy[unit].start()

    def z_copy(unit, dest, peer, final_inside):
        target = inward.at[unit] if final_inside else passing.at[unit, dest]
        slot = 4 if final_inside else dest
        return remote(
            totals.at[unit, dest],
            target,
            z_send_sem.at[unit, dest],
            z_recv_sem.at[unit, slot],
            peer,
        )

    far_end = jnp.where(lower, 3, 0)
    far_mid = jnp.where(lower, 2, 1)
    near_mid = jnp.where(lower, 1, 2)
    near_end = jnp.where(lower, 0, 3)

    def add_passing(unit, dest):
        totals[unit, dest] = (
            totals[unit, dest].astype(F32) + passing[unit, dest].astype(F32)
        ).astype(BF16)

    def second(unit):
        if unit >= units:
            piece = slice((unit - units) * rows, (unit - units + 1) * rows)
            lhs = left_four[:, piece, :].reshape(4 * rows, 4 * tokens)
            out = nn(lhs, right_four[...])
        else:
            out = product(unit, y)
            y_copy[unit].wait_recv()
            out = out + y_recv[unit].reshape(4 * rows, width).astype(F32)
        totals[unit] = out.astype(BF16).reshape(4, rows, width)

        @pl.when(at_end)
        def _():
            z_copy(unit, far_end, in_peer, False).start()
            z_copy(unit, far_mid, in_peer, False).start()
            z_copy(unit, near_mid, in_peer, False).start()

    def third(unit):
        @pl.when(jnp.logical_not(at_end))
        def _():
            z_copy(unit, far_end, in_peer, False).wait_recv()
            add_passing(unit, far_end)
            z_copy(unit, far_end, in_peer, False).start()
            z_copy(unit, far_mid, in_peer, False).wait_recv()
            add_passing(unit, far_mid)
            z_copy(unit, far_mid, in_peer, True).start()

    def fourth(unit):
        @pl.when(jnp.logical_not(at_end))
        def _():
            z_copy(unit, near_end, out_peer, False).wait_recv()
            add_passing(unit, near_end)
            z_copy(unit, near_end, out_peer, True).start()

    def store(unit, value):
        if unit < 4:
            g_fc1[:, unit * width : (unit + 1) * width] = value
        elif unit < 7:
            g_qkv[:, (unit - 4) * width : (unit - 3) * width] = value
        elif unit == 7:
            g_out[...] = value
        else:
            g_fc2[(unit - units) * rows : (unit - units + 1) * rows, :] = value

    def fifth(unit):
        z_copy(unit, z, in_peer, True).wait_recv()
        value = totals[unit, z].astype(F32) + inward[unit].astype(F32)

        @pl.when(at_end)
        def _():
            store(unit, value)

        @pl.when(jnp.logical_not(at_end))
        def _():
            z_copy(unit, z, in_peer, False).wait_recv()
            store(unit, value + passing[unit, z].astype(F32))

    def small_step(step):
        small_copy[step].wait_recv()
        small_own[step + 1] = small_own[step] + small_recv[step]
        if step < 3:
            small_copy[step + 1].start()

    stages = (first, second, third, fourth, fifth)
    for turn in range(len(order) + len(stages) - 1):
        for depth in (0, 1, 2, 3, 4):
            index = turn - depth
            if 0 <= index < len(order):
                stages[depth](order[index])
        if turn < 4:
            small_step(turn)

    g_gains[...] = small_own[4, 0:4, :]
    g_biases[...] = small_own[4, 4:10, :]
    for part in range(4):
        g_fc1_bias[0:1, part * width : (part + 1) * width] = small_own[4, 10 + part : 11 + part, :]
    g_table[...] = small_own[4, 16 : 16 + g_table.shape[0], 0 : g_table.shape[1]]

    for copy in four:
        copy.wait_send()
    for copy in x_left + x_right + y_copy + small_copy:
        copy.wait_send()

    @pl.when(at_end)
    def _():
        for unit in order:
            z_copy(unit, far_end, in_peer, False).wait_send()
            z_copy(unit, far_mid, in_peer, False).wait_send()
            z_copy(unit, near_mid, in_peer, False).wait_send()

    @pl.when(jnp.logical_not(at_end))
    def _():
        for unit in order:
            z_copy(unit, far_end, in_peer, False).wait_send()
            z_copy(unit, far_mid, in_peer, True).wait_send()
            z_copy(unit, near_end, out_peer, True).wait_send()


def run_shares(at_small, at_active, b_all, small, heads, rels):
    width, tokens = at_small.shape[1:]
    ff = at_active.shape[0]
    rows = width // 16
    units = len(UNIT_LEFT)
    all_units = units + ff // width
    at_small = at_small.reshape(3, 4, 2, 2, rows, tokens)
    at_active = at_active.reshape(4, 2, 2, ff // 16, tokens)
    whole = pl.BlockSpec(memory_space=pltpu.VMEM)
    anywhere = pl.BlockSpec(memory_space=pl.ANY)
    vm = pltpu.VMEM
    dma = pltpu.SemaphoreType.DMA
    return pl.pallas_call(
        share_kernel,
        out_shape=(
            jax.ShapeDtypeStruct((rows, 3 * width), F32),
            jax.ShapeDtypeStruct((rows, width), F32),
            jax.ShapeDtypeStruct((rows, ff), F32),
            jax.ShapeDtypeStruct((ff // 16, width), F32),
            jax.ShapeDtypeStruct((4, width), F32),
            jax.ShapeDtypeStruct((6, width), F32),
            jax.ShapeDtypeStruct((1, ff), F32),
            jax.ShapeDtypeStruct((heads, rels), F32),
        ),
        in_specs=[anywhere, anywhere, anywhere, whole],
        out_specs=(whole,) * 8,
        scratch_shapes=[
            vm((3, 4, 2, rows, 2 * tokens), BF16),
            vm((units, 2 * tokens, width), BF16),
            vm((4, ff // 16, 4 * tokens), BF16),
            vm((4 * tokens, width), BF16),
            vm((units, 4, rows, width), BF16),
            vm((units, 4, rows, width), BF16),
            vm((all_units, 4, rows, width), BF16),
            vm((all_units, 4, rows, width), BF16),
            vm((all_units, rows, width), BF16),
            vm((5, 32, width), F32),
            vm((4, 32, width), F32),
            dma((6,)),
            dma((units + 3,)),
            dma((units + 3,)),
            dma((units,)),
            dma((units,)),
            dma((2, 4)),
            dma((2, 4)),
            dma((all_units, 4)),
            dma((all_units, 5)),
            dma((4,)),
            dma((4,)),
        ],
        compiler_params=pltpu.CompilerParams(
            collective_id=1, has_side_effects=True, vmem_limit_bytes=56 * 2**20
        ),
        name="shares",
    )(at_small, at_active, b_all, small)


def plain_shares(at_small, at_active, b_all, small, heads, rels):
    width = at_small.shape[1]
    ff = at_active.shape[0]
    parts = ff // width

    def scattered(left, right):
        grad = jnp.dot(left, right, preferred_element_type=F32)
        return lax.psum_scatter(grad, "batch", scatter_dimension=0, tiled=True)

    def joined(first, count):
        return jnp.concatenate([b_all[first + number] for number in range(count)], axis=1)

    g_fc1 = scattered(at_small[0], joined(0, parts))
    g_qkv = scattered(at_small[1], joined(parts, 3))
    g_out = scattered(at_small[2], b_all[parts + 3])
    g_fc2 = scattered(at_active, b_all[parts + 4])
    small = lax.psum(small, "batch")
    return (
        g_qkv,
        g_out,
        g_fc1,
        g_fc2,
        small[0:4],
        small[4:10],
        small[10:14].reshape(1, ff),
        small[16 : 16 + heads, :rels],
    )


def per_device(
    inputs,
    cotangent,
    segments,
    row_widths,
    w_qkv,
    w_out,
    w_fc1,
    w_fc2,
    norm_gains,
    bias_rows,
    fc1_bias,
    rel_table,
):
    micro, _, slots, width = inputs.shape
    heads, rels = rel_table.shape[1:]
    weights = (w_qkv, w_out, w_fc1, w_fc2, norm_gains, bias_rows, fc1_bias, rel_table)
    activation, grad_in, at_small, at_active, b_all, small = run_block(
        inputs.reshape(micro * slots, width),
        cotangent.reshape(micro * slots, width),
        segments.reshape(micro, slots),
        row_widths.reshape(micro, row_widths.shape[2]),
        weights,
    )
    shares = run_shares if lax.axis_size("batch") == 16 else plain_shares
    grads = shares(at_small, at_active, b_all, small, heads, rels)
    g_qkv, g_out, g_fc1, g_fc2, g_gains, g_biases, g_fc1_bias, g_table = grads
    shape = (1, micro, 1, slots, width)
    return (
        activation.reshape(shape),
        grad_in.reshape(shape),
        g_qkv[None],
        g_out[None],
        g_fc1[None],
        g_fc2[None],
        g_gains[None],
        g_biases[None],
        g_fc1_bias,
        g_table[None],
    )


def solution(mesh):
    return jax.shard_map(
        per_device,
        mesh=mesh,
        in_specs=(
            P(None, "batch", None, None),
            P(None, "batch", None, None),
            P(None, "batch", None),
            P(None, "batch", None),
            P("section", None, None),
            P("section", None, None),
            P("section", None, None),
            P("section", None, None),
            P("section", None, None),
            P("section", None, None),
            P("section", None),
            P("section", None, None),
        ),
        out_specs=(
            P("section", None, "batch", None, None),
            P("section", None, "batch", None, None),
            P("section", "batch", None),
            P("section", "batch", None),
            P("section", "batch", None),
            P("section", "batch", None),
            P("section", None, None),
            P("section", None, None),
            P("section", None),
            P("section", None, None),
        ),
        check_vma=False,
    )
```

```python
import functools

import jax
import jax.numpy as jnp
from jax import lax
from jax.experimental import pallas as pl
from jax.experimental.pallas import tpu as pltpu
from jax.sharding import PartitionSpec as P

MESH = pl.DeviceIdType.MESH
F32 = jnp.float32
BF16 = jnp.bfloat16
REACH = 13
SPAN = 2 * REACH + 1
NORM_EPS = 1e-06
ROOT_HALF = 0.7071067811865476
INV_ROOT_TWO_PI = 0.3989422804014327
COLS = 256
GRID_ROWS = 8
GRID_COLS = 16
PITCH = 2 * GRID_COLS
WIDE = 2 * GRID_ROWS * PITCH
HALF = WIDE // 2


def nn(left, right):
    return lax.dot_general(left, right, (((1,), (0,)), ((), ())), preferred_element_type=F32)


def nt(left, right):
    return lax.dot_general(left, right, (((1,), (1,)), ((), ())), preferred_element_type=F32)


def tn(left, right):
    return lax.dot_general(left, right, (((0,), (0,)), ((), ())), preferred_element_type=F32)


def iota(shape, dim):
    return lax.broadcasted_iota(jnp.int32, shape, dim)


def two_parts(value):
    high = value.astype(BF16)
    return high, (value - high.astype(F32)).astype(BF16)


def norm_parts(values_in):
    row_mean = jnp.mean(values_in, axis=-1, keepdims=True)
    centered = values_in - row_mean
    inv_scale = lax.rsqrt(jnp.mean(centered * centered, axis=-1, keepdims=True) + NORM_EPS)
    return centered * inv_scale, inv_scale


def norm_back(upstream, normal_in, inv_scale):
    return inv_scale * (
        upstream
        - jnp.mean(upstream, axis=-1, keepdims=True)
        - normal_in * jnp.mean(upstream * normal_in, axis=-1, keepdims=True)
    )


def col_sum(value):
    return jnp.sum(value, axis=0, keepdims=True)


def chunk_loop(count, body):
    def step(index, carry):
        body(index)
        return carry

    lax.fori_loop(0, count, step, 0, unroll=True)


def cols_of(index, size=COLS):
    return pl.ds(pl.multiple_of(index * size, size), size)


def geometry(seg, wid, same, pick_q, pick_k, pick_kt, pick_qt):
    micro, slots = seg.shape
    tokens = micro * slots
    images = wid.shape[1]
    seg_f = seg[...].astype(F32)
    seg_row = jnp.concatenate(
        [seg_f[m : m + 1, :] + float(m * images) for m in range(micro)], axis=1
    )
    sub = iota((tokens, tokens), 0)
    lane = iota((tokens, tokens), 1)
    seg_col = jnp.sum(jnp.where(sub == lane, seg_row, 0.0), axis=1, keepdims=True)
    same[...] = (seg_col == seg_row).astype(F32)
    before_row = jnp.sum((seg_col < seg_row).astype(F32), axis=0, keepdims=True)
    before_col = jnp.sum((seg_row < seg_col).astype(F32), axis=1, keepdims=True)
    place_row = iota((1, tokens), 1).astype(F32) - before_row
    place_col = iota((tokens, 1), 0).astype(F32) - before_col
    width_row = jnp.zeros((1, tokens), F32)
    width_col = jnp.zeros((tokens, 1), F32)
    for m in range(micro):
        for image in range(images):
            width = wid[m, image].astype(F32)
            number = float(m * images + image)
            width_row = width_row + jnp.where(seg_row == number, width, 0.0)
            width_col = width_col + jnp.where(seg_col == number, width, 0.0)

    def grid(place, width):
        row = jnp.zeros_like(place)
        for k in range(1, GRID_ROWS):
            row = row + (place >= float(k) * width).astype(F32)
        return row, place - row * width

    row_r, col_r = grid(place_row, width_row)
    row_c, col_c = grid(place_col, width_col)
    cells = GRID_ROWS * GRID_COLS
    pick_q[...] = (iota((tokens, cells), 1).astype(F32) == row_c * GRID_COLS + col_c).astype(
        F32
    ).astype(BF16)
    pick_qt[...] = (
        iota((cells, tokens), 0).astype(F32) == row_r * GRID_COLS + (GRID_COLS - 1.0) - col_r
    ).astype(F32).astype(BF16)
    pick_k[...] = (iota((tokens, HALF), 1).astype(F32) == row_c * PITCH + col_c).astype(
        F32
    ).astype(BF16)
    pick_kt[...] = (iota((HALF, tokens), 0).astype(F32) == row_r * PITCH + col_r).astype(
        F32
    ).astype(BF16)


def spread_table(table, padded, spread, wide_table):
    heads, _, rels = table.shape
    padded[...] = jnp.zeros_like(padded)
    for head in range(heads):
        padded[head : head + 1, 0:rels] = table[head]
    shape = spread.shape
    where = iota((1, WIDE), 1)
    signed = jnp.where(where < HALF, where, where - WIDE)
    row_step = (signed + GRID_COLS + WIDE) // PITCH - WIDE // PITCH
    col_step = signed - row_step * PITCH
    entry = (REACH - row_step) * SPAN + jnp.clip(-col_step, -REACH, REACH) + REACH
    spread[...] = (iota(shape, 0) == entry).astype(F32).astype(BF16)
    high, low = two_parts(padded[...])
    vector = nn(high, spread[...]) + nn(low, spread[...])
    cells = GRID_ROWS * GRID_COLS
    for head in range(heads):
        line = jnp.broadcast_to(vector[head : head + 1, :], (GRID_COLS, WIDE))
        line = pltpu.roll(line, 0, 1, stride=1, stride_axis=0)
        for low_row in range(4):
            turned = line if low_row == 0 else pltpu.roll(line, low_row * PITCH, 1)
            for high_row in range(GRID_ROWS // 4):
                if high_row == 0:
                    part = turned[:, 0:HALF]
                else:
                    part = jnp.concatenate(
                        [turned[:, WIDE - 4 * PITCH : WIDE], turned[:, 0 : HALF - 4 * PITCH]], axis=1
                    )
                top = (high_row * 4 + low_row) * GRID_COLS
                part_high, part_low = two_parts(part)
                wide_table[top : top + GRID_COLS, head * HALF : (head + 1) * HALF] = part_high
                wide_table[
                    cells + top : cells + top + GRID_COLS, head * HALF : (head + 1) * HALF
                ] = part_low


def fold_table(head_grad):
    total = None
    for low_row in range(4):
        near = head_grad[low_row * GRID_COLS : (low_row + 1) * GRID_COLS, :]
        far = head_grad[(low_row + 4) * GRID_COLS : (low_row + 5) * GRID_COLS, :]
        step = 4 * PITCH
        laid = jnp.concatenate(
            [
                near[:, 0:step] + far[:, step : 2 * step],
                near[:, step : 2 * step],
                jnp.zeros((GRID_COLS, step), F32),
                far[:, 0:step],
            ],
            axis=1,
        )
        if low_row > 0:
            laid = pltpu.roll(laid, WIDE - low_row * PITCH, 1)
        total = laid if total is None else total + laid
    total = pltpu.roll(total, WIDE - (GRID_COLS - 1), 1, stride=1, stride_axis=0)
    return col_sum(total)


def block_kernel(
    inputs,
    cotangent,
    seg,
    wid,
    wqkv_in,
    wout_in,
    wfc1_in,
    wfc2_in,
    gains,
    biases,
    fc1_bias,
    table,
    activation,
    grad_in,
    at_small,
    at_active,
    b_all,
    small,
    wqkv,
    wout,
    wfc1,
    wfc2,
    arrived,
    leaving,
    stream,
    hat_one,
    hat_two,
    att_out,
    branch,
    d_middle,
    d_wide,
    normed,
    qkv,
    probs,
    bias,
    mixed,
    d_mixed,
    second,
    active,
    slope,
    same,
    pick_q,
    pick_k,
    pick_kt,
    pick_qt,
    padded,
    spread,
    wide_table,
    folded,
    scale_one,
    scale_two,
    weight_sem,
    send_sem,
    recv_sem,
):
    section = lax.axis_index("section")
    place = lax.axis_index("batch")
    other = (1 - section, place)
    width = inputs.shape[1]
    tokens = inputs.shape[0]
    ff = active.shape[1]
    heads = table.shape[0]
    pair = 2 * (width // heads)
    pairs = heads // 2
    parts = ff // width
    per_part = width // COLS

    loads = [
        pltpu.make_async_copy(source.at[0], target, weight_sem.at[index])
        for index, (source, target) in enumerate(
            [(wqkv_in, wqkv), (wout_in, wout), (wfc1_in, wfc1), (wfc2_in, wfc2)]
        )
    ]
    for load in loads:
        load.start()

    barrier = pltpu.get_barrier_semaphore()
    pl.semaphore_signal(barrier, inc=1, device_id=other, device_id_type=MESH)

    geometry(seg, wid, same, pick_q, pick_k, pick_kt, pick_qt)
    spread_table(table, padded, spread, wide_table)
    cells = GRID_ROWS * GRID_COLS

    def bias_of(head):
        where = cols_of(head, HALF)
        high = nn(pick_q[...], wide_table[0:cells, where]).astype(BF16)
        low = nn(pick_q[...], wide_table[cells : 2 * cells, where]).astype(BF16)
        bias[cols_of(head, tokens), :] = nn(high, pick_kt[...]) + nn(low, pick_kt[...])

    chunk_loop(heads, bias_of)

    pl.semaphore_wait(barrier, 1)

    def relay(source):
        return pltpu.make_async_remote_copy(
            src_ref=source,
            dst_ref=arrived,
            send_sem=send_sem,
            recv_sem=recv_sem,
            device_id=other,
            device_id_type=MESH,
        )

    @pl.when(section == 0)
    def _():
        stream[...] = inputs[...].astype(F32)

    @pl.when(section == 1)
    def _():
        relay(activation).wait_recv()
        stream[...] = arrived[...].astype(F32)

    hat, inv_scale = norm_parts(stream[...])
    hat_one[...] = hat
    scale_one[...] = inv_scale
    normed[...] = (hat * gains[0, 0:1, :] + biases[0, 0:1, :]).astype(BF16)
    loads[0].wait()
    for third in range(3):

        def project(index):
            out = nn(normed[...], wqkv[:, cols_of(third * per_part + index)])
            if third != 1:
                row = 1 if third == 0 else 2
                out = out + biases[row, 0:1, cols_of(index)]
            qkv[third, :, cols_of(index)] = out.astype(BF16)

        chunk_loop(per_part, project)

    lane = iota((1, pair), 1)
    low_lanes = (lane < pair // 2).astype(F32).astype(BF16)
    high_lanes = (lane >= pair // 2).astype(F32).astype(BF16)

    def stacked(value):
        return jnp.concatenate([value * low_lanes, value * high_lanes], axis=0)

    def side_by_side(value):
        return jnp.concatenate([value[0:tokens, :], value[tokens : 2 * tokens, :]], axis=1)

    for index in range(pairs):
        at = slice(index * pair, (index + 1) * pair)
        rows = slice(index * 2 * tokens, (index + 1) * 2 * tokens)
        raw = nt(stacked(qkv[0, :, at]), qkv[1, :, at])
        mask = jnp.concatenate([same[...], same[...]], axis=0) > 0.5
        scores = jnp.where(mask, raw * 0.125 + bias[rows, :], -1e30)
        exped = jnp.exp(scores - jnp.max(scores, axis=-1, keepdims=True))
        prob = exped / jnp.sum(exped, axis=-1, keepdims=True)
        probs[rows, :] = prob
        mixed[:, at] = nn(side_by_side(prob.astype(BF16)), stacked(qkv[2, :, at])).astype(BF16)

    loads[1].wait()

    def attend_out(index):
        at = cols_of(index)
        out = nn(mixed[...], wout[:, at]) + biases[3, 0:1, at]
        att_out[:, at] = out
        stream[:, at] = stream[:, at] + gains[0, 1:2, at] * out

    chunk_loop(per_part, attend_out)
    hat, inv_scale = norm_parts(stream[...])
    hat_two[...] = hat
    scale_two[...] = inv_scale
    second[...] = (hat * gains[0, 2:3, :] + biases[4, 0:1, :]).astype(BF16)
    loads[2].wait()

    def feed(index):
        at = cols_of(index)
        hidden = nn(second[...], wfc1[:, at]) + fc1_bias[0:1, at]
        cumul = 0.5 * (1.0 + lax.erf(hidden * ROOT_HALF))
        density = jnp.exp(-0.5 * hidden * hidden) * INV_ROOT_TWO_PI
        active[:, at] = (hidden * cumul).astype(BF16)
        slope[:, at] = cumul + hidden * density

    chunk_loop(ff // COLS, feed)
    loads[3].wait()

    def feed_out(index):
        at = cols_of(index)
        out = nn(active[...], wfc2[:, at]) + biases[5, 0:1, at]
        branch[:, at] = out
        activation[:, at] = (stream[:, at] + gains[0, 3:4, at] * out).astype(BF16)

    chunk_loop(per_part, feed_out)

    def turn():
        def turn_small(index):
            at = cols_of(index, 128)
            for number, source in enumerate((second, normed, mixed)):
                at_small[number, at, :] = source[:, at].T

        def turn_active(index):
            at = cols_of(index, 128)
            at_active[at, :] = active[:, at].T

        chunk_loop(width // 128, turn_small)
        chunk_loop(ff // 128, turn_active)

    @pl.when(section == 0)
    def _():
        relay(activation).start()
        turn()
        relay(activation).wait_send()
        relay(activation).wait_recv()
        stream[...] = arrived[...].astype(F32)

    @pl.when(section == 1)
    def _():
        stream[...] = cotangent[...].astype(F32)

    small[...] = jnp.zeros_like(small)
    upstream = stream[...]
    small[3:4, :] = col_sum(upstream * branch[...])
    d_branch = (gains[0, 3:4, :] * upstream).astype(BF16)
    b_all[parts + 4] = d_branch
    small[9:10, :] = col_sum(d_branch.astype(F32))

    def feed_back(index):
        at = cols_of(index)
        out = nt(b_all[parts + 4], wfc2[at, :])
        d_hidden = (out * slope[:, at]).astype(BF16)
        part = index // per_part
        inner = cols_of(index % per_part)
        b_all[part, :, inner] = d_hidden
        small[pl.ds(10 + part, 1), inner] = col_sum(d_hidden.astype(F32))

    chunk_loop(ff // COLS, feed_back)

    def second_back(index):
        at = cols_of(index)
        out = nt(b_all[0], wfc1[at, 0:width])
        for part in range(1, parts):
            out = out + nt(b_all[part], wfc1[at, part * width : (part + 1) * width])
        d_wide[:, at] = out

    chunk_loop(per_part, second_back)
    d_second = d_wide[...]
    small[2:3, :] = col_sum(d_second * hat_two[...])
    small[8:9, :] = col_sum(d_second)
    d_mid = stream[...] + norm_back(d_second * gains[0, 2:3, :], hat_two[...], scale_two[...])
    d_middle[...] = d_mid
    small[1:2, :] = col_sum(d_mid * att_out[...])
    d_att = (gains[0, 1:2, :] * d_mid).astype(BF16)
    b_all[parts + 3] = d_att
    small[7:8, :] = col_sum(d_att.astype(F32))

    def out_back(index):
        at = cols_of(index)
        d_mixed[:, at] = nt(b_all[parts + 3], wout[at, :]).astype(BF16)

    chunk_loop(per_part, out_back)

    folded[...] = jnp.zeros_like(folded)
    for index in range(pairs):
        at = slice(index * pair, (index + 1) * pair)
        rows = slice(index * 2 * tokens, (index + 1) * 2 * tokens)
        prob = probs[rows, :]
        d_mix = stacked(d_mixed[:, at])
        d_prob = nt(d_mix, qkv[2, :, at])
        b_all[parts + 2, :, at] = tn(prob.astype(BF16), d_mix).astype(BF16)
        d_scores = prob * (d_prob - jnp.sum(prob * d_prob, axis=-1, keepdims=True))
        d_raw = (0.125 * d_scores).astype(BF16)
        b_all[parts, :, at] = nn(side_by_side(d_raw), stacked(qkv[1, :, at])).astype(BF16)
        b_all[parts + 1, :, at] = tn(d_raw, stacked(qkv[0, :, at])).astype(BF16)
        high, low = two_parts(d_scores)
        high = nn(high, pick_k[...]).astype(BF16)
        low = nn(low, pick_k[...]).astype(BF16)
        for side in range(2):
            own = slice(side * tokens, (side + 1) * tokens)
            head_grad = nn(pick_qt[...], high[own, :]) + nn(pick_qt[...], low[own, :])
            folded[2 * index + side : 2 * index + side + 1, :] = fold_table(head_grad)

    small[5:6, :] = col_sum(b_all[parts].astype(F32))
    small[6:7, :] = col_sum(b_all[parts + 2].astype(F32))

    def normed_back(index):
        at = cols_of(index)
        out = nt(b_all[parts], wqkv[at, 0:width])
        for third in range(1, 3):
            out = out + nt(b_all[parts + third], wqkv[at, third * width : (third + 1) * width])
        d_wide[:, at] = out

    chunk_loop(per_part, normed_back)
    d_normed = d_wide[...]
    small[0:1, :] = col_sum(d_normed * hat_one[...])
    small[4:5, :] = col_sum(d_normed)
    d_in = d_middle[...] + norm_back(d_normed * gains[0, 0:1, :], hat_one[...], scale_one[...])
    grad_in[...] = d_in
    leaving[...] = d_in.astype(BF16)

    @pl.when(section == 1)
    def _():
        relay(leaving).start()
        turn()

    high, low = two_parts(folded[...])
    small[16:32, :] = nt(high, spread[...]) + nt(low, spread[...])

    @pl.when(section == 1)
    def _():
        relay(leaving).wait_send()


def run_block(inputs, cotangent, seg, wid, weights):
    w_qkv, w_out, w_fc1, w_fc2, gains, biases, fc1_bias, table = weights
    tokens, width = inputs.shape
    ff = w_fc1.shape[2]
    heads = table.shape[1]
    rels = table.shape[2]
    parts = ff // width
    cells = GRID_ROWS * GRID_COLS
    whole = pl.BlockSpec(memory_space=pltpu.VMEM)
    vm = pltpu.VMEM
    padded_rels = -(-rels // 256) * 256
    return pl.pallas_call(
        block_kernel,
        out_shape=(
            jax.ShapeDtypeStruct((tokens, width), BF16),
            jax.ShapeDtypeStruct((tokens, width), F32),
            jax.ShapeDtypeStruct((3, width, tokens), BF16),
            jax.ShapeDtypeStruct((ff, tokens), BF16),
            jax.ShapeDtypeStruct((parts + 5, tokens, width), BF16),
            jax.ShapeDtypeStruct((32, width), F32),
        ),
        in_specs=[whole, whole, whole, pl.BlockSpec(memory_space=pltpu.SMEM)]
        + [pl.BlockSpec(memory_space=pl.ANY)] * 4
        + [whole] * 4,
        out_specs=(whole,) * 6,
        scratch_shapes=[
            vm(w_qkv.shape[1:], BF16),
            vm(w_out.shape[1:], BF16),
            vm(w_fc1.shape[1:], BF16),
            vm(w_fc2.shape[1:], BF16),
            vm((tokens, width), BF16),
            vm((tokens, width), BF16),
        ]
        + [vm((tokens, width), F32)] * 7
        + [
            vm((tokens, width), BF16),
            vm((3, tokens, width), BF16),
            vm((heads * tokens, tokens), F32),
            vm((heads * tokens, tokens), F32),
            vm((tokens, width), BF16),
            vm((tokens, width), BF16),
            vm((tokens, width), BF16),
            vm((tokens, ff), BF16),
            vm((tokens, ff), F32),
            vm((tokens, tokens), F32),
            vm((tokens, cells), BF16),
            vm((tokens, HALF), BF16),
            vm((HALF, tokens), BF16),
            vm((cells, tokens), BF16),
            vm((16, padded_rels), F32),
            vm((padded_rels, WIDE), BF16),
            vm((2 * cells, heads * HALF), BF16),
            vm((16, WIDE), F32),
            vm((tokens, 1), F32),
            vm((tokens, 1), F32),
            pltpu.SemaphoreType.DMA((4,)),
            pltpu.SemaphoreType.DMA,
            pltpu.SemaphoreType.DMA,
        ],
        compiler_params=pltpu.CompilerParams(
            collective_id=0, has_side_effects=True, vmem_limit_bytes=56 * 2**20
        ),
        name="block",
    )(inputs, cotangent, seg, wid, w_qkv, w_out, w_fc1, w_fc2, gains, jnp.swapaxes(biases, 0, 1), fc1_bias, jnp.swapaxes(table, 0, 1))


AHEAD = 3
DEPTHS = (2, 4, 6, 8)
UNIT_LEFT = (0, 0, 0, 0, 1, 1, 1, 2)


def share_kernel(
    at_small,
    at_active,
    b_all,
    small,
    g_qkv,
    g_out,
    g_fc1,
    g_fc2,
    g_gains,
    g_biases,
    g_fc1_bias,
    g_table,
    left,
    right,
    left_four,
    right_four,
    y_send,
    y_recv,
    totals,
    passing,
    inward,
    small_own,
    small_recv,
    own_sem,
    x_send_sem,
    x_recv_sem,
    y_send_sem,
    y_recv_sem,
    four_send_sem,
    four_recv_sem,
    z_send_sem,
    z_recv_sem,
    small_send_sem,
    small_recv_sem,
):
    section = lax.axis_index("section")
    place = lax.axis_index("batch")
    z = place // 4
    y = (place // 2) % 2
    x = place % 2
    x_peer = z * 4 + y * 2 + (1 - x)
    y_peer = z * 4 + (1 - y) * 2 + x
    xy_peer = z * 4 + (1 - y) * 2 + (1 - x)
    at_end = (z == 0) | (z == 3)
    lower = z < 2
    in_peer = jnp.where(lower, place + 4, place - 4)
    out_peer = jnp.where(z == 1, place - 4, place + 4)
    out_peer = jnp.where(at_end, place, out_peer)
    far_z = jnp.where(lower, z + 2, z - 2)
    far_peer = far_z * 4 + y * 2 + x
    pair_peer = jnp.where(z % 2 == 0, place + 4, place - 4)
    units = len(UNIT_LEFT)
    tokens = b_all.shape[1]
    rows = left.shape[3]
    width = right.shape[2]

    def remote(source, target, send, recv, peer):
        return pltpu.make_async_remote_copy(
            src_ref=source,
            dst_ref=target,
            send_sem=send,
            recv_sem=recv,
            device_id=(section, peer),
            device_id_type=MESH,
        )

    barrier = pltpu.get_barrier_semaphore()

    def greet(peer):
        pl.semaphore_signal(barrier, inc=1, device_id=(section, peer), device_id_type=MESH)

    for peer in (x_peer, y_peer, xy_peer, in_peer, far_peer):
        greet(peer)

    @pl.when(jnp.logical_not(at_end))
    def _():
        greet(out_peer)

    own = []
    for number in range(3):
        own.append(
            pltpu.make_async_copy(
                at_small.at[number, :, :, x],
                left.at[number, :, :, :, 0:tokens],
                own_sem.at[number],
            )
        )
    own.append(
        pltpu.make_async_copy(
            b_all.at[0:units], right.at[:, 0:tokens, :], own_sem.at[3]
        )
    )
    own.append(
        pltpu.make_async_copy(at_active.at[:, y, x], left_four.at[:, :, 0:tokens], own_sem.at[4])
    )
    own.append(
        pltpu.make_async_copy(b_all.at[units], right_four.at[0:tokens, :], own_sem.at[5])
    )
    for copy in own:
        copy.start()
    small_own[0] = small[...]

    @pl.when(at_end)
    def _():
        pl.semaphore_wait(barrier, 5)

    @pl.when(jnp.logical_not(at_end))
    def _():
        pl.semaphore_wait(barrier, 6)

    def send_four(slot, peer_y, peer_x, peer):
        lanes = slice(slot * tokens, (slot + 1) * tokens)
        return (
            remote(
                at_active.at[:, peer_y, peer_x],
                left_four.at[:, :, lanes],
                four_send_sem.at[0, slot],
                four_recv_sem.at[0, slot],
                peer,
            ),
            remote(
                b_all.at[units],
                right_four.at[lanes, :],
                four_send_sem.at[1, slot],
                four_recv_sem.at[1, slot],
                peer,
            ),
        )

    four = (
        send_four(1, y, 1 - x, x_peer)
        + send_four(2, 1 - y, x, y_peer)
        + send_four(3, 1 - y, 1 - x, xy_peer)
    )
    x_left = [
        remote(
            at_small.at[number, :, :, 1 - x],
            left.at[number, :, :, :, tokens : 2 * tokens],
            x_send_sem.at[units + number],
            x_recv_sem.at[units + number],
            x_peer,
        )
        for number in range(3)
    ]
    x_right = [
        remote(
            b_all.at[unit],
            right.at[unit, tokens : 2 * tokens, :],
            x_send_sem.at[unit],
            x_recv_sem.at[unit],
            x_peer,
        )
        for unit in range(units)
    ]
    small_peers = (x_peer, y_peer, pair_peer, far_peer)
    small_copy = [
        remote(
            small_own.at[step],
            small_recv.at[step],
            small_send_sem.at[step],
            small_recv_sem.at[step],
            small_peers[step],
        )
        for step in range(4)
    ]
    queue = [
        [x_left[0], x_right[0]],
        [x_right[1]],
        [x_right[2]],
        list(four[4:6]),
        [x_right[3]],
        list(four[0:2]),
        [x_left[1], x_right[4]],
        [x_right[5]],
        [x_right[6]],
        [x_left[2], x_right[7]],
    ]

    def issue(count):
        for _ in range(count):
            if queue:
                for copy in queue.pop(0):
                    copy.start()

    small_copy[0].start()
    issue(1)
    for copy in four[2:4]:
        copy.start()
    issue(AHEAD)

    y_copy = [
        remote(
            y_send.at[unit],
            y_recv.at[unit],
            y_send_sem.at[unit],
            y_recv_sem.at[unit],
            y_peer,
        )
        for unit in range(units)
    ]
    order = [0, 1, 2, 3, 8, 4, 9, 5, 10, 6, 11, 7]
    for copy in own:
        copy.wait()
    waited = set()

    def product(unit, side):
        lhs = left[UNIT_LEFT[unit], :, side].reshape(4 * rows, 2 * tokens)
        return nn(lhs, right[unit])

    def first(unit):
        if unit >= units:
            if not waited & {"four"}:
                waited.add("four")
                for copy in four:
                    copy.wait_recv()
            issue(1)
            return
        if UNIT_LEFT[unit] not in waited:
            waited.add(UNIT_LEFT[unit])
            x_left[UNIT_LEFT[unit]].wait_recv()
        x_right[unit].wait_recv()
        issue(1)
        y_send[unit] = product(unit, 1 - y).astype(BF16).reshape(4, rows, width)
        y_copy[unit].start()

    def z_copy(unit, dest, peer, final_inside):
        target = inward.at[unit] if final_inside else passing.at[unit, dest]
        slot = 4 if final_inside else dest
        return remote(
            totals.at[unit, dest],
            target,
            z_send_sem.at[unit, dest],
            z_recv_sem.at[unit, slot],
            peer,
        )

    far_end = jnp.where(lower, 3, 0)
    far_mid = jnp.where(lower, 2, 1)
    near_mid = jnp.where(lower, 1, 2)
    near_end = jnp.where(lower, 0, 3)

    def add_passing(unit, dest):
        totals[unit, dest] = (
            totals[unit, dest].astype(F32) + passing[unit, dest].astype(F32)
        ).astype(BF16)

    def second(unit):
        if unit >= units:
            piece = slice((unit - units) * rows, (unit - units + 1) * rows)
            lhs = left_four[:, piece, :].reshape(4 * rows, 4 * tokens)
            out = nn(lhs, right_four[...])
        else:
            out = product(unit, y)
            y_copy[unit].wait_recv()
            out = out + y_recv[unit].reshape(4 * rows, width).astype(F32)
        totals[unit] = out.astype(BF16).reshape(4, rows, width)

        @pl.when(at_end)
        def _():
            z_copy(unit, far_end, in_peer, False).start()
            z_copy(unit, far_mid, in_peer, False).start()
            z_copy(unit, near_mid, in_peer, False).start()

    def third(unit):
        @pl.when(jnp.logical_not(at_end))
        def _():
            z_copy(unit, far_end, in_peer, False).wait_recv()
            add_passing(unit, far_end)
            z_copy(unit, far_end, in_peer, False).start()
            z_copy(unit, far_mid, in_peer, False).wait_recv()
            add_passing(unit, far_mid)
            z_copy(unit, far_mid, in_peer, True).start()

    def fourth(unit):
        @pl.when(jnp.logical_not(at_end))
        def _():
            z_copy(unit, near_end, out_peer, False).wait_recv()
            add_passing(unit, near_end)
            z_copy(unit, near_end, out_peer, True).start()

    def store(unit, value):
        if unit < 4:
            g_fc1[:, unit * width : (unit + 1) * width] = value
        elif unit < 7:
            g_qkv[:, (unit - 4) * width : (unit - 3) * width] = value
        elif unit == 7:
            g_out[...] = value
        else:
            g_fc2[(unit - units) * rows : (unit - units + 1) * rows, :] = value

    def fifth(unit):
        z_copy(unit, z, in_peer, True).wait_recv()
        value = totals[unit, z].astype(F32) + inward[unit].astype(F32)

        @pl.when(at_end)
        def _():
            store(unit, value)

        @pl.when(jnp.logical_not(at_end))
        def _():
            z_copy(unit, z, in_peer, False).wait_recv()
            store(unit, value + passing[unit, z].astype(F32))

    def small_step(step):
        small_copy[step].wait_recv()
        small_own[step + 1] = small_own[step] + small_recv[step]
        if step < 3:
            small_copy[step + 1].start()

    stages = ((first, 0), (second, DEPTHS[0]), (third, DEPTHS[1]), (fourth, DEPTHS[2]), (fifth, DEPTHS[3]))
    for turn in range(len(order) + DEPTHS[3]):
        for stage, depth in stages:
            index = turn - depth
            if 0 <= index < len(order):
                stage(order[index])
        if turn < 4:
            small_step(turn)

    g_gains[...] = small_own[4, 0:4, :]
    g_biases[...] = small_own[4, 4:10, :]
    for part in range(4):
        g_fc1_bias[0:1, part * width : (part + 1) * width] = small_own[4, 10 + part : 11 + part, :]
    g_table[...] = small_own[4, 16 : 16 + g_table.shape[0], 0 : g_table.shape[1]]

    for copy in four:
        copy.wait_send()
    for copy in x_left + x_right + y_copy + small_copy:
        copy.wait_send()

    @pl.when(at_end)
    def _():
        for unit in order:
            z_copy(unit, far_end, in_peer, False).wait_send()
            z_copy(unit, far_mid, in_peer, False).wait_send()
            z_copy(unit, near_mid, in_peer, False).wait_send()

    @pl.when(jnp.logical_not(at_end))
    def _():
        for unit in order:
            z_copy(unit, far_end, in_peer, False).wait_send()
            z_copy(unit, far_mid, in_peer, True).wait_send()
            z_copy(unit, near_end, out_peer, True).wait_send()


def run_shares(at_small, at_active, b_all, small, heads, rels):
    width, tokens = at_small.shape[1:]
    ff = at_active.shape[0]
    rows = width // 16
    units = len(UNIT_LEFT)
    all_units = units + ff // width
    at_small = at_small.reshape(3, 4, 2, 2, rows, tokens)
    at_active = at_active.reshape(4, 2, 2, ff // 16, tokens)
    whole = pl.BlockSpec(memory_space=pltpu.VMEM)
    anywhere = pl.BlockSpec(memory_space=pl.ANY)
    vm = pltpu.VMEM
    dma = pltpu.SemaphoreType.DMA
    return pl.pallas_call(
        share_kernel,
        out_shape=(
            jax.ShapeDtypeStruct((rows, 3 * width), F32),
            jax.ShapeDtypeStruct((rows, width), F32),
            jax.ShapeDtypeStruct((rows, ff), F32),
            jax.ShapeDtypeStruct((ff // 16, width), F32),
            jax.ShapeDtypeStruct((4, width), F32),
            jax.ShapeDtypeStruct((6, width), F32),
            jax.ShapeDtypeStruct((1, ff), F32),
            jax.ShapeDtypeStruct((heads, rels), F32),
        ),
        in_specs=[anywhere, anywhere, anywhere, whole],
        out_specs=(whole,) * 8,
        scratch_shapes=[
            vm((3, 4, 2, rows, 2 * tokens), BF16),
            vm((units, 2 * tokens, width), BF16),
            vm((4, ff // 16, 4 * tokens), BF16),
            vm((4 * tokens, width), BF16),
            vm((units, 4, rows, width), BF16),
            vm((units, 4, rows, width), BF16),
            vm((all_units, 4, rows, width), BF16),
            vm((all_units, 4, rows, width), BF16),
            vm((all_units, rows, width), BF16),
            vm((5, 32, width), F32),
            vm((4, 32, width), F32),
            dma((6,)),
            dma((units + 3,)),
            dma((units + 3,)),
            dma((units,)),
            dma((units,)),
            dma((2, 4)),
            dma((2, 4)),
            dma((all_units, 4)),
            dma((all_units, 5)),
            dma((4,)),
            dma((4,)),
        ],
        compiler_params=pltpu.CompilerParams(
            collective_id=1, has_side_effects=True, vmem_limit_bytes=56 * 2**20
        ),
        name="shares",
    )(at_small, at_active, b_all, small)


def plain_shares(at_small, at_active, b_all, small, heads, rels):
    width = at_small.shape[1]
    ff = at_active.shape[0]
    parts = ff // width

    def scattered(left, right):
        grad = jnp.dot(left, right, preferred_element_type=F32)
        return lax.psum_scatter(grad, "batch", scatter_dimension=0, tiled=True)

    def joined(first, count):
        return jnp.concatenate([b_all[first + number] for number in range(count)], axis=1)

    g_fc1 = scattered(at_small[0], joined(0, parts))
    g_qkv = scattered(at_small[1], joined(parts, 3))
    g_out = scattered(at_small[2], b_all[parts + 3])
    g_fc2 = scattered(at_active, b_all[parts + 4])
    small = lax.psum(small, "batch")
    return (
        g_qkv,
        g_out,
        g_fc1,
        g_fc2,
        small[0:4],
        small[4:10],
        small[10:14].reshape(1, ff),
        small[16 : 16 + heads, :rels],
    )


def finish_kernel(count, *refs):
    for source, target in zip(refs[:count], refs[count:]):
        if source.shape == target.shape:
            target[...] = source[...]
        else:
            for row in range(target.shape[0]):
                target[row] = source[row : row + 1, :]


def finish(plain, spaced):
    shapes = [array.shape for array in plain] + [
        (array.shape[0], 1, array.shape[1]) for array in spaced
    ]
    arrays = list(plain) + list(spaced)
    whole = pl.BlockSpec(memory_space=pltpu.VMEM)
    return pl.pallas_call(
        functools.partial(finish_kernel, len(arrays)),
        out_shape=tuple(
            jax.ShapeDtypeStruct(shape, array.dtype) for shape, array in zip(shapes, arrays)
        ),
        in_specs=[whole] * len(arrays),
        out_specs=(whole,) * len(arrays),
        compiler_params=pltpu.CompilerParams(vmem_limit_bytes=24 * 2**20),
        name="finish",
    )(*arrays)


def per_device(
    inputs,
    cotangent,
    segments,
    row_widths,
    w_qkv,
    w_out,
    w_fc1,
    w_fc2,
    norm_gains,
    bias_rows,
    fc1_bias,
    rel_table,
):
    micro, _, slots, width = inputs.shape
    heads, rels = rel_table.shape[1:]
    weights = (w_qkv, w_out, w_fc1, w_fc2, norm_gains, bias_rows, fc1_bias, rel_table)
    activation, grad_in, at_small, at_active, b_all, small = run_block(
        inputs.reshape(micro * slots, width),
        cotangent.reshape(micro * slots, width),
        segments.reshape(micro, slots),
        row_widths.reshape(micro, row_widths.shape[2]),
        weights,
    )
    shares = run_shares if lax.axis_size("batch") == 16 else plain_shares
    grads = shares(at_small, at_active, b_all, small, heads, rels)
    g_qkv, g_out, g_fc1, g_fc2, g_gains, g_biases, g_fc1_bias, g_table = grads
    activation, grad_in, g_qkv, g_out, g_fc1, g_fc2, g_gains, g_fc1_bias, g_biases, g_table = finish(
        (activation, grad_in, g_qkv, g_out, g_fc1, g_fc2, g_gains, g_fc1_bias), (g_biases, g_table)
    )
    shape = (1, micro, 1, slots, width)
    return (
        activation.reshape(shape),
        grad_in.reshape(shape),
        g_qkv[None],
        g_out[None],
        g_fc1[None],
        g_fc2[None],
        g_gains[None],
        jnp.swapaxes(g_biases, 0, 1),
        g_fc1_bias,
        jnp.swapaxes(g_table, 0, 1),
    )


def solution(mesh):
    return jax.shard_map(
        per_device,
        mesh=mesh,
        in_specs=(
            P(None, "batch", None, None),
            P(None, "batch", None, None),
            P(None, "batch", None),
            P(None, "batch", None),
            P("section", None, None),
            P("section", None, None),
            P("section", None, None),
            P("section", None, None),
            P("section", None, None),
            P("section", None, None),
            P("section", None),
            P("section", None, None),
        ),
        out_specs=(
            P("section", None, "batch", None, None),
            P("section", None, "batch", None, None),
            P("section", "batch", None),
            P("section", "batch", None),
            P("section", "batch", None),
            P("section", "batch", None),
            P("section", None, None),
            P("section", None, None),
            P("section", None),
            P("section", None, None),
        ),
        check_vma=False,
    )
```

```python
import functools

import jax
import jax.numpy as jnp
from jax import lax
from jax.experimental import pallas as pl
from jax.experimental.pallas import tpu as pltpu
from jax.sharding import PartitionSpec as P

MESH = pl.DeviceIdType.MESH
F32 = jnp.float32
BF16 = jnp.bfloat16
REACH = 13
SPAN = 2 * REACH + 1
NORM_EPS = 1e-06
ROOT_HALF = 0.7071067811865476
INV_ROOT_TWO_PI = 0.3989422804014327
COLS = 256
GRID_ROWS = 8
GRID_COLS = 16
PITCH = 2 * GRID_COLS
WIDE = 2 * GRID_ROWS * PITCH
HALF = WIDE // 2


def nn(left, right):
    return lax.dot_general(left, right, (((1,), (0,)), ((), ())), preferred_element_type=F32)


def nt(left, right):
    return lax.dot_general(left, right, (((1,), (1,)), ((), ())), preferred_element_type=F32)


def tn(left, right):
    return lax.dot_general(left, right, (((0,), (0,)), ((), ())), preferred_element_type=F32)


def iota(shape, dim):
    return lax.broadcasted_iota(jnp.int32, shape, dim)


def two_parts(value):
    high = value.astype(BF16)
    return high, (value - high.astype(F32)).astype(BF16)


def norm_parts(values_in):
    row_mean = jnp.mean(values_in, axis=-1, keepdims=True)
    centered = values_in - row_mean
    inv_scale = lax.rsqrt(jnp.mean(centered * centered, axis=-1, keepdims=True) + NORM_EPS)
    return centered * inv_scale, inv_scale


def norm_back(upstream, normal_in, inv_scale):
    return inv_scale * (
        upstream
        - jnp.mean(upstream, axis=-1, keepdims=True)
        - normal_in * jnp.mean(upstream * normal_in, axis=-1, keepdims=True)
    )


def col_sum(value):
    return jnp.sum(value, axis=0, keepdims=True)


def cols_of(index, size=COLS):
    return slice(index * size, (index + 1) * size)


def geometry(seg, wid, same, pick_q, pick_k, pick_kt, pick_qt):
    micro, slots = seg.shape
    tokens = micro * slots
    images = wid.shape[1]
    seg_f = seg[...].astype(F32)
    seg_row = jnp.concatenate(
        [seg_f[m : m + 1, :] + float(m * images) for m in range(micro)], axis=1
    )
    sub = iota((tokens, tokens), 0)
    lane = iota((tokens, tokens), 1)
    seg_col = jnp.sum(jnp.where(sub == lane, seg_row, 0.0), axis=1, keepdims=True)
    same[...] = (seg_col == seg_row).astype(F32)
    before_row = jnp.sum((seg_col < seg_row).astype(F32), axis=0, keepdims=True)
    before_col = jnp.sum((seg_row < seg_col).astype(F32), axis=1, keepdims=True)
    place_row = iota((1, tokens), 1).astype(F32) - before_row
    place_col = iota((tokens, 1), 0).astype(F32) - before_col
    width_row = jnp.zeros((1, tokens), F32)
    width_col = jnp.zeros((tokens, 1), F32)
    for m in range(micro):
        for image in range(images):
            width = wid[m, image].astype(F32)
            number = float(m * images + image)
            width_row = width_row + jnp.where(seg_row == number, width, 0.0)
            width_col = width_col + jnp.where(seg_col == number, width, 0.0)

    def grid(place, width):
        row = jnp.zeros_like(place)
        for k in range(1, GRID_ROWS):
            row = row + (place >= float(k) * width).astype(F32)
        return row, place - row * width

    row_r, col_r = grid(place_row, width_row)
    row_c, col_c = grid(place_col, width_col)
    cells = GRID_ROWS * GRID_COLS
    pick_q[...] = (iota((tokens, cells), 1).astype(F32) == row_c * GRID_COLS + col_c).astype(
        F32
    ).astype(BF16)
    pick_qt[...] = (
        iota((cells, tokens), 0).astype(F32) == row_r * GRID_COLS + (GRID_COLS - 1.0) - col_r
    ).astype(F32).astype(BF16)
    pick_k[...] = (iota((tokens, HALF), 1).astype(F32) == row_c * PITCH + col_c).astype(
        F32
    ).astype(BF16)
    pick_kt[...] = (iota((HALF, tokens), 0).astype(F32) == row_r * PITCH + col_r).astype(
        F32
    ).astype(BF16)


def spread_table(table, padded, spread, wide_table):
    heads, _, rels = table.shape
    padded[...] = jnp.zeros_like(padded)
    for head in range(heads):
        padded[head : head + 1, 0:rels] = table[head]
    shape = spread.shape
    where = iota((1, WIDE), 1)
    signed = jnp.where(where < HALF, where, where - WIDE)
    row_step = (signed + GRID_COLS + WIDE) // PITCH - WIDE // PITCH
    col_step = signed - row_step * PITCH
    entry = (REACH - row_step) * SPAN + jnp.clip(-col_step, -REACH, REACH) + REACH
    spread[...] = (iota(shape, 0) == entry).astype(F32).astype(BF16)
    high, low = two_parts(padded[...])
    vector = nn(high, spread[...]) + nn(low, spread[...])
    cells = GRID_ROWS * GRID_COLS
    for head in range(heads):
        line = jnp.broadcast_to(vector[head : head + 1, :], (GRID_COLS, WIDE))
        line = pltpu.roll(line, 0, 1, stride=1, stride_axis=0)
        for low_row in range(4):
            turned = line if low_row == 0 else pltpu.roll(line, low_row * PITCH, 1)
            for high_row in range(GRID_ROWS // 4):
                if high_row == 0:
                    part = turned[:, 0:HALF]
                else:
                    part = jnp.concatenate(
                        [turned[:, WIDE - 4 * PITCH : WIDE], turned[:, 0 : HALF - 4 * PITCH]], axis=1
                    )
                top = (high_row * 4 + low_row) * GRID_COLS
                part_high, part_low = two_parts(part)
                wide_table[top : top + GRID_COLS, head * HALF : (head + 1) * HALF] = part_high
                wide_table[
                    cells + top : cells + top + GRID_COLS, head * HALF : (head + 1) * HALF
                ] = part_low


def fold_table(head_grad):
    total = None
    for low_row in range(4):
        near = head_grad[low_row * GRID_COLS : (low_row + 1) * GRID_COLS, :]
        far = head_grad[(low_row + 4) * GRID_COLS : (low_row + 5) * GRID_COLS, :]
        step = 4 * PITCH
        laid = jnp.concatenate(
            [
                near[:, 0:step] + far[:, step : 2 * step],
                near[:, step : 2 * step],
                jnp.zeros((GRID_COLS, step), F32),
                far[:, 0:step],
            ],
            axis=1,
        )
        if low_row > 0:
            laid = pltpu.roll(laid, WIDE - low_row * PITCH, 1)
        total = laid if total is None else total + laid
    total = pltpu.roll(total, WIDE - (GRID_COLS - 1), 1, stride=1, stride_axis=0)
    return col_sum(total)


def block_body(
    hooks,
    at_small,
    at_active,
    b_at,
    inputs,
    cotangent,
    seg,
    wid,
    wqkv_in,
    wout_in,
    wfc1_in,
    wfc2_in,
    gains,
    biases,
    fc1_bias,
    table,
    activation,
    grad_in,
    small,
    wqkv,
    wout,
    wfc1,
    wfc2,
    arrived,
    leaving,
    stream,
    hat_one,
    hat_two,
    att_out,
    branch,
    d_middle,
    d_wide,
    normed,
    qkv,
    probs,
    bias,
    mixed,
    d_mixed,
    second,
    active,
    slope,
    same,
    pick_q,
    pick_k,
    pick_kt,
    pick_qt,
    padded,
    spread,
    wide_table,
    folded,
    scale_one,
    scale_two,
    weight_sem,
    send_sem,
    recv_sem,
):
    section = lax.axis_index("section")
    place = lax.axis_index("batch")
    other = (1 - section, place)
    width = inputs.shape[1]
    tokens = inputs.shape[0]
    ff = active.shape[1]
    heads = table.shape[0]
    pair = 2 * (width // heads)
    pairs = heads // 2
    parts = ff // width
    per_part = width // COLS

    loads = [
        pltpu.make_async_copy(source.at[0], target, weight_sem.at[index])
        for index, (source, target) in enumerate(
            [(wqkv_in, wqkv), (wout_in, wout), (wfc1_in, wfc1), (wfc2_in, wfc2)]
        )
    ]
    for load in loads:
        load.start()

    hooks.greet(other)

    geometry(seg, wid, same, pick_q, pick_k, pick_kt, pick_qt)
    spread_table(table, padded, spread, wide_table)
    cells = GRID_ROWS * GRID_COLS

    def bias_of(head):
        where = cols_of(head, HALF)
        high = nn(pick_q[...], wide_table[0:cells, where]).astype(BF16)
        low = nn(pick_q[...], wide_table[cells : 2 * cells, where]).astype(BF16)
        bias[cols_of(head, tokens), :] = nn(high, pick_kt[...]) + nn(low, pick_kt[...])

    for index in range(heads):
        bias_of(index)

    hooks.met()

    def relay(source):
        return pltpu.make_async_remote_copy(
            src_ref=source,
            dst_ref=arrived,
            send_sem=send_sem,
            recv_sem=recv_sem,
            device_id=other,
            device_id_type=MESH,
        )

    @pl.when(section == 0)
    def _():
        stream[...] = inputs[...].astype(F32)

    @pl.when(section == 1)
    def _():
        relay(activation).wait_recv()
        stream[...] = arrived[...].astype(F32)

    def turn_small(number, source):
        at_small[number] = source[...].T.reshape(at_small.shape[1:])

    hat, inv_scale = norm_parts(stream[...])
    hat_one[...] = hat
    scale_one[...] = inv_scale
    normed[...] = (hat * gains[0, 0:1, :] + biases[0, 0:1, :]).astype(BF16)
    turn_small(1, normed)
    loads[0].wait()
    for third in range(3):

        def project(index):
            out = nn(normed[...], wqkv[:, cols_of(third * per_part + index)])
            if third != 1:
                row = 1 if third == 0 else 2
                out = out + biases[row, 0:1, cols_of(index)]
            qkv[third, :, cols_of(index)] = out.astype(BF16)

        for index in range(per_part):
            project(index)

    lane = iota((1, pair), 1)
    low_lanes = (lane < pair // 2).astype(F32).astype(BF16)
    high_lanes = (lane >= pair // 2).astype(F32).astype(BF16)

    def stacked(value):
        return jnp.concatenate([value * low_lanes, value * high_lanes], axis=0)

    def side_by_side(value):
        return jnp.concatenate([value[0:tokens, :], value[tokens : 2 * tokens, :]], axis=1)

    for index in range(pairs):
        at = slice(index * pair, (index + 1) * pair)
        rows = slice(index * 2 * tokens, (index + 1) * 2 * tokens)
        raw = nt(stacked(qkv[0, :, at]), qkv[1, :, at])
        mask = jnp.concatenate([same[...], same[...]], axis=0) > 0.5
        scores = jnp.where(mask, raw * 0.125 + bias[rows, :], -1e30)
        exped = jnp.exp(scores - jnp.max(scores, axis=-1, keepdims=True))
        prob = exped / jnp.sum(exped, axis=-1, keepdims=True)
        probs[rows, :] = prob
        mixed[:, at] = nn(side_by_side(prob.astype(BF16)), stacked(qkv[2, :, at])).astype(BF16)

    turn_small(2, mixed)
    loads[1].wait()

    def attend_out(index):
        at = cols_of(index)
        out = nn(mixed[...], wout[:, at]) + biases[3, 0:1, at]
        att_out[:, at] = out
        stream[:, at] = stream[:, at] + gains[0, 1:2, at] * out

    for index in range(per_part):
        attend_out(index)
    hat, inv_scale = norm_parts(stream[...])
    hat_two[...] = hat
    scale_two[...] = inv_scale
    second[...] = (hat * gains[0, 2:3, :] + biases[4, 0:1, :]).astype(BF16)
    turn_small(0, second)
    loads[2].wait()

    def feed(index):
        at = cols_of(index)
        hidden = nn(second[...], wfc1[:, at]) + fc1_bias[0:1, at]
        cumul = 0.5 * (1.0 + lax.erf(hidden * ROOT_HALF))
        density = jnp.exp(-0.5 * hidden * hidden) * INV_ROOT_TWO_PI
        active[:, at] = (hidden * cumul).astype(BF16)
        slope[:, at] = cumul + hidden * density
        if (index + 1) % per_part == 0:
            part = index // per_part
            at_active[part] = active[:, cols_of(part, width)].T.reshape(at_active.shape[1:])

    for index in range(ff // COLS):
        feed(index)
    loads[3].wait()

    def feed_out(index):
        at = cols_of(index)
        out = nn(active[...], wfc2[:, at]) + biases[5, 0:1, at]
        branch[:, at] = out
        activation[:, at] = (stream[:, at] + gains[0, 3:4, at] * out).astype(BF16)

    for index in range(per_part):
        feed_out(index)

    @pl.when(section == 0)
    def _():
        relay(activation).start()

    hooks.forward_done()

    @pl.when(section == 0)
    def _():
        relay(activation).wait_send()
        relay(activation).wait_recv()
        stream[...] = arrived[...].astype(F32)

    @pl.when(section == 1)
    def _():
        stream[...] = cotangent[...].astype(F32)

    small[...] = jnp.zeros_like(small)
    upstream = stream[...]
    small[3:4, :] = col_sum(upstream * branch[...])
    d_branch = (gains[0, 3:4, :] * upstream).astype(BF16)
    b_at(parts + 4)[...] = d_branch
    small[9:10, :] = col_sum(d_branch.astype(F32))
    hooks.branch_done()

    def feed_back(index):
        at = cols_of(index)
        out = nt(b_at(parts + 4)[...], wfc2[at, :])
        d_hidden = (out * slope[:, at]).astype(BF16)
        part = index // per_part
        inner = cols_of(index % per_part)
        b_at(part)[:, inner] = d_hidden
        small[10 + part : 11 + part, inner] = col_sum(d_hidden.astype(F32))
        if (index + 1) % per_part == 0:
            hooks.hidden_done(part)

    for index in range(ff // COLS):
        feed_back(index)

    def second_back(index):
        at = cols_of(index)
        out = nt(b_at(0)[...], wfc1[at, 0:width])
        for part in range(1, parts):
            out = out + nt(b_at(part)[...], wfc1[at, part * width : (part + 1) * width])
        d_wide[:, at] = out

    for index in range(per_part):
        second_back(index)
    d_second = d_wide[...]
    small[2:3, :] = col_sum(d_second * hat_two[...])
    small[8:9, :] = col_sum(d_second)
    d_mid = stream[...] + norm_back(d_second * gains[0, 2:3, :], hat_two[...], scale_two[...])
    d_middle[...] = d_mid
    small[1:2, :] = col_sum(d_mid * att_out[...])
    d_att = (gains[0, 1:2, :] * d_mid).astype(BF16)
    b_at(parts + 3)[...] = d_att
    small[7:8, :] = col_sum(d_att.astype(F32))
    hooks.attention_out_done()

    def out_back(index):
        at = cols_of(index)
        d_mixed[:, at] = nt(b_at(parts + 3)[...], wout[at, :]).astype(BF16)

    for index in range(per_part):
        out_back(index)

    hooks.attention_next()
    folded[...] = jnp.zeros_like(folded)
    for index in range(pairs):
        at = slice(index * pair, (index + 1) * pair)
        rows = slice(index * 2 * tokens, (index + 1) * 2 * tokens)
        prob = probs[rows, :]
        d_mix = stacked(d_mixed[:, at])
        d_prob = nt(d_mix, qkv[2, :, at])
        b_at(parts + 2)[:, at] = tn(prob.astype(BF16), d_mix).astype(BF16)
        d_scores = prob * (d_prob - jnp.sum(prob * d_prob, axis=-1, keepdims=True))
        d_raw = (0.125 * d_scores).astype(BF16)
        b_at(parts)[:, at] = nn(side_by_side(d_raw), stacked(qkv[1, :, at])).astype(BF16)
        b_at(parts + 1)[:, at] = tn(d_raw, stacked(qkv[0, :, at])).astype(BF16)
        high, low = two_parts(d_scores)
        high = nn(high, pick_k[...]).astype(BF16)
        low = nn(low, pick_k[...]).astype(BF16)
        for side in range(2):
            own = slice(side * tokens, (side + 1) * tokens)
            head_grad = nn(pick_qt[...], high[own, :]) + nn(pick_qt[...], low[own, :])
            folded[2 * index + side : 2 * index + side + 1, :] = fold_table(head_grad)

    hooks.qkv_done()
    small[5:6, :] = col_sum(b_at(parts)[...].astype(F32))
    small[6:7, :] = col_sum(b_at(parts + 2)[...].astype(F32))

    def normed_back(index):
        at = cols_of(index)
        out = nt(b_at(parts)[...], wqkv[at, 0:width])
        for third in range(1, 3):
            out = out + nt(b_at(parts + third)[...], wqkv[at, third * width : (third + 1) * width])
        d_wide[:, at] = out

    for index in range(per_part):
        normed_back(index)
    d_normed = d_wide[...]
    small[0:1, :] = col_sum(d_normed * hat_one[...])
    small[4:5, :] = col_sum(d_normed)
    d_in = d_middle[...] + norm_back(d_normed * gains[0, 0:1, :], hat_one[...], scale_one[...])
    grad_in[...] = d_in
    leaving[...] = d_in.astype(BF16)

    @pl.when(section == 1)
    def _():
        relay(leaving).start()

    high, low = two_parts(folded[...])
    small[16:32, :] = nt(high, spread[...]) + nt(low, spread[...])
    hooks.small_done()

    @pl.when(section == 1)
    def _():
        relay(leaving).wait_send()


class Alone:
    def greet(self, other):
        pl.semaphore_signal(
            pltpu.get_barrier_semaphore(), inc=1, device_id=other, device_id_type=MESH
        )

    def met(self):
        pl.semaphore_wait(pltpu.get_barrier_semaphore(), 1)

    def nothing(self, *_):
        pass

    forward_done = branch_done = hidden_done = attention_out_done = nothing
    attention_next = qkv_done = small_done = nothing


def block_kernel(*refs):
    given, (activation, grad_in, at_small, at_active, b_all, small), rest = (
        refs[:12],
        refs[12:18],
        refs[18:],
    )
    block_body(
        Alone(), at_small, at_active, lambda k: b_all.at[k], *given, activation, grad_in, small, *rest
    )


def block_specs():
    whole = pl.BlockSpec(memory_space=pltpu.VMEM)
    return (
        [whole, whole, whole, pl.BlockSpec(memory_space=pltpu.SMEM)]
        + [pl.BlockSpec(memory_space=pl.ANY)] * 4
        + [whole] * 4
    )


def block_scratch(tokens, width, ff, heads, rels):
    cells = GRID_ROWS * GRID_COLS
    padded_rels = -(-rels // 256) * 256
    vm = pltpu.VMEM
    return (
        [
            vm((width, 3 * width), BF16),
            vm((width, width), BF16),
            vm((width, ff), BF16),
            vm((ff, width), BF16),
            vm((tokens, width), BF16),
            vm((tokens, width), BF16),
        ]
        + [vm((tokens, width), F32)] * 7
        + [
            vm((tokens, width), BF16),
            vm((3, tokens, width), BF16),
            vm((heads * tokens, tokens), F32),
            vm((heads * tokens, tokens), F32),
            vm((tokens, width), BF16),
            vm((tokens, width), BF16),
            vm((tokens, width), BF16),
            vm((tokens, ff), BF16),
            vm((tokens, ff), F32),
            vm((tokens, tokens), F32),
            vm((tokens, cells), BF16),
            vm((tokens, HALF), BF16),
            vm((HALF, tokens), BF16),
            vm((cells, tokens), BF16),
            vm((16, padded_rels), F32),
            vm((padded_rels, WIDE), BF16),
            vm((2 * cells, heads * HALF), BF16),
            vm((16, WIDE), F32),
            vm((tokens, 1), F32),
            vm((tokens, 1), F32),
            pltpu.SemaphoreType.DMA((4,)),
            pltpu.SemaphoreType.DMA,
            pltpu.SemaphoreType.DMA,
        ]
    )


N_BLOCK_SCRATCH = 36
UNIT_LEFT = (0, 0, 0, 0, 1, 1, 1, 2)
UNITS = len(UNIT_LEFT)
FOUR_UNITS = 4
EARLY = ((0, 1), (2, 3))
FIRST_ORDER = (7, 4, 5, 6)
SECOND_ORDER = (8, 9, 0, 1, 10, 2, 3, 11, 7, 4, 5, 6)
DEPTHS = (2, 3, 5)


def whole_kernel(*refs):
    given, (activation, grad_in, g_all, small_sum), rest = refs[:12], refs[12:16], refs[16:]
    block_scratches = rest[:N_BLOCK_SCRATCH]
    (
        at_small,
        at_active,
        left,
        right,
        left_four,
        right_four,
        y_send,
        y_recv,
        totals,
        passing,
        inward,
        small_own,
        small_recv,
        own_sem,
        x_send_sem,
        x_recv_sem,
        y_send_sem,
        y_recv_sem,
        four_send_sem,
        four_recv_sem,
        z_send_sem,
        z_recv_sem,
        small_send_sem,
        small_recv_sem,
    ) = rest[N_BLOCK_SCRATCH:]
    section = lax.axis_index("section")
    place = lax.axis_index("batch")
    z = place // 4
    y = (place // 2) % 2
    x = place % 2
    x_peer = z * 4 + y * 2 + (1 - x)
    y_peer = z * 4 + (1 - y) * 2 + x
    xy_peer = z * 4 + (1 - y) * 2 + (1 - x)
    at_end = (z == 0) | (z == 3)
    between = jnp.logical_not(at_end)
    lower = z < 2
    in_peer = jnp.where(lower, place + 4, place - 4)
    out_peer = jnp.where(at_end, place, jnp.where(z == 1, place - 4, place + 4))
    far_peer = jnp.where(lower, place + 8, place - 8)
    pair_peer = jnp.where(z % 2 == 0, place + 4, place - 4)
    tokens = given[0].shape[0]
    rows = left.shape[3]
    width = right.shape[2]
    barrier = pltpu.get_barrier_semaphore()

    def remote(source, target, send, recv, peer):
        return pltpu.make_async_remote_copy(
            src_ref=source,
            dst_ref=target,
            send_sem=send,
            recv_sem=recv,
            device_id=(section, peer),
            device_id_type=MESH,
        )

    own = [
        pltpu.make_async_copy(
            at_small.at[number, :, :, x], left.at[number, :, :, :, 0:tokens], own_sem.at[number]
        )
        for number in range(3)
    ] + [pltpu.make_async_copy(at_active.at[:, y, x], left_four.at[:, :, 0:tokens], own_sem.at[3])]

    others = ((1, y, 1 - x, x_peer), (2, 1 - y, x, y_peer), (3, 1 - y, 1 - x, xy_peer))
    four_left = [
        remote(
            at_active.at[:, peer_y, peer_x],
            left_four.at[:, :, slot * tokens : (slot + 1) * tokens],
            four_send_sem.at[0, slot],
            four_recv_sem.at[0, slot],
            peer,
        )
        for slot, peer_y, peer_x, peer in others
    ]
    four_right = [
        remote(
            right_four.at[0:tokens, :],
            right_four.at[slot * tokens : (slot + 1) * tokens, :],
            four_send_sem.at[1, slot],
            four_recv_sem.at[1, slot],
            peer,
        )
        for slot, _, _, peer in others
    ]
    x_left = [
        remote(
            at_small.at[number, :, :, 1 - x],
            left.at[number, :, :, :, tokens : 2 * tokens],
            x_send_sem.at[UNITS + number],
            x_recv_sem.at[UNITS + number],
            x_peer,
        )
        for number in range(3)
    ]
    x_right = [
        remote(
            right.at[unit, 0:tokens, :],
            right.at[unit, tokens : 2 * tokens, :],
            x_send_sem.at[unit],
            x_recv_sem.at[unit],
            x_peer,
        )
        for unit in range(UNITS)
    ]
    y_copy = [
        remote(
            y_send.at[unit], y_recv.at[unit], y_send_sem.at[unit], y_recv_sem.at[unit], y_peer
        )
        for unit in range(UNITS)
    ]
    small_copy = [
        remote(
            small_own.at[step],
            small_recv.at[step],
            small_send_sem.at[step],
            small_recv_sem.at[step],
            peer,
        )
        for step, peer in enumerate((x_peer, y_peer, pair_peer, far_peer))
    ]

    def start(copies):
        for copy in copies:
            copy.start()

    waited = set()

    def once(name, copies):
        if name not in waited:
            waited.add(name)
            for copy in copies:
                copy.wait_recv()

    def own_ready(number):
        if ("own", number) not in waited:
            waited.add(("own", number))
            own[number].wait()

    def product(unit, side):
        lhs = left[UNIT_LEFT[unit], :, side].reshape(4 * rows, 2 * tokens)
        return nn(lhs, right[unit])

    def first(unit):
        number = UNIT_LEFT[unit]
        own_ready(number)
        once(("left", number), [x_left[number]])
        once(("right", unit), [x_right[unit]])
        y_send[unit] = product(unit, 1 - y).astype(BF16).reshape(4, rows, width)
        y_copy[unit].start()

    far_end = jnp.where(lower, 3, 0)
    far_mid = jnp.where(lower, 2, 1)
    near_mid = jnp.where(lower, 1, 2)
    near_end = jnp.where(lower, 0, 3)

    def z_copy(unit, dest, peer, final_inside):
        target = inward.at[unit] if final_inside else passing.at[unit, dest]
        slot = 4 if final_inside else dest
        return remote(
            totals.at[unit, dest],
            target,
            z_send_sem.at[unit, dest],
            z_recv_sem.at[unit, slot],
            peer,
        )

    def add_passing(unit, dest):
        totals[unit, dest] = (
            totals[unit, dest].astype(F32) + passing[unit, dest].astype(F32)
        ).astype(BF16)

    def second(unit):
        if unit >= UNITS:
            own_ready(3)
            once("four", four_left + four_right)
            piece = slice((unit - UNITS) * rows, (unit - UNITS + 1) * rows)
            lhs = left_four[:, piece, :].reshape(4 * rows, 4 * tokens)
            out = nn(lhs, right_four[...])
        else:
            out = product(unit, y)
            y_copy[unit].wait_recv()
            out = out + y_recv[unit].reshape(4 * rows, width).astype(F32)
        totals[unit] = out.astype(BF16).reshape(4, rows, width)

        @pl.when(at_end)
        def _():
            z_copy(unit, far_end, in_peer, False).start()
            z_copy(unit, far_mid, in_peer, False).start()
            z_copy(unit, near_mid, in_peer, False).start()

    def third(unit):
        @pl.when(between)
        def _():
            z_copy(unit, far_end, in_peer, False).wait_recv()
            add_passing(unit, far_end)
            z_copy(unit, far_end, in_peer, False).start()
            z_copy(unit, far_mid, in_peer, False).wait_recv()
            add_passing(unit, far_mid)
            z_copy(unit, far_mid, in_peer, True).start()

    def fourth(unit):
        @pl.when(between)
        def _():
            z_copy(unit, near_end, out_peer, False).wait_recv()
            add_passing(unit, near_end)
            z_copy(unit, near_end, out_peer, True).start()

    def fifth(unit):
        z_copy(unit, z, in_peer, True).wait_recv()
        value = totals[unit, z].astype(F32) + inward[unit].astype(F32)

        @pl.when(at_end)
        def _():
            g_all[unit] = value

        @pl.when(between)
        def _():
            z_copy(unit, z, in_peer, False).wait_recv()
            g_all[unit] = value + passing[unit, z].astype(F32)

    def small_step(step):
        small_copy[step].wait_recv()
        total = small_own[step] + small_recv[step]
        if step < 3:
            small_own[step + 1] = total
            small_copy[step + 1].start()
        else:
            small_sum[...] = total

    class Sending:
        def greet(self, other):
            pl.semaphore_signal(barrier, inc=1, device_id=other, device_id_type=MESH)
            for peer in (x_peer, y_peer, xy_peer, in_peer, far_peer):
                pl.semaphore_signal(
                    barrier, inc=1, device_id=(section, peer), device_id_type=MESH
                )

            @pl.when(between)
            def _():
                pl.semaphore_signal(
                    barrier, inc=1, device_id=(section, out_peer), device_id_type=MESH
                )

        def met(self):
            @pl.when(at_end)
            def _():
                pl.semaphore_wait(barrier, 6)

            @pl.when(between)
            def _():
                pl.semaphore_wait(barrier, 7)

        def forward_done(self):
            start(own)
            start([four_left[1], x_left[0], four_left[2], four_left[0], x_left[2], x_left[1]])

        def branch_done(self):
            start([four_right[1], four_right[2], four_right[0]])

        def hidden_done(self, part):
            x_right[part].start()

        def attention_out_done(self):
            x_right[7].start()

        def attention_next(self):
            for unit in EARLY[0]:
                first(unit)

        def qkv_done(self):
            start(x_right[4:7])
            for unit in EARLY[1]:
                first(unit)

        def small_done(self):
            small_copy[0].start()

    block_body(
        Sending(),
        at_small,
        at_active,
        lambda k: right.at[k, 0:tokens] if k < UNITS else right_four.at[0:tokens],
        *given,
        activation,
        grad_in,
        small_own.at[0],
        *block_scratches,
    )

    stages = ((second, 0), (third, DEPTHS[0]), (fourth, DEPTHS[1]), (fifth, DEPTHS[2]))
    for turn in range(len(SECOND_ORDER) + DEPTHS[2]):
        if turn < len(FIRST_ORDER):
            first(FIRST_ORDER[turn])
        for stage, depth in stages:
            if 0 <= turn - depth < len(SECOND_ORDER):
                stage(SECOND_ORDER[turn - depth])
        if turn < 4:
            small_step(turn)

    for copy in four_left + four_right + x_left + x_right + y_copy + small_copy:
        copy.wait_send()

    @pl.when(at_end)
    def _():
        for unit in SECOND_ORDER:
            z_copy(unit, far_end, in_peer, False).wait_send()
            z_copy(unit, far_mid, in_peer, False).wait_send()
            z_copy(unit, near_mid, in_peer, False).wait_send()

    @pl.when(between)
    def _():
        for unit in SECOND_ORDER:
            z_copy(unit, far_end, in_peer, False).wait_send()
            z_copy(unit, far_mid, in_peer, True).wait_send()
            z_copy(unit, near_end, out_peer, True).wait_send()


def finish_kernel(
    activation,
    grad_in,
    g_all,
    small,
    activation_out,
    grad_in_out,
    g_qkv,
    g_out,
    g_fc1,
    g_fc2,
    g_gains,
    g_biases,
    g_fc1_bias,
    g_table,
    small_here,
    sems,
):
    rows, width = g_all.shape[1:]
    pairs = [(small, small_here), (activation, activation_out), (grad_in, grad_in_out)]
    for unit in range(UNITS + FOUR_UNITS):
        if unit < 4:
            target = g_fc1.at[:, unit * width : (unit + 1) * width]
        elif unit < 7:
            target = g_qkv.at[:, (unit - 4) * width : (unit - 3) * width]
        elif unit == 7:
            target = g_out
        else:
            target = g_fc2.at[(unit - UNITS) * rows : (unit - UNITS + 1) * rows, :]
        pairs.append((g_all.at[unit], target))
    copies = [
        pltpu.make_async_copy(source, target, sems.at[index])
        for index, (source, target) in enumerate(pairs)
    ]
    for copy in copies:
        copy.start()
    copies[0].wait()
    g_gains[...] = small_here[0:4, :]
    for row in range(g_biases.shape[0]):
        g_biases[row] = small_here[4 + row : 5 + row, :]
    for part in range(4):
        g_fc1_bias[0:1, part * width : (part + 1) * width] = small_here[10 + part : 11 + part, :]
    for head in range(g_table.shape[0]):
        g_table[head] = small_here[16 + head : 17 + head, 0 : g_table.shape[2]]
    for copy in copies[1:]:
        copy.wait()


def run_whole(inputs, cotangent, seg, wid, weights):
    w_qkv, w_out, w_fc1, w_fc2, gains, biases, fc1_bias, table = weights
    tokens, width = inputs.shape
    ff = w_fc1.shape[2]
    heads, rels = table.shape[1:]
    rows = width // 16
    all_units = UNITS + FOUR_UNITS
    whole = pl.BlockSpec(memory_space=pltpu.VMEM)
    anywhere = pl.BlockSpec(memory_space=pl.ANY)
    vm = pltpu.VMEM
    dma = pltpu.SemaphoreType.DMA
    activation, grad_in, g_all, small = pl.pallas_call(
        whole_kernel,
        out_shape=(
            jax.ShapeDtypeStruct((tokens, width), BF16),
            jax.ShapeDtypeStruct((tokens, width), F32),
            jax.ShapeDtypeStruct((all_units, rows, width), F32),
            jax.ShapeDtypeStruct((32, width), F32),
        ),
        in_specs=block_specs(),
        out_specs=(whole,) * 4,
        scratch_shapes=block_scratch(tokens, width, ff, heads, rels)
        + [
            vm((3, 4, 2, 2, rows, tokens), BF16),
            vm((4, 2, 2, ff // 16, tokens), BF16),
            vm((3, 4, 2, rows, 2 * tokens), BF16),
            vm((UNITS, 2 * tokens, width), BF16),
            vm((4, ff // 16, 4 * tokens), BF16),
            vm((4 * tokens, width), BF16),
            vm((UNITS, 4, rows, width), BF16),
            vm((UNITS, 4, rows, width), BF16),
            vm((all_units, 4, rows, width), BF16),
            vm((all_units, 4, rows, width), BF16),
            vm((all_units, rows, width), BF16),
            vm((4, 32, width), F32),
            vm((4, 32, width), F32),
            dma((4,)),
            dma((UNITS + 3,)),
            dma((UNITS + 3,)),
            dma((UNITS,)),
            dma((UNITS,)),
            dma((2, 4)),
            dma((2, 4)),
            dma((all_units, 4)),
            dma((all_units, 5)),
            dma((4,)),
            dma((4,)),
        ],
        compiler_params=pltpu.CompilerParams(
            collective_id=0, has_side_effects=True, vmem_limit_bytes=60 * 2**20
        ),
        name="whole",
    )(
        inputs,
        cotangent,
        seg,
        wid,
        w_qkv,
        w_out,
        w_fc1,
        w_fc2,
        gains,
        jnp.swapaxes(biases, 0, 1),
        fc1_bias,
        jnp.swapaxes(table, 0, 1),
    )
    activation, grad_in, g_qkv, g_out, g_fc1, g_fc2, g_gains, g_biases, g_fc1_bias, g_table = (
        pl.pallas_call(
            finish_kernel,
            out_shape=(
                jax.ShapeDtypeStruct((tokens, width), BF16),
                jax.ShapeDtypeStruct((tokens, width), F32),
                jax.ShapeDtypeStruct((rows, 3 * width), F32),
                jax.ShapeDtypeStruct((rows, width), F32),
                jax.ShapeDtypeStruct((rows, ff), F32),
                jax.ShapeDtypeStruct((ff // 16, width), F32),
                jax.ShapeDtypeStruct((4, width), F32),
                jax.ShapeDtypeStruct((6, 1, width), F32),
                jax.ShapeDtypeStruct((1, ff), F32),
                jax.ShapeDtypeStruct((heads, 1, rels), F32),
            ),
            in_specs=[anywhere] * 4,
            out_specs=(whole,) * 10,
            scratch_shapes=[vm((32, width), F32), dma((all_units + 3,))],
            compiler_params=pltpu.CompilerParams(vmem_limit_bytes=60 * 2**20),
            name="finish",
        )(activation, grad_in, g_all, small)
    )
    return (
        activation,
        grad_in,
        g_qkv[None],
        g_out[None],
        g_fc1[None],
        g_fc2[None],
        g_gains[None],
        jnp.swapaxes(g_biases, 0, 1),
        g_fc1_bias,
        jnp.swapaxes(g_table, 0, 1),
    )


def run_plain(inputs, cotangent, seg, wid, weights):
    w_qkv, w_out, w_fc1, w_fc2, gains, biases, fc1_bias, table = weights
    tokens, width = inputs.shape
    ff = w_fc1.shape[2]
    heads, rels = table.shape[1:]
    parts = ff // width
    whole = pl.BlockSpec(memory_space=pltpu.VMEM)
    activation, grad_in, at_small, at_active, b_all, small = pl.pallas_call(
        block_kernel,
        out_shape=(
            jax.ShapeDtypeStruct((tokens, width), BF16),
            jax.ShapeDtypeStruct((tokens, width), F32),
            jax.ShapeDtypeStruct((3, width, tokens), BF16),
            jax.ShapeDtypeStruct((parts, width, tokens), BF16),
            jax.ShapeDtypeStruct((parts + 5, tokens, width), BF16),
            jax.ShapeDtypeStruct((32, width), F32),
        ),
        in_specs=block_specs(),
        out_specs=(whole,) * 6,
        scratch_shapes=block_scratch(tokens, width, ff, heads, rels),
        compiler_params=pltpu.CompilerParams(
            collective_id=1, has_side_effects=True, vmem_limit_bytes=56 * 2**20
        ),
        name="block",
    )(
        inputs,
        cotangent,
        seg,
        wid,
        w_qkv,
        w_out,
        w_fc1,
        w_fc2,
        gains,
        jnp.swapaxes(biases, 0, 1),
        fc1_bias,
        jnp.swapaxes(table, 0, 1),
    )

    def scattered(left, right):
        grad = jnp.dot(left, right, preferred_element_type=F32)
        return lax.psum_scatter(grad, "batch", scatter_dimension=0, tiled=True)[None]

    def joined(first, count):
        return jnp.concatenate([b_all[first + number] for number in range(count)], axis=1)

    g_fc1 = scattered(at_small[0], joined(0, parts))
    g_qkv = scattered(at_small[1], joined(parts, 3))
    g_out = scattered(at_small[2], b_all[parts + 3])
    g_fc2 = scattered(at_active.reshape(ff, tokens), b_all[parts + 4])
    small = lax.psum(small, "batch")
    return (
        activation,
        grad_in,
        g_qkv,
        g_out,
        g_fc1,
        g_fc2,
        small[None, 0:4],
        small[None, 4:10],
        small[10:14].reshape(1, ff),
        small[None, 16 : 16 + heads, :rels],
    )


def per_device(
    inputs,
    cotangent,
    segments,
    row_widths,
    w_qkv,
    w_out,
    w_fc1,
    w_fc2,
    norm_gains,
    bias_rows,
    fc1_bias,
    rel_table,
):
    micro, _, slots, width = inputs.shape
    weights = (w_qkv, w_out, w_fc1, w_fc2, norm_gains, bias_rows, fc1_bias, rel_table)
    run = run_whole if lax.axis_size("batch") == 16 else run_plain
    activation, grad_in, *grads = run(
        inputs.reshape(micro * slots, width),
        cotangent.reshape(micro * slots, width),
        segments.reshape(micro, slots),
        row_widths.reshape(micro, row_widths.shape[2]),
        weights,
    )
    shape = (1, micro, 1, slots, width)
    return (activation.reshape(shape), grad_in.reshape(shape), *grads)


def solution(mesh):
    return jax.shard_map(
        per_device,
        mesh=mesh,
        in_specs=(
            P(None, "batch", None, None),
            P(None, "batch", None, None),
            P(None, "batch", None),
            P(None, "batch", None),
            P("section", None, None),
            P("section", None, None),
            P("section", None, None),
            P("section", None, None),
            P("section", None, None),
            P("section", None, None),
            P("section", None),
            P("section", None, None),
        ),
        out_specs=(
            P("section", None, "batch", None, None),
            P("section", None, "batch", None, None),
            P("section", "batch", None),
            P("section", "batch", None),
            P("section", "batch", None),
            P("section", "batch", None),
            P("section", None, None),
            P("section", None, None),
            P("section", None),
            P("section", None, None),
        ),
        check_vma=False,
    )
```

```python
import functools

import jax
import jax.numpy as jnp
from jax import lax
from jax.experimental import pallas as pl
from jax.experimental.pallas import tpu as pltpu
from jax.sharding import PartitionSpec as P

MESH = pl.DeviceIdType.MESH
F32 = jnp.float32
BF16 = jnp.bfloat16
REACH = 13
SPAN = 2 * REACH + 1
NORM_EPS = 1e-06
ROOT_HALF = 0.7071067811865476
INV_ROOT_TWO_PI = 0.3989422804014327
COLS = 256
GRID_ROWS = 8
GRID_COLS = 16
PITCH = 2 * GRID_COLS
WIDE = 2 * GRID_ROWS * PITCH
HALF = WIDE // 2


def nn(left, right):
    return lax.dot_general(left, right, (((1,), (0,)), ((), ())), preferred_element_type=F32)


def nt(left, right):
    return lax.dot_general(left, right, (((1,), (1,)), ((), ())), preferred_element_type=F32)


def tn(left, right):
    return lax.dot_general(left, right, (((0,), (0,)), ((), ())), preferred_element_type=F32)


def iota(shape, dim):
    return lax.broadcasted_iota(jnp.int32, shape, dim)


def two_parts(value):
    high = value.astype(BF16)
    return high, (value - high.astype(F32)).astype(BF16)


def norm_parts(values_in):
    row_mean = jnp.mean(values_in, axis=-1, keepdims=True)
    centered = values_in - row_mean
    inv_scale = lax.rsqrt(jnp.mean(centered * centered, axis=-1, keepdims=True) + NORM_EPS)
    return centered * inv_scale, inv_scale


def norm_back(upstream, normal_in, inv_scale):
    return inv_scale * (
        upstream
        - jnp.mean(upstream, axis=-1, keepdims=True)
        - normal_in * jnp.mean(upstream * normal_in, axis=-1, keepdims=True)
    )


def col_sum(value):
    return jnp.sum(value, axis=0, keepdims=True)


def cols_of(index, size=COLS):
    return slice(index * size, (index + 1) * size)


def geometry(seg, wid, same, pick_q, pick_k, pick_kt, pick_qt):
    micro, slots = seg.shape
    tokens = micro * slots
    images = wid.shape[1]
    seg_f = seg[...].astype(F32)
    seg_row = jnp.concatenate(
        [seg_f[m : m + 1, :] + float(m * images) for m in range(micro)], axis=1
    )
    sub = iota((tokens, tokens), 0)
    lane = iota((tokens, tokens), 1)
    seg_col = jnp.sum(jnp.where(sub == lane, seg_row, 0.0), axis=1, keepdims=True)
    same[...] = (seg_col == seg_row).astype(F32)
    before_row = jnp.sum((seg_col < seg_row).astype(F32), axis=0, keepdims=True)
    before_col = jnp.sum((seg_row < seg_col).astype(F32), axis=1, keepdims=True)
    place_row = iota((1, tokens), 1).astype(F32) - before_row
    place_col = iota((tokens, 1), 0).astype(F32) - before_col
    width_row = jnp.zeros((1, tokens), F32)
    width_col = jnp.zeros((tokens, 1), F32)
    for m in range(micro):
        for image in range(images):
            width = wid[m, image].astype(F32)
            number = float(m * images + image)
            width_row = width_row + jnp.where(seg_row == number, width, 0.0)
            width_col = width_col + jnp.where(seg_col == number, width, 0.0)

    def grid(place, width):
        row = jnp.zeros_like(place)
        for k in range(1, GRID_ROWS):
            row = row + (place >= float(k) * width).astype(F32)
        return row, place - row * width

    row_r, col_r = grid(place_row, width_row)
    row_c, col_c = grid(place_col, width_col)
    cells = GRID_ROWS * GRID_COLS
    pick_q[...] = (iota((tokens, cells), 1).astype(F32) == row_c * GRID_COLS + col_c).astype(
        F32
    ).astype(BF16)
    pick_qt[...] = (
        iota((cells, tokens), 0).astype(F32) == row_r * GRID_COLS + (GRID_COLS - 1.0) - col_r
    ).astype(F32).astype(BF16)
    pick_k[...] = (iota((tokens, HALF), 1).astype(F32) == row_c * PITCH + col_c).astype(
        F32
    ).astype(BF16)
    pick_kt[...] = (iota((HALF, tokens), 0).astype(F32) == row_r * PITCH + col_r).astype(
        F32
    ).astype(BF16)


def spread_table(table, padded, spread, wide_table):
    heads, _, rels = table.shape
    padded[...] = jnp.zeros_like(padded)
    for head in range(heads):
        padded[head : head + 1, 0:rels] = table[head]
    shape = spread.shape
    where = iota((1, WIDE), 1)
    signed = jnp.where(where < HALF, where, where - WIDE)
    row_step = (signed + GRID_COLS + WIDE) // PITCH - WIDE // PITCH
    col_step = signed - row_step * PITCH
    entry = (REACH - row_step) * SPAN + jnp.clip(-col_step, -REACH, REACH) + REACH
    spread[...] = (iota(shape, 0) == entry).astype(F32).astype(BF16)
    high, low = two_parts(padded[...])
    vector = nn(high, spread[...]) + nn(low, spread[...])
    cells = GRID_ROWS * GRID_COLS
    for head in range(heads):
        line = jnp.broadcast_to(vector[head : head + 1, :], (GRID_COLS, WIDE))
        line = pltpu.roll(line, 0, 1, stride=1, stride_axis=0)
        for low_row in range(4):
            turned = line if low_row == 0 else pltpu.roll(line, low_row * PITCH, 1)
            for high_row in range(GRID_ROWS // 4):
                if high_row == 0:
                    part = turned[:, 0:HALF]
                else:
                    part = jnp.concatenate(
                        [turned[:, WIDE - 4 * PITCH : WIDE], turned[:, 0 : HALF - 4 * PITCH]], axis=1
                    )
                top = (high_row * 4 + low_row) * GRID_COLS
                part_high, part_low = two_parts(part)
                wide_table[top : top + GRID_COLS, head * HALF : (head + 1) * HALF] = part_high
                wide_table[
                    cells + top : cells + top + GRID_COLS, head * HALF : (head + 1) * HALF
                ] = part_low


def fold_table(head_grad):
    total = None
    for low_row in range(4):
        near = head_grad[low_row * GRID_COLS : (low_row + 1) * GRID_COLS, :]
        far = head_grad[(low_row + 4) * GRID_COLS : (low_row + 5) * GRID_COLS, :]
        step = 4 * PITCH
        laid = jnp.concatenate(
            [
                near[:, 0:step] + far[:, step : 2 * step],
                near[:, step : 2 * step],
                jnp.zeros((GRID_COLS, step), F32),
                far[:, 0:step],
            ],
            axis=1,
        )
        if low_row > 0:
            laid = pltpu.roll(laid, WIDE - low_row * PITCH, 1)
        total = laid if total is None else total + laid
    total = pltpu.roll(total, WIDE - (GRID_COLS - 1), 1, stride=1, stride_axis=0)
    return col_sum(total)


def block_body(
    hooks,
    at_small,
    at_active,
    b_at,
    inputs,
    cotangent,
    seg,
    wid,
    wqkv_in,
    wout_in,
    wfc1_in,
    wfc2_in,
    gains,
    biases,
    fc1_bias,
    table,
    activation,
    grad_in,
    small,
    wqkv,
    wout,
    wfc1,
    wfc2,
    arrived,
    leaving,
    stream,
    hat_one,
    hat_two,
    att_out,
    branch,
    d_middle,
    d_wide,
    normed,
    qkv,
    probs,
    bias,
    mixed,
    d_mixed,
    second,
    active,
    slope,
    same,
    pick_q,
    pick_k,
    pick_kt,
    pick_qt,
    padded,
    spread,
    wide_table,
    folded,
    scale_one,
    scale_two,
    weight_sem,
    send_sem,
    recv_sem,
):
    section = lax.axis_index("section")
    place = lax.axis_index("batch")
    other = (1 - section, place)
    width = inputs.shape[1]
    tokens = inputs.shape[0]
    ff = active.shape[1]
    heads = table.shape[0]
    pair = 2 * (width // heads)
    pairs = heads // 2
    parts = ff // width
    per_part = width // COLS

    loads = [
        pltpu.make_async_copy(source.at[0], target, weight_sem.at[index])
        for index, (source, target) in enumerate(
            [(wqkv_in, wqkv), (wout_in, wout), (wfc1_in, wfc1), (wfc2_in, wfc2)]
        )
    ]
    for load in loads:
        load.start()

    hooks.greet(other)

    geometry(seg, wid, same, pick_q, pick_k, pick_kt, pick_qt)
    spread_table(table, padded, spread, wide_table)
    cells = GRID_ROWS * GRID_COLS

    def bias_of(head):
        where = cols_of(head, HALF)
        high = nn(pick_q[...], wide_table[0:cells, where]).astype(BF16)
        low = nn(pick_q[...], wide_table[cells : 2 * cells, where]).astype(BF16)
        bias[cols_of(head, tokens), :] = nn(high, pick_kt[...]) + nn(low, pick_kt[...])

    for index in range(heads):
        bias_of(index)

    hooks.met()

    def relay(source):
        return pltpu.make_async_remote_copy(
            src_ref=source,
            dst_ref=arrived,
            send_sem=send_sem,
            recv_sem=recv_sem,
            device_id=other,
            device_id_type=MESH,
        )

    @pl.when(section == 0)
    def _():
        stream[...] = inputs[...].astype(F32)

    @pl.when(section == 1)
    def _():
        relay(activation).wait_recv()
        stream[...] = arrived[...].astype(F32)

    def turn_small(number, source):
        at_small[number] = source[...].T.reshape(at_small.shape[1:])
        hooks.turned(number)

    hat, inv_scale = norm_parts(stream[...])
    hat_one[...] = hat
    scale_one[...] = inv_scale
    normed[...] = (hat * gains[0, 0:1, :] + biases[0, 0:1, :]).astype(BF16)
    turn_small(1, normed)
    loads[0].wait()
    for third in range(3):

        def project(index):
            out = nn(normed[...], wqkv[:, cols_of(third * per_part + index)])
            if third != 1:
                row = 1 if third == 0 else 2
                out = out + biases[row, 0:1, cols_of(index)]
            qkv[third, :, cols_of(index)] = out.astype(BF16)

        for index in range(per_part):
            project(index)

    lane = iota((1, pair), 1)
    low_lanes = (lane < pair // 2).astype(F32).astype(BF16)
    high_lanes = (lane >= pair // 2).astype(F32).astype(BF16)

    def stacked(value):
        return jnp.concatenate([value * low_lanes, value * high_lanes], axis=0)

    def side_by_side(value):
        return jnp.concatenate([value[0:tokens, :], value[tokens : 2 * tokens, :]], axis=1)

    for index in range(pairs):
        at = slice(index * pair, (index + 1) * pair)
        rows = slice(index * 2 * tokens, (index + 1) * 2 * tokens)
        raw = nt(stacked(qkv[0, :, at]), qkv[1, :, at])
        mask = jnp.concatenate([same[...], same[...]], axis=0) > 0.5
        scores = jnp.where(mask, raw * 0.125 + bias[rows, :], -1e30)
        exped = jnp.exp(scores - jnp.max(scores, axis=-1, keepdims=True))
        prob = exped / jnp.sum(exped, axis=-1, keepdims=True)
        probs[rows, :] = prob
        mixed[:, at] = nn(side_by_side(prob.astype(BF16)), stacked(qkv[2, :, at])).astype(BF16)

    turn_small(2, mixed)
    loads[1].wait()

    def attend_out(index):
        at = cols_of(index)
        out = nn(mixed[...], wout[:, at]) + biases[3, 0:1, at]
        att_out[:, at] = out
        stream[:, at] = stream[:, at] + gains[0, 1:2, at] * out

    for index in range(per_part):
        attend_out(index)
    hat, inv_scale = norm_parts(stream[...])
    hat_two[...] = hat
    scale_two[...] = inv_scale
    second[...] = (hat * gains[0, 2:3, :] + biases[4, 0:1, :]).astype(BF16)
    turn_small(0, second)
    loads[2].wait()

    def feed(index):
        at = cols_of(index)
        hidden = nn(second[...], wfc1[:, at]) + fc1_bias[0:1, at]
        cumul = 0.5 * (1.0 + lax.erf(hidden * ROOT_HALF))
        density = jnp.exp(-0.5 * hidden * hidden) * INV_ROOT_TWO_PI
        active[:, at] = (hidden * cumul).astype(BF16)
        slope[:, at] = cumul + hidden * density
        if (index + 1) % per_part == 0:
            part = index // per_part
            at_active[part] = active[:, cols_of(part, width)].T.reshape(at_active.shape[1:])

    for index in range(ff // COLS):
        feed(index)
    loads[3].wait()

    def feed_out(index):
        at = cols_of(index)
        out = nn(active[...], wfc2[:, at]) + biases[5, 0:1, at]
        branch[:, at] = out
        activation[:, at] = (stream[:, at] + gains[0, 3:4, at] * out).astype(BF16)

    for index in range(per_part):
        feed_out(index)

    @pl.when(section == 0)
    def _():
        relay(activation).start()

    hooks.forward_done()

    @pl.when(section == 0)
    def _():
        relay(activation).wait_send()
        relay(activation).wait_recv()
        stream[...] = arrived[...].astype(F32)

    @pl.when(section == 1)
    def _():
        stream[...] = cotangent[...].astype(F32)

    small[...] = jnp.zeros_like(small)
    upstream = stream[...]
    small[3:4, :] = col_sum(upstream * branch[...])
    d_branch = (gains[0, 3:4, :] * upstream).astype(BF16)
    b_at(parts + 4)[...] = d_branch
    small[9:10, :] = col_sum(d_branch.astype(F32))
    hooks.branch_done()

    def feed_back(index):
        at = cols_of(index)
        out = nt(b_at(parts + 4)[...], wfc2[at, :])
        d_hidden = (out * slope[:, at]).astype(BF16)
        part = index // per_part
        inner = cols_of(index % per_part)
        b_at(part)[:, inner] = d_hidden
        small[10 + part : 11 + part, inner] = col_sum(d_hidden.astype(F32))
        if (index + 1) % per_part == 0:
            hooks.hidden_done(part)

    for index in range(ff // COLS):
        feed_back(index)

    def second_back(index):
        at = cols_of(index)
        out = nt(b_at(0)[...], wfc1[at, 0:width])
        for part in range(1, parts):
            out = out + nt(b_at(part)[...], wfc1[at, part * width : (part + 1) * width])
        d_wide[:, at] = out

    for index in range(per_part):
        second_back(index)
    d_second = d_wide[...]
    small[2:3, :] = col_sum(d_second * hat_two[...])
    small[8:9, :] = col_sum(d_second)
    d_mid = stream[...] + norm_back(d_second * gains[0, 2:3, :], hat_two[...], scale_two[...])
    d_middle[...] = d_mid
    small[1:2, :] = col_sum(d_mid * att_out[...])
    d_att = (gains[0, 1:2, :] * d_mid).astype(BF16)
    b_at(parts + 3)[...] = d_att
    small[7:8, :] = col_sum(d_att.astype(F32))
    hooks.attention_out_done()

    def out_back(index):
        at = cols_of(index)
        d_mixed[:, at] = nt(b_at(parts + 3)[...], wout[at, :]).astype(BF16)

    for index in range(per_part):
        out_back(index)

    hooks.attention_next()
    folded[...] = jnp.zeros_like(folded)
    for index in range(pairs):
        at = slice(index * pair, (index + 1) * pair)
        rows = slice(index * 2 * tokens, (index + 1) * 2 * tokens)
        prob = probs[rows, :]
        d_mix = stacked(d_mixed[:, at])
        d_prob = nt(d_mix, qkv[2, :, at])
        b_at(parts + 2)[:, at] = tn(prob.astype(BF16), d_mix).astype(BF16)
        d_scores = prob * (d_prob - jnp.sum(prob * d_prob, axis=-1, keepdims=True))
        d_raw = (0.125 * d_scores).astype(BF16)
        b_at(parts)[:, at] = nn(side_by_side(d_raw), stacked(qkv[1, :, at])).astype(BF16)
        b_at(parts + 1)[:, at] = tn(d_raw, stacked(qkv[0, :, at])).astype(BF16)
        high, low = two_parts(d_scores)
        high = nn(high, pick_k[...]).astype(BF16)
        low = nn(low, pick_k[...]).astype(BF16)
        for side in range(2):
            own = slice(side * tokens, (side + 1) * tokens)
            head_grad = nn(pick_qt[...], high[own, :]) + nn(pick_qt[...], low[own, :])
            folded[2 * index + side : 2 * index + side + 1, :] = fold_table(head_grad)

    hooks.qkv_done()
    small[5:6, :] = col_sum(b_at(parts)[...].astype(F32))
    small[6:7, :] = col_sum(b_at(parts + 2)[...].astype(F32))

    def normed_back(index):
        at = cols_of(index)
        out = nt(b_at(parts)[...], wqkv[at, 0:width])
        for third in range(1, 3):
            out = out + nt(b_at(parts + third)[...], wqkv[at, third * width : (third + 1) * width])
        d_wide[:, at] = out

    for index in range(per_part):
        normed_back(index)
    d_normed = d_wide[...]
    small[0:1, :] = col_sum(d_normed * hat_one[...])
    small[4:5, :] = col_sum(d_normed)
    d_in = d_middle[...] + norm_back(d_normed * gains[0, 0:1, :], hat_one[...], scale_one[...])
    grad_in[...] = d_in
    leaving[...] = d_in.astype(BF16)

    @pl.when(section == 1)
    def _():
        relay(leaving).start()

    high, low = two_parts(folded[...])
    small[16:32, :] = nt(high, spread[...]) + nt(low, spread[...])
    hooks.small_done()

    @pl.when(section == 1)
    def _():
        relay(leaving).wait_send()


class Alone:
    def greet(self, other):
        pl.semaphore_signal(
            pltpu.get_barrier_semaphore(), inc=1, device_id=other, device_id_type=MESH
        )

    def met(self):
        pl.semaphore_wait(pltpu.get_barrier_semaphore(), 1)

    def nothing(self, *_):
        pass

    turned = forward_done = branch_done = hidden_done = attention_out_done = nothing
    attention_next = qkv_done = small_done = nothing


def block_kernel(*refs):
    given, (activation, grad_in, at_small, at_active, b_all, small), rest = (
        refs[:12],
        refs[12:18],
        refs[18:],
    )
    block_body(
        Alone(), at_small, at_active, lambda k: b_all.at[k], *given, activation, grad_in, small, *rest
    )


def block_specs():
    whole = pl.BlockSpec(memory_space=pltpu.VMEM)
    return (
        [whole, whole, whole, pl.BlockSpec(memory_space=pltpu.SMEM)]
        + [pl.BlockSpec(memory_space=pl.ANY)] * 4
        + [whole] * 4
    )


def block_scratch(tokens, width, ff, heads, rels):
    cells = GRID_ROWS * GRID_COLS
    padded_rels = -(-rels // 256) * 256
    vm = pltpu.VMEM
    return (
        [
            vm((width, 3 * width), BF16),
            vm((width, width), BF16),
            vm((width, ff), BF16),
            vm((ff, width), BF16),
            vm((tokens, width), BF16),
            vm((tokens, width), BF16),
        ]
        + [vm((tokens, width), F32)] * 7
        + [
            vm((tokens, width), BF16),
            vm((3, tokens, width), BF16),
            vm((heads * tokens, tokens), F32),
            vm((heads * tokens, tokens), F32),
            vm((tokens, width), BF16),
            vm((tokens, width), BF16),
            vm((tokens, width), BF16),
            vm((tokens, ff), BF16),
            vm((tokens, ff), F32),
            vm((tokens, tokens), F32),
            vm((tokens, cells), BF16),
            vm((tokens, HALF), BF16),
            vm((HALF, tokens), BF16),
            vm((cells, tokens), BF16),
            vm((16, padded_rels), F32),
            vm((padded_rels, WIDE), BF16),
            vm((2 * cells, heads * HALF), BF16),
            vm((16, WIDE), F32),
            vm((tokens, 1), F32),
            vm((tokens, 1), F32),
            pltpu.SemaphoreType.DMA((4,)),
            pltpu.SemaphoreType.DMA,
            pltpu.SemaphoreType.DMA,
        ]
    )


N_BLOCK_SCRATCH = 36
UNIT_LEFT = (0, 0, 0, 0, 1, 1, 1, 2)
UNITS = len(UNIT_LEFT)
FOUR_UNITS = 4
AHEAD = 3
FOUR_AT = 0


def schedule(firsts, seconds, depths, small_at, started=0):
    ops = []
    for turn in range(started, len(seconds) + depths[2]):
        if turn - started < len(firsts):
            ops.append(f"x{firsts[turn - started]}")
        for name, depth in zip("yzwe", (0,) + depths):
            if max(0, started if depth == 0 else 0) <= turn - depth < len(seconds):
                ops.append(f"{name}{seconds[turn - depth]}")
        if turn == small_at:
            ops.append("s")
    for unit in seconds[: max(0, started - depths[0])]:
        ops.insert(0, f"z{unit}")
    return " ".join(ops + ["t"])


OPS = (
    "",
    "y8 y9",
    schedule((0, 1, 2, 3, 7, 4, 5, 6), (8, 9, 10, 11, 0, 1, 2, 3, 7, 4, 5, 6), (2, 3, 5), 12, 2),
)


def whole_kernel(*refs):
    given, (activation, grad_in, g_all, small_sum), rest = refs[:12], refs[12:16], refs[16:]
    block_scratches = rest[:N_BLOCK_SCRATCH]
    (
        at_small,
        at_active,
        left,
        right,
        left_four,
        right_four,
        y_send,
        y_recv,
        totals,
        passing,
        inward,
        small,
        small_parts,
        small_in,
        small_all,
        own_sem,
        x_send_sem,
        x_recv_sem,
        y_send_sem,
        y_recv_sem,
        four_send_sem,
        four_recv_sem,
        z_send_sem,
        z_recv_sem,
        small_sem,
    ) = rest[N_BLOCK_SCRATCH:]
    section = lax.axis_index("section")
    place = lax.axis_index("batch")
    z = place // 4
    y = (place // 2) % 2
    x = place % 2
    x_peer = z * 4 + y * 2 + (1 - x)
    y_peer = z * 4 + (1 - y) * 2 + x
    xy_peer = z * 4 + (1 - y) * 2 + (1 - x)
    at_end = (z == 0) | (z == 3)
    between = jnp.logical_not(at_end)
    lower = z < 2
    in_peer = jnp.where(lower, place + 4, place - 4)
    out_peer = jnp.where(at_end, place, jnp.where(z == 1, place - 4, place + 4))
    tokens = given[0].shape[0]
    rows = left.shape[3]
    width = right.shape[2]
    barrier = pltpu.get_barrier_semaphore()

    def remote(source, target, send, recv, peer):
        return pltpu.make_async_remote_copy(
            src_ref=source,
            dst_ref=target,
            send_sem=send,
            recv_sem=recv,
            device_id=(section, peer),
            device_id_type=MESH,
        )

    own = [
        pltpu.make_async_copy(
            at_small.at[number, :, :, x], left.at[number, :, :, :, 0:tokens], own_sem.at[number]
        )
        for number in range(3)
    ] + [pltpu.make_async_copy(at_active.at[:, y, x], left_four.at[:, :, 0:tokens], own_sem.at[3])]

    others = ((1, y, 1 - x, x_peer), (2, 1 - y, x, y_peer), (3, 1 - y, 1 - x, xy_peer))
    four_left = [
        remote(
            at_active.at[:, peer_y, peer_x],
            left_four.at[:, :, slot * tokens : (slot + 1) * tokens],
            four_send_sem.at[0, slot],
            four_recv_sem.at[0, slot],
            peer,
        )
        for slot, peer_y, peer_x, peer in others
    ]
    four_right = [
        remote(
            right_four.at[0:tokens, :],
            right_four.at[slot * tokens : (slot + 1) * tokens, :],
            four_send_sem.at[1, slot],
            four_recv_sem.at[1, slot],
            peer,
        )
        for slot, _, _, peer in others
    ]
    x_left = [
        remote(
            at_small.at[number, :, :, 1 - x],
            left.at[number, :, :, :, tokens : 2 * tokens],
            x_send_sem.at[UNITS + number],
            x_recv_sem.at[UNITS + number],
            x_peer,
        )
        for number in range(3)
    ]
    x_right = [
        remote(
            right.at[unit, 0:tokens, :],
            right.at[unit, tokens : 2 * tokens, :],
            x_send_sem.at[unit],
            x_recv_sem.at[unit],
            x_peer,
        )
        for unit in range(UNITS)
    ]
    y_copy = [
        remote(
            y_send.at[unit], y_recv.at[unit], y_send_sem.at[unit], y_recv_sem.at[unit], y_peer
        )
        for unit in range(UNITS)
    ]
    small_out = [
        remote(
            small_parts.at[place ^ step],
            small_in.at[place],
            small_sem.at[0, step],
            small_sem.at[1, step],
            place ^ step,
        )
        for step in range(1, 16)
    ]
    small_back = [
        remote(
            small_all.at[place],
            small_all.at[place],
            small_sem.at[2, step],
            small_sem.at[3, step],
            place ^ step,
        )
        for step in range(1, 16)
    ]

    def start(copies):
        for copy in copies:
            copy.start()

    waited = set()

    def once(name, copies):
        if name not in waited:
            waited.add(name)
            for copy in copies:
                copy.wait_recv()

    def own_ready(number):
        if ("own", number) not in waited:
            waited.add(("own", number))
            own[number].wait()

    def product(unit, side):
        lhs = left[UNIT_LEFT[unit], :, side].reshape(4 * rows, 2 * tokens)
        return nn(lhs, right[unit])

    ready, sent, used = [], [], []

    def issue(units):
        ready.extend(units)
        while len(sent) < len(ready) and len(sent) - len(used) < AHEAD:
            x_right[ready[len(sent)]].start()
            sent.append(ready[len(sent)])

    def first(unit):
        number = UNIT_LEFT[unit]
        own_ready(number)
        once(("left", number), [x_left[number]])
        once(("right", unit), [x_right[unit]])
        used.append(unit)
        issue([])
        y_send[unit] = product(unit, 1 - y).astype(BF16).reshape(4, rows, width)
        y_copy[unit].start()

    far_end = jnp.where(lower, 3, 0)
    far_mid = jnp.where(lower, 2, 1)
    near_mid = jnp.where(lower, 1, 2)
    near_end = jnp.where(lower, 0, 3)

    def z_copy(unit, dest, peer, final_inside):
        target = inward.at[unit] if final_inside else passing.at[unit, dest]
        slot = 4 if final_inside else dest
        return remote(
            totals.at[unit, dest],
            target,
            z_send_sem.at[unit, dest],
            z_recv_sem.at[unit, slot],
            peer,
        )

    def add_passing(unit, dest):
        totals[unit, dest] = (
            totals[unit, dest].astype(F32) + passing[unit, dest].astype(F32)
        ).astype(BF16)

    def second(unit):
        if unit >= UNITS:
            own_ready(3)
            once("four", four_left + four_right)
            piece = slice((unit - UNITS) * rows, (unit - UNITS + 1) * rows)
            lhs = left_four[:, piece, :].reshape(4 * rows, 4 * tokens)
            out = nn(lhs, right_four[...])
        else:
            out = product(unit, y)
            y_copy[unit].wait_recv()
            out = out + y_recv[unit].reshape(4 * rows, width).astype(F32)
        totals[unit] = out.astype(BF16).reshape(4, rows, width)

        @pl.when(at_end)
        def _():
            z_copy(unit, far_end, in_peer, False).start()
            z_copy(unit, far_mid, in_peer, False).start()
            z_copy(unit, near_mid, in_peer, False).start()

    def third(unit):
        @pl.when(between)
        def _():
            z_copy(unit, far_end, in_peer, False).wait_recv()
            add_passing(unit, far_end)
            z_copy(unit, far_end, in_peer, False).start()
            z_copy(unit, far_mid, in_peer, False).wait_recv()
            add_passing(unit, far_mid)
            z_copy(unit, far_mid, in_peer, True).start()

    def fourth(unit):
        @pl.when(between)
        def _():
            z_copy(unit, near_end, out_peer, False).wait_recv()
            add_passing(unit, near_end)
            z_copy(unit, near_end, out_peer, True).start()

    def fifth(unit):
        z_copy(unit, z, in_peer, True).wait_recv()
        value = totals[unit, z].astype(F32) + inward[unit].astype(F32)

        @pl.when(at_end)
        def _():
            g_all[unit] = value

        @pl.when(between)
        def _():
            z_copy(unit, z, in_peer, False).wait_recv()
            g_all[unit] = value + passing[unit, z].astype(F32)

    def small_first():
        for index in range(16):
            small_parts[index] = small[2 * index : 2 * index + 2, :]
        start(small_out)

    def small_second():
        total = small_parts[place]
        for step, copy in enumerate(small_out, 1):
            copy.wait_recv()
            total = total + small_in[place ^ step]
        small_all[place] = total
        start(small_back)

    def small_third():
        for copy in small_back:
            copy.wait_recv()
        for index in range(16):
            small_sum[2 * index : 2 * index + 2, :] = small_all[index]

    stages = {"x": first, "y": second, "z": third, "w": fourth, "e": fifth}

    def run_ops(ops):
        for op in ops.split():
            if op == "s":
                small_second()
            elif op == "t":
                small_third()
            else:
                stages[op[0]](int(op[1:]))

    class Sending:
        def greet(self, other):
            pl.semaphore_signal(barrier, inc=1, device_id=other, device_id_type=MESH)
            for step in range(1, 16):
                pl.semaphore_signal(
                    barrier, inc=1, device_id=(section, place ^ step), device_id_type=MESH
                )

        def met(self):
            pl.semaphore_wait(barrier, 16)

        def turned(self, number):
            own[number].start()
            x_left[number].start()

        def forward_done(self):
            own[3].start()
            start(four_left)

        def branch_done(self):
            start([four_right[1]])
            if FOUR_AT == 0:
                start([four_right[0], four_right[2]])

        def hidden_done(self, part):
            issue([part])
            if part == 1 and FOUR_AT == 1:
                start([four_right[0], four_right[2]])

        def attention_out_done(self):
            issue([7])

        def attention_next(self):
            run_ops(OPS[0])

        def qkv_done(self):
            issue([4, 5, 6])
            run_ops(OPS[1])

        def small_done(self):
            small_first()

    block_body(
        Sending(),
        at_small,
        at_active,
        lambda k: right.at[k, 0:tokens] if k < UNITS else right_four.at[0:tokens],
        *given,
        activation,
        grad_in,
        small,
        *block_scratches,
    )

    run_ops(OPS[2])

    for copy in four_left + four_right + x_left + x_right + y_copy + small_out + small_back:
        copy.wait_send()

    @pl.when(at_end)
    def _():
        for unit in range(UNITS + FOUR_UNITS):
            z_copy(unit, far_end, in_peer, False).wait_send()
            z_copy(unit, far_mid, in_peer, False).wait_send()
            z_copy(unit, near_mid, in_peer, False).wait_send()

    @pl.when(between)
    def _():
        for unit in range(UNITS + FOUR_UNITS):
            z_copy(unit, far_end, in_peer, False).wait_send()
            z_copy(unit, far_mid, in_peer, True).wait_send()
            z_copy(unit, near_end, out_peer, True).wait_send()


def finish_kernel(
    activation,
    grad_in,
    g_all,
    small,
    activation_out,
    grad_in_out,
    g_qkv,
    g_out,
    g_fc1,
    g_fc2,
    g_gains,
    g_biases,
    g_fc1_bias,
    g_table,
    small_here,
    sems,
):
    rows, width = g_all.shape[1:]
    pairs = [(small, small_here), (activation, activation_out), (grad_in, grad_in_out)]
    for unit in range(UNITS + FOUR_UNITS):
        if unit < 4:
            target = g_fc1.at[:, unit * width : (unit + 1) * width]
        elif unit < 7:
            target = g_qkv.at[:, (unit - 4) * width : (unit - 3) * width]
        elif unit == 7:
            target = g_out
        else:
            target = g_fc2.at[(unit - UNITS) * rows : (unit - UNITS + 1) * rows, :]
        pairs.append((g_all.at[unit], target))
    copies = [
        pltpu.make_async_copy(source, target, sems.at[index])
        for index, (source, target) in enumerate(pairs)
    ]
    for copy in copies:
        copy.start()
    copies[0].wait()
    g_gains[...] = small_here[0:4, :]
    for row in range(g_biases.shape[0]):
        g_biases[row] = small_here[4 + row : 5 + row, :]
    for part in range(4):
        g_fc1_bias[0:1, part * width : (part + 1) * width] = small_here[10 + part : 11 + part, :]
    for head in range(g_table.shape[0]):
        g_table[head] = small_here[16 + head : 17 + head, 0 : g_table.shape[2]]
    for copy in copies[1:]:
        copy.wait()


def run_whole(inputs, cotangent, seg, wid, weights):
    w_qkv, w_out, w_fc1, w_fc2, gains, biases, fc1_bias, table = weights
    tokens, width = inputs.shape
    ff = w_fc1.shape[2]
    heads, rels = table.shape[1:]
    rows = width // 16
    all_units = UNITS + FOUR_UNITS
    whole = pl.BlockSpec(memory_space=pltpu.VMEM)
    anywhere = pl.BlockSpec(memory_space=pl.ANY)
    vm = pltpu.VMEM
    dma = pltpu.SemaphoreType.DMA
    activation, grad_in, g_all, small = pl.pallas_call(
        whole_kernel,
        out_shape=(
            jax.ShapeDtypeStruct((tokens, width), BF16),
            jax.ShapeDtypeStruct((tokens, width), F32),
            jax.ShapeDtypeStruct((all_units, rows, width), F32),
            jax.ShapeDtypeStruct((32, width), F32),
        ),
        in_specs=block_specs(),
        out_specs=(whole,) * 4,
        scratch_shapes=block_scratch(tokens, width, ff, heads, rels)
        + [
            vm((3, 4, 2, 2, rows, tokens), BF16),
            vm((4, 2, 2, ff // 16, tokens), BF16),
            vm((3, 4, 2, rows, 2 * tokens), BF16),
            vm((UNITS, 2 * tokens, width), BF16),
            vm((4, ff // 16, 4 * tokens), BF16),
            vm((4 * tokens, width), BF16),
            vm((UNITS, 4, rows, width), BF16),
            vm((UNITS, 4, rows, width), BF16),
            vm((all_units, 4, rows, width), BF16),
            vm((all_units, 4, rows, width), BF16),
            vm((all_units, rows, width), BF16),
            vm((32, width), F32),
            vm((16, 2, width), F32),
            vm((16, 2, width), F32),
            vm((16, 2, width), F32),
            dma((4,)),
            dma((UNITS + 3,)),
            dma((UNITS + 3,)),
            dma((UNITS,)),
            dma((UNITS,)),
            dma((2, 4)),
            dma((2, 4)),
            dma((all_units, 4)),
            dma((all_units, 5)),
            dma((4, 16)),
        ],
        compiler_params=pltpu.CompilerParams(
            collective_id=0, has_side_effects=True, vmem_limit_bytes=60 * 2**20
        ),
        name="whole",
    )(
        inputs,
        cotangent,
        seg,
        wid,
        w_qkv,
        w_out,
        w_fc1,
        w_fc2,
        gains,
        jnp.swapaxes(biases, 0, 1),
        fc1_bias,
        jnp.swapaxes(table, 0, 1),
    )
    activation, grad_in, g_qkv, g_out, g_fc1, g_fc2, g_gains, g_biases, g_fc1_bias, g_table = (
        pl.pallas_call(
            finish_kernel,
            out_shape=(
                jax.ShapeDtypeStruct((tokens, width), BF16),
                jax.ShapeDtypeStruct((tokens, width), F32),
                jax.ShapeDtypeStruct((rows, 3 * width), F32),
                jax.ShapeDtypeStruct((rows, width), F32),
                jax.ShapeDtypeStruct((rows, ff), F32),
                jax.ShapeDtypeStruct((ff // 16, width), F32),
                jax.ShapeDtypeStruct((4, width), F32),
                jax.ShapeDtypeStruct((6, 1, width), F32),
                jax.ShapeDtypeStruct((1, ff), F32),
                jax.ShapeDtypeStruct((heads, 1, rels), F32),
            ),
            in_specs=[anywhere] * 4,
            out_specs=(whole,) * 10,
            scratch_shapes=[vm((32, width), F32), dma((all_units + 3,))],
            compiler_params=pltpu.CompilerParams(vmem_limit_bytes=60 * 2**20),
            name="finish",
        )(activation, grad_in, g_all, small)
    )
    return (
        activation,
        grad_in,
        g_qkv[None],
        g_out[None],
        g_fc1[None],
        g_fc2[None],
        g_gains[None],
        jnp.swapaxes(g_biases, 0, 1),
        g_fc1_bias,
        jnp.swapaxes(g_table, 0, 1),
    )


def run_plain(inputs, cotangent, seg, wid, weights):
    w_qkv, w_out, w_fc1, w_fc2, gains, biases, fc1_bias, table = weights
    tokens, width = inputs.shape
    ff = w_fc1.shape[2]
    heads, rels = table.shape[1:]
    parts = ff // width
    whole = pl.BlockSpec(memory_space=pltpu.VMEM)
    activation, grad_in, at_small, at_active, b_all, small = pl.pallas_call(
        block_kernel,
        out_shape=(
            jax.ShapeDtypeStruct((tokens, width), BF16),
            jax.ShapeDtypeStruct((tokens, width), F32),
            jax.ShapeDtypeStruct((3, width, tokens), BF16),
            jax.ShapeDtypeStruct((parts, width, tokens), BF16),
            jax.ShapeDtypeStruct((parts + 5, tokens, width), BF16),
            jax.ShapeDtypeStruct((32, width), F32),
        ),
        in_specs=block_specs(),
        out_specs=(whole,) * 6,
        scratch_shapes=block_scratch(tokens, width, ff, heads, rels),
        compiler_params=pltpu.CompilerParams(
            collective_id=1, has_side_effects=True, vmem_limit_bytes=56 * 2**20
        ),
        name="block",
    )(
        inputs,
        cotangent,
        seg,
        wid,
        w_qkv,
        w_out,
        w_fc1,
        w_fc2,
        gains,
        jnp.swapaxes(biases, 0, 1),
        fc1_bias,
        jnp.swapaxes(table, 0, 1),
    )

    def scattered(left, right):
        grad = jnp.dot(left, right, preferred_element_type=F32)
        return lax.psum_scatter(grad, "batch", scatter_dimension=0, tiled=True)[None]

    def joined(first, count):
        return jnp.concatenate([b_all[first + number] for number in range(count)], axis=1)

    g_fc1 = scattered(at_small[0], joined(0, parts))
    g_qkv = scattered(at_small[1], joined(parts, 3))
    g_out = scattered(at_small[2], b_all[parts + 3])
    g_fc2 = scattered(at_active.reshape(ff, tokens), b_all[parts + 4])
    small = lax.psum(small, "batch")
    return (
        activation,
        grad_in,
        g_qkv,
        g_out,
        g_fc1,
        g_fc2,
        small[None, 0:4],
        small[None, 4:10],
        small[10:14].reshape(1, ff),
        small[None, 16 : 16 + heads, :rels],
    )


def per_device(
    inputs,
    cotangent,
    segments,
    row_widths,
    w_qkv,
    w_out,
    w_fc1,
    w_fc2,
    norm_gains,
    bias_rows,
    fc1_bias,
    rel_table,
):
    micro, _, slots, width = inputs.shape
    weights = (w_qkv, w_out, w_fc1, w_fc2, norm_gains, bias_rows, fc1_bias, rel_table)
    run = run_whole if lax.axis_size("batch") == 16 else run_plain
    activation, grad_in, *grads = run(
        inputs.reshape(micro * slots, width),
        cotangent.reshape(micro * slots, width),
        segments.reshape(micro, slots),
        row_widths.reshape(micro, row_widths.shape[2]),
        weights,
    )
    shape = (1, micro, 1, slots, width)
    return (activation.reshape(shape), grad_in.reshape(shape), *grads)


def solution(mesh):
    return jax.shard_map(
        per_device,
        mesh=mesh,
        in_specs=(
            P(None, "batch", None, None),
            P(None, "batch", None, None),
            P(None, "batch", None),
            P(None, "batch", None),
            P("section", None, None),
            P("section", None, None),
            P("section", None, None),
            P("section", None, None),
            P("section", None, None),
            P("section", None, None),
            P("section", None),
            P("section", None, None),
        ),
        out_specs=(
            P("section", None, "batch", None, None),
            P("section", None, "batch", None, None),
            P("section", "batch", None),
            P("section", "batch", None),
            P("section", "batch", None),
            P("section", "batch", None),
            P("section", None, None),
            P("section", None, None),
            P("section", None),
            P("section", None, None),
        ),
        check_vma=False,
    )
```

```python
import functools

import jax
import jax.numpy as jnp
from jax import lax
from jax.experimental import pallas as pl
from jax.experimental.pallas import tpu as pltpu
from jax.sharding import PartitionSpec as P

MESH = pl.DeviceIdType.MESH
F32 = jnp.float32
BF16 = jnp.bfloat16
REACH = 13
SPAN = 2 * REACH + 1
NORM_EPS = 1e-06
ROOT_HALF = 0.7071067811865476
INV_ROOT_TWO_PI = 0.3989422804014327
COLS = 256
GRID_ROWS = 8
GRID_COLS = 16
PITCH = 2 * GRID_COLS
WIDE = 2 * GRID_ROWS * PITCH
HALF = WIDE // 2


def nn(left, right):
    return lax.dot_general(left, right, (((1,), (0,)), ((), ())), preferred_element_type=F32)


def nt(left, right):
    return lax.dot_general(left, right, (((1,), (1,)), ((), ())), preferred_element_type=F32)


def tn(left, right):
    return lax.dot_general(left, right, (((0,), (0,)), ((), ())), preferred_element_type=F32)


def iota(shape, dim):
    return lax.broadcasted_iota(jnp.int32, shape, dim)


def two_parts(value):
    high = value.astype(BF16)
    return high, (value - high.astype(F32)).astype(BF16)


def norm_parts(values_in):
    row_mean = jnp.mean(values_in, axis=-1, keepdims=True)
    centered = values_in - row_mean
    inv_scale = lax.rsqrt(jnp.mean(centered * centered, axis=-1, keepdims=True) + NORM_EPS)
    return centered * inv_scale, inv_scale


def norm_back(upstream, normal_in, inv_scale):
    return inv_scale * (
        upstream
        - jnp.mean(upstream, axis=-1, keepdims=True)
        - normal_in * jnp.mean(upstream * normal_in, axis=-1, keepdims=True)
    )


def col_sum(value):
    return jnp.sum(value, axis=0, keepdims=True)


def cols_of(index, size=COLS):
    return slice(index * size, (index + 1) * size)


def geometry(seg, wid, same, pick_q, pick_k, pick_kt, pick_qt):
    micro, slots = seg.shape
    tokens = micro * slots
    images = wid.shape[1]
    seg_f = seg[...].astype(F32)
    seg_row = jnp.concatenate(
        [seg_f[m : m + 1, :] + float(m * images) for m in range(micro)], axis=1
    )
    sub = iota((tokens, tokens), 0)
    lane = iota((tokens, tokens), 1)
    seg_col = jnp.sum(jnp.where(sub == lane, seg_row, 0.0), axis=1, keepdims=True)
    same[...] = (seg_col == seg_row).astype(F32)
    before_row = jnp.sum((seg_col < seg_row).astype(F32), axis=0, keepdims=True)
    before_col = jnp.sum((seg_row < seg_col).astype(F32), axis=1, keepdims=True)
    place_row = iota((1, tokens), 1).astype(F32) - before_row
    place_col = iota((tokens, 1), 0).astype(F32) - before_col
    width_row = jnp.zeros((1, tokens), F32)
    width_col = jnp.zeros((tokens, 1), F32)
    for m in range(micro):
        for image in range(images):
            width = wid[m, image].astype(F32)
            number = float(m * images + image)
            width_row = width_row + jnp.where(seg_row == number, width, 0.0)
            width_col = width_col + jnp.where(seg_col == number, width, 0.0)

    def grid(place, width):
        row = jnp.zeros_like(place)
        for k in range(1, GRID_ROWS):
            row = row + (place >= float(k) * width).astype(F32)
        return row, place - row * width

    row_r, col_r = grid(place_row, width_row)
    row_c, col_c = grid(place_col, width_col)
    cells = GRID_ROWS * GRID_COLS
    pick_q[...] = (iota((tokens, cells), 1).astype(F32) == row_c * GRID_COLS + col_c).astype(
        F32
    ).astype(BF16)
    pick_qt[...] = (
        iota((cells, tokens), 0).astype(F32) == row_r * GRID_COLS + (GRID_COLS - 1.0) - col_r
    ).astype(F32).astype(BF16)
    pick_k[...] = (iota((tokens, HALF), 1).astype(F32) == row_c * PITCH + col_c).astype(
        F32
    ).astype(BF16)
    pick_kt[...] = (iota((HALF, tokens), 0).astype(F32) == row_r * PITCH + col_r).astype(
        F32
    ).astype(BF16)


def spread_table(table, padded, spread, wide_table):
    heads, _, rels = table.shape
    padded[...] = jnp.zeros_like(padded)
    for head in range(heads):
        padded[head : head + 1, 0:rels] = table[head]
    shape = spread.shape
    where = iota((1, WIDE), 1)
    signed = jnp.where(where < HALF, where, where - WIDE)
    row_step = (signed + GRID_COLS + WIDE) // PITCH - WIDE // PITCH
    col_step = signed - row_step * PITCH
    entry = (REACH - row_step) * SPAN + jnp.clip(-col_step, -REACH, REACH) + REACH
    spread[...] = (iota(shape, 0) == entry).astype(F32).astype(BF16)
    high, low = two_parts(padded[...])
    vector = nn(high, spread[...]) + nn(low, spread[...])
    cells = GRID_ROWS * GRID_COLS
    for head in range(heads):
        line = jnp.broadcast_to(vector[head : head + 1, :], (GRID_COLS, WIDE))
        line = pltpu.roll(line, 0, 1, stride=1, stride_axis=0)
        for low_row in range(4):
            turned = line if low_row == 0 else pltpu.roll(line, low_row * PITCH, 1)
            for high_row in range(GRID_ROWS // 4):
                if high_row == 0:
                    part = turned[:, 0:HALF]
                else:
                    part = jnp.concatenate(
                        [turned[:, WIDE - 4 * PITCH : WIDE], turned[:, 0 : HALF - 4 * PITCH]], axis=1
                    )
                top = (high_row * 4 + low_row) * GRID_COLS
                part_high, part_low = two_parts(part)
                wide_table[top : top + GRID_COLS, head * HALF : (head + 1) * HALF] = part_high
                wide_table[
                    cells + top : cells + top + GRID_COLS, head * HALF : (head + 1) * HALF
                ] = part_low


def fold_table(head_grad):
    total = None
    for low_row in range(4):
        near = head_grad[low_row * GRID_COLS : (low_row + 1) * GRID_COLS, :]
        far = head_grad[(low_row + 4) * GRID_COLS : (low_row + 5) * GRID_COLS, :]
        step = 4 * PITCH
        laid = jnp.concatenate(
            [
                near[:, 0:step] + far[:, step : 2 * step],
                near[:, step : 2 * step],
                jnp.zeros((GRID_COLS, step), F32),
                far[:, 0:step],
            ],
            axis=1,
        )
        if low_row > 0:
            laid = pltpu.roll(laid, WIDE - low_row * PITCH, 1)
        total = laid if total is None else total + laid
    total = pltpu.roll(total, WIDE - (GRID_COLS - 1), 1, stride=1, stride_axis=0)
    return col_sum(total)


def block_body(
    hooks,
    b_at,
    inputs,
    cotangent,
    seg,
    wid,
    wqkv_in,
    wout_in,
    wfc1_in,
    wfc2_in,
    gains,
    biases,
    fc1_bias,
    table,
    activation,
    grad_in,
    small,
    wqkv,
    wout,
    wfc1,
    wfc2,
    arrived,
    leaving,
    stream,
    hat_one,
    hat_two,
    att_out,
    branch,
    d_middle,
    d_wide,
    normed,
    qkv,
    probs,
    bias,
    mixed,
    d_mixed,
    second,
    active,
    slope,
    same,
    pick_q,
    pick_k,
    pick_kt,
    pick_qt,
    padded,
    spread,
    wide_table,
    folded,
    scale_one,
    scale_two,
    weight_sem,
    send_sem,
    recv_sem,
):
    section = lax.axis_index("section")
    place = lax.axis_index("batch")
    other = (1 - section, place)
    width = inputs.shape[1]
    tokens = inputs.shape[0]
    ff = active.shape[1]
    heads = table.shape[0]
    pair = 2 * (width // heads)
    pairs = heads // 2
    parts = ff // width
    per_part = width // COLS

    loads = [
        pltpu.make_async_copy(source.at[0], target, weight_sem.at[index])
        for index, (source, target) in enumerate(
            [(wqkv_in, wqkv), (wout_in, wout), (wfc1_in, wfc1), (wfc2_in, wfc2)]
        )
    ]
    for load in loads:
        load.start()

    hooks.greet(other)

    geometry(seg, wid, same, pick_q, pick_k, pick_kt, pick_qt)
    spread_table(table, padded, spread, wide_table)
    cells = GRID_ROWS * GRID_COLS

    def bias_of(head):
        where = cols_of(head, HALF)
        high = nn(pick_q[...], wide_table[0:cells, where]).astype(BF16)
        low = nn(pick_q[...], wide_table[cells : 2 * cells, where]).astype(BF16)
        bias[cols_of(head, tokens), :] = nn(high, pick_kt[...]) + nn(low, pick_kt[...])

    for index in range(heads):
        bias_of(index)

    hooks.met()

    def relay(source):
        return pltpu.make_async_remote_copy(
            src_ref=source,
            dst_ref=arrived,
            send_sem=send_sem,
            recv_sem=recv_sem,
            device_id=other,
            device_id_type=MESH,
        )

    @pl.when(section == 0)
    def _():
        stream[...] = inputs[...].astype(F32)

    @pl.when(section == 1)
    def _():
        relay(activation).wait_recv()
        stream[...] = arrived[...].astype(F32)

    def turn_small(number, source):
        hooks.turned(number, source[...].T)

    hat, inv_scale = norm_parts(stream[...])
    hat_one[...] = hat
    scale_one[...] = inv_scale
    normed[...] = (hat * gains[0, 0:1, :] + biases[0, 0:1, :]).astype(BF16)
    turn_small(1, normed)
    loads[0].wait()
    for third in range(3):

        def project(index):
            out = nn(normed[...], wqkv[:, cols_of(third * per_part + index)])
            if third != 1:
                row = 1 if third == 0 else 2
                out = out + biases[row, 0:1, cols_of(index)]
            qkv[third, :, cols_of(index)] = out.astype(BF16)

        for index in range(per_part):
            project(index)

    lane = iota((1, pair), 1)
    low_lanes = (lane < pair // 2).astype(F32).astype(BF16)
    high_lanes = (lane >= pair // 2).astype(F32).astype(BF16)

    def stacked(value):
        return jnp.concatenate([value * low_lanes, value * high_lanes], axis=0)

    def side_by_side(value):
        return jnp.concatenate([value[0:tokens, :], value[tokens : 2 * tokens, :]], axis=1)

    for index in range(pairs):
        at = slice(index * pair, (index + 1) * pair)
        rows = slice(index * 2 * tokens, (index + 1) * 2 * tokens)
        raw = nt(stacked(qkv[0, :, at]), qkv[1, :, at])
        mask = jnp.concatenate([same[...], same[...]], axis=0) > 0.5
        scores = jnp.where(mask, raw * 0.125 + bias[rows, :], -1e30)
        exped = jnp.exp(scores - jnp.max(scores, axis=-1, keepdims=True))
        prob = exped / jnp.sum(exped, axis=-1, keepdims=True)
        probs[rows, :] = prob
        mixed[:, at] = nn(side_by_side(prob.astype(BF16)), stacked(qkv[2, :, at])).astype(BF16)

    turn_small(2, mixed)
    loads[1].wait()

    def attend_out(index):
        at = cols_of(index)
        out = nn(mixed[...], wout[:, at]) + biases[3, 0:1, at]
        att_out[:, at] = out
        stream[:, at] = stream[:, at] + gains[0, 1:2, at] * out

    for index in range(per_part):
        attend_out(index)
    hat, inv_scale = norm_parts(stream[...])
    hat_two[...] = hat
    scale_two[...] = inv_scale
    second[...] = (hat * gains[0, 2:3, :] + biases[4, 0:1, :]).astype(BF16)
    turn_small(0, second)
    loads[2].wait()

    def feed(index):
        at = cols_of(index)
        hidden = nn(second[...], wfc1[:, at]) + fc1_bias[0:1, at]
        cumul = 0.5 * (1.0 + lax.erf(hidden * ROOT_HALF))
        density = jnp.exp(-0.5 * hidden * hidden) * INV_ROOT_TWO_PI
        active[:, at] = (hidden * cumul).astype(BF16)
        slope[:, at] = cumul + hidden * density
        if (index + 1) % per_part == 0:
            part = index // per_part
            hooks.active_turned(part, active[:, cols_of(part, width)].T)

    for index in range(ff // COLS):
        feed(index)
    loads[3].wait()

    def feed_out(index):
        at = cols_of(index)
        out = nn(active[...], wfc2[:, at]) + biases[5, 0:1, at]
        branch[:, at] = out
        activation[:, at] = (stream[:, at] + gains[0, 3:4, at] * out).astype(BF16)

    for index in range(per_part):
        feed_out(index)

    @pl.when(section == 0)
    def _():
        relay(activation).start()

    hooks.forward_done()

    @pl.when(section == 0)
    def _():
        relay(activation).wait_send()
        relay(activation).wait_recv()
        stream[...] = arrived[...].astype(F32)

    @pl.when(section == 1)
    def _():
        stream[...] = cotangent[...].astype(F32)

    small[...] = jnp.zeros_like(small)
    upstream = stream[...]
    small[3:4, :] = col_sum(upstream * branch[...])
    d_branch = (gains[0, 3:4, :] * upstream).astype(BF16)
    b_at(parts + 4)[...] = d_branch
    small[9:10, :] = col_sum(d_branch.astype(F32))
    hooks.branch_done()

    def feed_back(index):
        at = cols_of(index)
        out = nt(b_at(parts + 4)[...], wfc2[at, :])
        d_hidden = (out * slope[:, at]).astype(BF16)
        part = index // per_part
        inner = cols_of(index % per_part)
        b_at(part)[:, inner] = d_hidden
        small[10 + part : 11 + part, inner] = col_sum(d_hidden.astype(F32))
        if (index + 1) % per_part == 0:
            hooks.hidden_done(part)

    for index in range(ff // COLS):
        feed_back(index)

    def second_back(index):
        at = cols_of(index)
        out = nt(b_at(0)[...], wfc1[at, 0:width])
        for part in range(1, parts):
            out = out + nt(b_at(part)[...], wfc1[at, part * width : (part + 1) * width])
        d_wide[:, at] = out

    for index in range(per_part):
        second_back(index)
    d_second = d_wide[...]
    small[2:3, :] = col_sum(d_second * hat_two[...])
    small[8:9, :] = col_sum(d_second)
    d_mid = stream[...] + norm_back(d_second * gains[0, 2:3, :], hat_two[...], scale_two[...])
    d_middle[...] = d_mid
    small[1:2, :] = col_sum(d_mid * att_out[...])
    d_att = (gains[0, 1:2, :] * d_mid).astype(BF16)
    b_at(parts + 3)[...] = d_att
    small[7:8, :] = col_sum(d_att.astype(F32))
    hooks.attention_out_done()

    def out_back(index):
        at = cols_of(index)
        d_mixed[:, at] = nt(b_at(parts + 3)[...], wout[at, :]).astype(BF16)

    for index in range(per_part):
        out_back(index)

    hooks.attention_next()
    folded[...] = jnp.zeros_like(folded)
    for index in range(pairs):
        at = slice(index * pair, (index + 1) * pair)
        rows = slice(index * 2 * tokens, (index + 1) * 2 * tokens)
        prob = probs[rows, :]
        d_mix = stacked(d_mixed[:, at])
        d_prob = nt(d_mix, qkv[2, :, at])
        b_at(parts + 2)[:, at] = tn(prob.astype(BF16), d_mix).astype(BF16)
        d_scores = prob * (d_prob - jnp.sum(prob * d_prob, axis=-1, keepdims=True))
        d_raw = (0.125 * d_scores).astype(BF16)
        b_at(parts)[:, at] = nn(side_by_side(d_raw), stacked(qkv[1, :, at])).astype(BF16)
        b_at(parts + 1)[:, at] = tn(d_raw, stacked(qkv[0, :, at])).astype(BF16)
        high, low = two_parts(d_scores)
        high = nn(high, pick_k[...]).astype(BF16)
        low = nn(low, pick_k[...]).astype(BF16)
        for side in range(2):
            own = slice(side * tokens, (side + 1) * tokens)
            head_grad = nn(pick_qt[...], high[own, :]) + nn(pick_qt[...], low[own, :])
            folded[2 * index + side : 2 * index + side + 1, :] = fold_table(head_grad)

    hooks.qkv_done()
    small[5:6, :] = col_sum(b_at(parts)[...].astype(F32))
    small[6:7, :] = col_sum(b_at(parts + 2)[...].astype(F32))

    def normed_back(index):
        at = cols_of(index)
        out = nt(b_at(parts)[...], wqkv[at, 0:width])
        for third in range(1, 3):
            out = out + nt(b_at(parts + third)[...], wqkv[at, third * width : (third + 1) * width])
        d_wide[:, at] = out

    for index in range(per_part):
        normed_back(index)
    d_normed = d_wide[...]
    small[0:1, :] = col_sum(d_normed * hat_one[...])
    small[4:5, :] = col_sum(d_normed)
    d_in = d_middle[...] + norm_back(d_normed * gains[0, 0:1, :], hat_one[...], scale_one[...])
    grad_in[...] = d_in
    leaving[...] = d_in.astype(BF16)

    @pl.when(section == 1)
    def _():
        relay(leaving).start()

    high, low = two_parts(folded[...])
    small[16:32, :] = nt(high, spread[...]) + nt(low, spread[...])
    hooks.small_done()

    @pl.when(section == 1)
    def _():
        relay(leaving).wait_send()


class Alone:
    def __init__(self, at_small, at_active):
        self.at_small, self.at_active = at_small, at_active

    def turned(self, number, value):
        self.at_small[number] = value

    def active_turned(self, part, value):
        self.at_active[part] = value

    def greet(self, other):
        pl.semaphore_signal(
            pltpu.get_barrier_semaphore(), inc=1, device_id=other, device_id_type=MESH
        )

    def met(self):
        pl.semaphore_wait(pltpu.get_barrier_semaphore(), 1)

    def nothing(self, *_):
        pass

    forward_done = branch_done = hidden_done = attention_out_done = nothing
    attention_next = qkv_done = small_done = nothing


def block_kernel(*refs):
    given, (activation, grad_in, at_small, at_active, b_all, small), rest = (
        refs[:12],
        refs[12:18],
        refs[18:],
    )
    block_body(
        Alone(at_small, at_active),
        lambda k: b_all.at[k],
        *given,
        activation,
        grad_in,
        small,
        *rest,
    )


def block_specs():
    whole = pl.BlockSpec(memory_space=pltpu.VMEM)
    return (
        [whole, whole, whole, pl.BlockSpec(memory_space=pltpu.SMEM)]
        + [pl.BlockSpec(memory_space=pl.ANY)] * 4
        + [whole] * 4
    )


def block_scratch(tokens, width, ff, heads, rels):
    cells = GRID_ROWS * GRID_COLS
    padded_rels = -(-rels // 256) * 256
    vm = pltpu.VMEM
    return (
        [
            vm((width, 3 * width), BF16),
            vm((width, width), BF16),
            vm((width, ff), BF16),
            vm((ff, width), BF16),
            vm((tokens, width), BF16),
            vm((tokens, width), BF16),
        ]
        + [vm((tokens, width), F32)] * 7
        + [
            vm((tokens, width), BF16),
            vm((3, tokens, width), BF16),
            vm((heads * tokens, tokens), F32),
            vm((heads * tokens, tokens), F32),
            vm((tokens, width), BF16),
            vm((tokens, width), BF16),
            vm((tokens, width), BF16),
            vm((tokens, ff), BF16),
            vm((tokens, ff), F32),
            vm((tokens, tokens), F32),
            vm((tokens, cells), BF16),
            vm((tokens, HALF), BF16),
            vm((HALF, tokens), BF16),
            vm((cells, tokens), BF16),
            vm((16, padded_rels), F32),
            vm((padded_rels, WIDE), BF16),
            vm((2 * cells, heads * HALF), BF16),
            vm((16, WIDE), F32),
            vm((tokens, 1), F32),
            vm((tokens, 1), F32),
            pltpu.SemaphoreType.DMA((4,)),
            pltpu.SemaphoreType.DMA,
            pltpu.SemaphoreType.DMA,
        ]
    )


N_BLOCK_SCRATCH = 36
UNIT_LEFT = (0, 0, 0, 0, 1, 1, 1, 2)
UNITS = len(UNIT_LEFT)
FOUR_UNITS = 4
SWAPPED = (1,)
AHEAD = 8
FOUR_AT = 0


def schedule(firsts, seconds, depths, small_at, started=0):
    ops = []
    for turn in range(started, len(seconds) + depths[2]):
        if turn - started < len(firsts):
            ops.append(f"x{firsts[turn - started]}")
        for name, depth in zip("yzwe", (0,) + depths):
            if max(0, started if depth == 0 else 0) <= turn - depth < len(seconds):
                ops.append(f"{name}{seconds[turn - depth]}")
        if turn == small_at:
            ops.append("s")
    for unit in seconds[: max(0, started - depths[0])]:
        ops.insert(0, f"z{unit}")
    return " ".join(ops + ["t"])


OPS = (
    "",
    "y8 y9",
    schedule((0, 1, 2, 4, 3, 5, 7, 6), (8, 9, 10, 11, 0, 1, 2, 4, 3, 5, 7, 6), (2, 3, 5), 12, 2),
)


def whole_kernel(*refs):
    given, (activation, grad_in, g_all, small_sum), rest = refs[:12], refs[12:16], refs[16:]
    block_scratches = rest[:N_BLOCK_SCRATCH]
    (
        at_small,
        at_active,
        left,
        right,
        left_four,
        right_four,
        y_send,
        y_recv,
        totals,
        passing,
        inward,
        small,
        small_parts,
        small_in,
        small_all,
        x_send_sem,
        x_recv_sem,
        y_send_sem,
        y_recv_sem,
        four_send_sem,
        four_recv_sem,
        z_send_sem,
        z_recv_sem,
        small_sem,
    ) = rest[N_BLOCK_SCRATCH:]
    section = lax.axis_index("section")
    place = lax.axis_index("batch")
    z = place // 4
    y = (place // 2) % 2
    x = place % 2
    x_peer = z * 4 + y * 2 + (1 - x)
    y_peer = z * 4 + (1 - y) * 2 + x
    xy_peer = z * 4 + (1 - y) * 2 + (1 - x)
    at_end = (z == 0) | (z == 3)
    between = jnp.logical_not(at_end)
    lower = z < 2
    in_peer = jnp.where(lower, place + 4, place - 4)
    out_peer = jnp.where(at_end, place, jnp.where(z == 1, place - 4, place + 4))
    tokens = given[0].shape[0]
    rows = left.shape[3]
    width = right.shape[2]
    barrier = pltpu.get_barrier_semaphore()

    def remote(source, target, send, recv, peer):
        return pltpu.make_async_remote_copy(
            src_ref=source,
            dst_ref=target,
            send_sem=send,
            recv_sem=recv,
            device_id=(section, peer),
            device_id_type=MESH,
        )

    others = ((1, y, 1 - x, x_peer), (2, 1 - y, x, y_peer), (3, 1 - y, 1 - x, xy_peer))
    four_left = [
        remote(
            at_active.at[peer_y, peer_x],
            left_four.at[slot - 1],
            four_send_sem.at[0, slot],
            four_recv_sem.at[0, slot],
            peer,
        )
        for slot, peer_y, peer_x, peer in others
    ]
    four_right = [
        remote(
            right_four.at[0:tokens, :],
            right_four.at[slot * tokens : (slot + 1) * tokens, :],
            four_send_sem.at[1, slot],
            four_recv_sem.at[1, slot],
            peer,
        )
        for slot, _, _, peer in others
    ]
    x_left = [
        remote(
            at_small.at[number, 1 - (y if number in SWAPPED else x)],
            left.at[number],
            x_send_sem.at[UNITS + number],
            x_recv_sem.at[UNITS + number],
            y_peer if number in SWAPPED else x_peer,
        )
        for number in range(3)
    ]
    x_right = [
        remote(
            right.at[unit, 0:tokens, :],
            right.at[unit, tokens : 2 * tokens, :],
            x_send_sem.at[unit],
            x_recv_sem.at[unit],
            y_peer if UNIT_LEFT[unit] in SWAPPED else x_peer,
        )
        for unit in range(UNITS)
    ]
    y_copy = [
        remote(
            y_send.at[unit],
            y_recv.at[unit],
            y_send_sem.at[unit],
            y_recv_sem.at[unit],
            x_peer if UNIT_LEFT[unit] in SWAPPED else y_peer,
        )
        for unit in range(UNITS)
    ]
    small_out = [
        remote(
            small_parts.at[place ^ step],
            small_in.at[place],
            small_sem.at[0, step],
            small_sem.at[1, step],
            place ^ step,
        )
        for step in range(1, 16)
    ]
    small_back = [
        remote(
            small_all.at[place],
            small_all.at[place],
            small_sem.at[2, step],
            small_sem.at[3, step],
            place ^ step,
        )
        for step in range(1, 16)
    ]

    def start(copies):
        for copy in copies:
            copy.start()

    waited = set()

    def once(name, copies):
        if name not in waited:
            waited.add(name)
            for copy in copies:
                copy.wait_recv()

    def product(unit, own):
        number = UNIT_LEFT[unit]
        held, side = (y, x) if number in SWAPPED else (x, y)
        if not own:
            side = 1 - side
        lhs = jnp.concatenate([at_small[number, held, :, side], left[number, :, side]], axis=2)
        return nn(lhs.reshape(4 * rows, 2 * tokens), right[unit])

    ready, sent, used = [], [], []

    def issue(units):
        ready.extend(units)
        while len(sent) < len(ready) and len(sent) - len(used) < AHEAD:
            x_right[ready[len(sent)]].start()
            sent.append(ready[len(sent)])

    def first(unit):
        number = UNIT_LEFT[unit]
        once(("left", number), [x_left[number]])
        once(("right", unit), [x_right[unit]])
        used.append(unit)
        issue([])
        y_send[unit] = product(unit, False).astype(BF16).reshape(4, rows, width)
        y_copy[unit].start()

    far_end = jnp.where(lower, 3, 0)
    far_mid = jnp.where(lower, 2, 1)
    near_mid = jnp.where(lower, 1, 2)
    near_end = jnp.where(lower, 0, 3)

    def z_copy(unit, dest, peer, final_inside):
        target = inward.at[unit] if final_inside else passing.at[unit, dest]
        slot = 4 if final_inside else dest
        return remote(
            totals.at[unit, dest],
            target,
            z_send_sem.at[unit, dest],
            z_recv_sem.at[unit, slot],
            peer,
        )

    def add_passing(unit, dest):
        totals[unit, dest] = (
            totals[unit, dest].astype(F32) + passing[unit, dest].astype(F32)
        ).astype(BF16)

    def second(unit):
        if unit >= UNITS:
            once("four", four_left + four_right)
            piece = slice((unit - UNITS) * rows, (unit - UNITS + 1) * rows)
            lhs = jnp.concatenate(
                [at_active[y, x, :, piece, :]] + [left_four[slot, :, piece, :] for slot in range(3)],
                axis=2,
            )
            out = nn(lhs.reshape(4 * rows, 4 * tokens), right_four[...])
        else:
            out = product(unit, True)
            y_copy[unit].wait_recv()
            out = out + y_recv[unit].reshape(4 * rows, width).astype(F32)
        totals[unit] = out.astype(BF16).reshape(4, rows, width)

        @pl.when(at_end)
        def _():
            z_copy(unit, far_end, in_peer, False).start()
            z_copy(unit, far_mid, in_peer, False).start()
            z_copy(unit, near_mid, in_peer, False).start()

    def third(unit):
        @pl.when(between)
        def _():
            z_copy(unit, far_end, in_peer, False).wait_recv()
            add_passing(unit, far_end)
            z_copy(unit, far_end, in_peer, False).start()
            z_copy(unit, far_mid, in_peer, False).wait_recv()
            add_passing(unit, far_mid)
            z_copy(unit, far_mid, in_peer, True).start()

    def fourth(unit):
        @pl.when(between)
        def _():
            z_copy(unit, near_end, out_peer, False).wait_recv()
            add_passing(unit, near_end)
            z_copy(unit, near_end, out_peer, True).start()

    def fifth(unit):
        z_copy(unit, z, in_peer, True).wait_recv()
        value = totals[unit, z].astype(F32) + inward[unit].astype(F32)

        @pl.when(at_end)
        def _():
            g_all[unit] = value

        @pl.when(between)
        def _():
            z_copy(unit, z, in_peer, False).wait_recv()
            g_all[unit] = value + passing[unit, z].astype(F32)

    def small_first():
        for index in range(16):
            small_parts[index] = small[2 * index : 2 * index + 2, :]
        start(small_out)

    def small_second():
        total = small_parts[place]
        for step, copy in enumerate(small_out, 1):
            copy.wait_recv()
            total = total + small_in[place ^ step]
        small_all[place] = total
        start(small_back)

    def small_third():
        for copy in small_back:
            copy.wait_recv()
        for index in range(16):
            small_sum[2 * index : 2 * index + 2, :] = small_all[index]

    stages = {"x": first, "y": second, "z": third, "w": fourth, "e": fifth}

    def run_ops(ops):
        for op in ops.split():
            if op == "s":
                small_second()
            elif op == "t":
                small_third()
            else:
                stages[op[0]](int(op[1:]))

    class Sending:
        def greet(self, other):
            pl.semaphore_signal(barrier, inc=1, device_id=other, device_id_type=MESH)
            for step in range(1, 16):
                pl.semaphore_signal(
                    barrier, inc=1, device_id=(section, place ^ step), device_id_type=MESH
                )

        def met(self):
            pl.semaphore_wait(barrier, 16)

        def turned(self, number, value):
            shares = value.reshape(4, 2, 2, rows, tokens)
            for side in range(2):
                at_small[number, side] = (
                    shares[:, side] if number in SWAPPED else shares[:, :, side]
                )
            x_left[number].start()

        def active_turned(self, part, value):
            shares = value.reshape(2, 2, left_four.shape[2], tokens)
            for high in range(2):
                for side in range(2):
                    at_active[high, side, part] = shares[high, side]

        def forward_done(self):
            start(four_left)

        def branch_done(self):
            start([four_right[1]])
            if FOUR_AT == 0:
                start([four_right[0], four_right[2]])

        def hidden_done(self, part):
            issue([part])
            if part == 1 and FOUR_AT == 1:
                start([four_right[0], four_right[2]])

        def attention_out_done(self):
            issue([7])

        def attention_next(self):
            run_ops(OPS[0])

        def qkv_done(self):
            issue([4, 5, 6])
            run_ops(OPS[1])

        def small_done(self):
            small_first()

    block_body(
        Sending(),
        lambda k: right.at[k, 0:tokens] if k < UNITS else right_four.at[0:tokens],
        *given,
        activation,
        grad_in,
        small,
        *block_scratches,
    )

    run_ops(OPS[2])

    for copy in four_left + four_right + x_left + x_right + y_copy + small_out + small_back:
        copy.wait_send()

    @pl.when(at_end)
    def _():
        for unit in range(UNITS + FOUR_UNITS):
            z_copy(unit, far_end, in_peer, False).wait_send()
            z_copy(unit, far_mid, in_peer, False).wait_send()
            z_copy(unit, near_mid, in_peer, False).wait_send()

    @pl.when(between)
    def _():
        for unit in range(UNITS + FOUR_UNITS):
            z_copy(unit, far_end, in_peer, False).wait_send()
            z_copy(unit, far_mid, in_peer, True).wait_send()
            z_copy(unit, near_end, out_peer, True).wait_send()


def finish_kernel(
    activation,
    grad_in,
    g_all,
    small,
    activation_out,
    grad_in_out,
    g_qkv,
    g_out,
    g_fc1,
    g_fc2,
    g_gains,
    g_biases,
    g_fc1_bias,
    g_table,
    small_here,
    sems,
):
    rows, width = g_all.shape[1:]
    pairs = [(small, small_here), (activation, activation_out), (grad_in, grad_in_out)]
    for unit in range(UNITS + FOUR_UNITS):
        if unit < 4:
            target = g_fc1.at[:, unit * width : (unit + 1) * width]
        elif unit < 7:
            target = g_qkv.at[:, (unit - 4) * width : (unit - 3) * width]
        elif unit == 7:
            target = g_out
        else:
            target = g_fc2.at[(unit - UNITS) * rows : (unit - UNITS + 1) * rows, :]
        pairs.append((g_all.at[unit], target))
    copies = [
        pltpu.make_async_copy(source, target, sems.at[index])
        for index, (source, target) in enumerate(pairs)
    ]
    for copy in copies:
        copy.start()
    copies[0].wait()
    g_gains[...] = small_here[0:4, :]
    for row in range(g_biases.shape[0]):
        g_biases[row] = small_here[4 + row : 5 + row, :]
    for part in range(4):
        g_fc1_bias[0:1, part * width : (part + 1) * width] = small_here[10 + part : 11 + part, :]
    for head in range(g_table.shape[0]):
        g_table[head] = small_here[16 + head : 17 + head, 0 : g_table.shape[2]]
    for copy in copies[1:]:
        copy.wait()


def run_whole(inputs, cotangent, seg, wid, weights):
    w_qkv, w_out, w_fc1, w_fc2, gains, biases, fc1_bias, table = weights
    tokens, width = inputs.shape
    ff = w_fc1.shape[2]
    heads, rels = table.shape[1:]
    rows = width // 16
    all_units = UNITS + FOUR_UNITS
    whole = pl.BlockSpec(memory_space=pltpu.VMEM)
    anywhere = pl.BlockSpec(memory_space=pl.ANY)
    vm = pltpu.VMEM
    dma = pltpu.SemaphoreType.DMA
    activation, grad_in, g_all, small = pl.pallas_call(
        whole_kernel,
        out_shape=(
            jax.ShapeDtypeStruct((tokens, width), BF16),
            jax.ShapeDtypeStruct((tokens, width), F32),
            jax.ShapeDtypeStruct((all_units, rows, width), F32),
            jax.ShapeDtypeStruct((32, width), F32),
        ),
        in_specs=block_specs(),
        out_specs=(whole,) * 4,
        scratch_shapes=block_scratch(tokens, width, ff, heads, rels)
        + [
            vm((3, 2, 4, 2, rows, tokens), BF16),
            vm((2, 2, 4, ff // 16, tokens), BF16),
            vm((3, 4, 2, rows, tokens), BF16),
            vm((UNITS, 2 * tokens, width), BF16),
            vm((3, 4, ff // 16, tokens), BF16),
            vm((4 * tokens, width), BF16),
            vm((UNITS, 4, rows, width), BF16),
            vm((UNITS, 4, rows, width), BF16),
            vm((all_units, 4, rows, width), BF16),
            vm((all_units, 4, rows, width), BF16),
            vm((all_units, rows, width), BF16),
            vm((32, width), F32),
            vm((16, 2, width), F32),
            vm((16, 2, width), F32),
            vm((16, 2, width), F32),
            dma((UNITS + 3,)),
            dma((UNITS + 3,)),
            dma((UNITS,)),
            dma((UNITS,)),
            dma((2, 4)),
            dma((2, 4)),
            dma((all_units, 4)),
            dma((all_units, 5)),
            dma((4, 16)),
        ],
        compiler_params=pltpu.CompilerParams(
            collective_id=0, has_side_effects=True, vmem_limit_bytes=60 * 2**20
        ),
        name="whole",
    )(
        inputs,
        cotangent,
        seg,
        wid,
        w_qkv,
        w_out,
        w_fc1,
        w_fc2,
        gains,
        jnp.swapaxes(biases, 0, 1),
        fc1_bias,
        jnp.swapaxes(table, 0, 1),
    )
    activation, grad_in, g_qkv, g_out, g_fc1, g_fc2, g_gains, g_biases, g_fc1_bias, g_table = (
        pl.pallas_call(
            finish_kernel,
            out_shape=(
                jax.ShapeDtypeStruct((tokens, width), BF16),
                jax.ShapeDtypeStruct((tokens, width), F32),
                jax.ShapeDtypeStruct((rows, 3 * width), F32),
                jax.ShapeDtypeStruct((rows, width), F32),
                jax.ShapeDtypeStruct((rows, ff), F32),
                jax.ShapeDtypeStruct((ff // 16, width), F32),
                jax.ShapeDtypeStruct((4, width), F32),
                jax.ShapeDtypeStruct((6, 1, width), F32),
                jax.ShapeDtypeStruct((1, ff), F32),
                jax.ShapeDtypeStruct((heads, 1, rels), F32),
            ),
            in_specs=[anywhere] * 4,
            out_specs=(whole,) * 10,
            scratch_shapes=[vm((32, width), F32), dma((all_units + 3,))],
            compiler_params=pltpu.CompilerParams(vmem_limit_bytes=60 * 2**20),
            name="finish",
        )(activation, grad_in, g_all, small)
    )
    return (
        activation,
        grad_in,
        g_qkv[None],
        g_out[None],
        g_fc1[None],
        g_fc2[None],
        g_gains[None],
        jnp.swapaxes(g_biases, 0, 1),
        g_fc1_bias,
        jnp.swapaxes(g_table, 0, 1),
    )


def run_plain(inputs, cotangent, seg, wid, weights):
    w_qkv, w_out, w_fc1, w_fc2, gains, biases, fc1_bias, table = weights
    tokens, width = inputs.shape
    ff = w_fc1.shape[2]
    heads, rels = table.shape[1:]
    parts = ff // width
    whole = pl.BlockSpec(memory_space=pltpu.VMEM)
    activation, grad_in, at_small, at_active, b_all, small = pl.pallas_call(
        block_kernel,
        out_shape=(
            jax.ShapeDtypeStruct((tokens, width), BF16),
            jax.ShapeDtypeStruct((tokens, width), F32),
            jax.ShapeDtypeStruct((3, width, tokens), BF16),
            jax.ShapeDtypeStruct((parts, width, tokens), BF16),
            jax.ShapeDtypeStruct((parts + 5, tokens, width), BF16),
            jax.ShapeDtypeStruct((32, width), F32),
        ),
        in_specs=block_specs(),
        out_specs=(whole,) * 6,
        scratch_shapes=block_scratch(tokens, width, ff, heads, rels),
        compiler_params=pltpu.CompilerParams(
            collective_id=1, has_side_effects=True, vmem_limit_bytes=56 * 2**20
        ),
        name="block",
    )(
        inputs,
        cotangent,
        seg,
        wid,
        w_qkv,
        w_out,
        w_fc1,
        w_fc2,
        gains,
        jnp.swapaxes(biases, 0, 1),
        fc1_bias,
        jnp.swapaxes(table, 0, 1),
    )

    def scattered(left, right):
        grad = jnp.dot(left, right, preferred_element_type=F32)
        return lax.psum_scatter(grad, "batch", scatter_dimension=0, tiled=True)[None]

    def joined(first, count):
        return jnp.concatenate([b_all[first + number] for number in range(count)], axis=1)

    g_fc1 = scattered(at_small[0], joined(0, parts))
    g_qkv = scattered(at_small[1], joined(parts, 3))
    g_out = scattered(at_small[2], b_all[parts + 3])
    g_fc2 = scattered(at_active.reshape(ff, tokens), b_all[parts + 4])
    small = lax.psum(small, "batch")
    return (
        activation,
        grad_in,
        g_qkv,
        g_out,
        g_fc1,
        g_fc2,
        small[None, 0:4],
        small[None, 4:10],
        small[10:14].reshape(1, ff),
        small[None, 16 : 16 + heads, :rels],
    )


def per_device(
    inputs,
    cotangent,
    segments,
    row_widths,
    w_qkv,
    w_out,
    w_fc1,
    w_fc2,
    norm_gains,
    bias_rows,
    fc1_bias,
    rel_table,
):
    micro, _, slots, width = inputs.shape
    weights = (w_qkv, w_out, w_fc1, w_fc2, norm_gains, bias_rows, fc1_bias, rel_table)
    run = run_whole if lax.axis_size("batch") == 16 else run_plain
    activation, grad_in, *grads = run(
        inputs.reshape(micro * slots, width),
        cotangent.reshape(micro * slots, width),
        segments.reshape(micro, slots),
        row_widths.reshape(micro, row_widths.shape[2]),
        weights,
    )
    shape = (1, micro, 1, slots, width)
    return (activation.reshape(shape), grad_in.reshape(shape), *grads)


def solution(mesh):
    return jax.shard_map(
        per_device,
        mesh=mesh,
        in_specs=(
            P(None, "batch", None, None),
            P(None, "batch", None, None),
            P(None, "batch", None),
            P(None, "batch", None),
            P("section", None, None),
            P("section", None, None),
            P("section", None, None),
            P("section", None, None),
            P("section", None, None),
            P("section", None, None),
            P("section", None),
            P("section", None, None),
        ),
        out_specs=(
            P("section", None, "batch", None, None),
            P("section", None, "batch", None, None),
            P("section", "batch", None),
            P("section", "batch", None),
            P("section", "batch", None),
            P("section", "batch", None),
            P("section", None, None),
            P("section", None, None),
            P("section", None),
            P("section", None, None),
        ),
        check_vma=False,
    )
```

```python
import functools

import jax
import jax.numpy as jnp
from jax import lax
from jax.experimental import pallas as pl
from jax.experimental.pallas import tpu as pltpu
from jax.sharding import PartitionSpec as P

MESH = pl.DeviceIdType.MESH
F32 = jnp.float32
BF16 = jnp.bfloat16
REACH = 13
SPAN = 2 * REACH + 1
NORM_EPS = 1e-06
ROOT_HALF = 0.7071067811865476
INV_ROOT_TWO_PI = 0.3989422804014327
COLS = 256
GRID_ROWS = 8
GRID_COLS = 16
PITCH = 2 * GRID_COLS
WIDE = 2 * GRID_ROWS * PITCH
HALF = WIDE // 2


def nn(left, right):
    return lax.dot_general(left, right, (((1,), (0,)), ((), ())), preferred_element_type=F32)


def nt(left, right):
    return lax.dot_general(left, right, (((1,), (1,)), ((), ())), preferred_element_type=F32)


def tn(left, right):
    return lax.dot_general(left, right, (((0,), (0,)), ((), ())), preferred_element_type=F32)


def iota(shape, dim):
    return lax.broadcasted_iota(jnp.int32, shape, dim)


def two_parts(value):
    high = value.astype(BF16)
    return high, (value - high.astype(F32)).astype(BF16)


def norm_parts(values_in):
    row_mean = jnp.mean(values_in, axis=-1, keepdims=True)
    centered = values_in - row_mean
    inv_scale = lax.rsqrt(jnp.mean(centered * centered, axis=-1, keepdims=True) + NORM_EPS)
    return centered * inv_scale, inv_scale


def norm_back(upstream, normal_in, inv_scale):
    return inv_scale * (
        upstream
        - jnp.mean(upstream, axis=-1, keepdims=True)
        - normal_in * jnp.mean(upstream * normal_in, axis=-1, keepdims=True)
    )


def col_sum(value):
    return jnp.sum(value, axis=0, keepdims=True)


def cols_of(index, size=COLS):
    return slice(index * size, (index + 1) * size)


def geometry(seg, wid, same, pick_q, pick_k, pick_kt, pick_qt):
    micro, slots = seg.shape
    tokens = micro * slots
    images = wid.shape[1]
    seg_f = seg[...].astype(F32)
    seg_row = jnp.concatenate(
        [seg_f[m : m + 1, :] + float(m * images) for m in range(micro)], axis=1
    )
    sub = iota((tokens, tokens), 0)
    lane = iota((tokens, tokens), 1)
    seg_col = jnp.sum(jnp.where(sub == lane, seg_row, 0.0), axis=1, keepdims=True)
    same[...] = (seg_col == seg_row).astype(F32)
    before_row = jnp.sum((seg_col < seg_row).astype(F32), axis=0, keepdims=True)
    before_col = jnp.sum((seg_row < seg_col).astype(F32), axis=1, keepdims=True)
    place_row = iota((1, tokens), 1).astype(F32) - before_row
    place_col = iota((tokens, 1), 0).astype(F32) - before_col
    width_row = jnp.zeros((1, tokens), F32)
    width_col = jnp.zeros((tokens, 1), F32)
    for m in range(micro):
        for image in range(images):
            width = wid[m, image].astype(F32)
            number = float(m * images + image)
            width_row = width_row + jnp.where(seg_row == number, width, 0.0)
            width_col = width_col + jnp.where(seg_col == number, width, 0.0)

    def grid(place, width):
        row = jnp.zeros_like(place)
        for k in range(1, GRID_ROWS):
            row = row + (place >= float(k) * width).astype(F32)
        return row, place - row * width

    row_r, col_r = grid(place_row, width_row)
    row_c, col_c = grid(place_col, width_col)
    cells = GRID_ROWS * GRID_COLS
    pick_q[...] = (iota((tokens, cells), 1).astype(F32) == row_c * GRID_COLS + col_c).astype(
        F32
    ).astype(BF16)
    pick_qt[...] = (
        iota((cells, tokens), 0).astype(F32) == row_r * GRID_COLS + (GRID_COLS - 1.0) - col_r
    ).astype(F32).astype(BF16)
    pick_k[...] = (iota((tokens, HALF), 1).astype(F32) == row_c * PITCH + col_c).astype(
        F32
    ).astype(BF16)
    pick_kt[...] = (iota((HALF, tokens), 0).astype(F32) == row_r * PITCH + col_r).astype(
        F32
    ).astype(BF16)


def spread_table(table, padded, spread, wide_table):
    heads, _, rels = table.shape
    padded[...] = jnp.zeros_like(padded)
    for head in range(heads):
        padded[head : head + 1, 0:rels] = table[head]
    shape = spread.shape
    where = iota((1, WIDE), 1)
    signed = jnp.where(where < HALF, where, where - WIDE)
    row_step = (signed + GRID_COLS + WIDE) // PITCH - WIDE // PITCH
    col_step = signed - row_step * PITCH
    entry = (REACH - row_step) * SPAN + jnp.clip(-col_step, -REACH, REACH) + REACH
    spread[...] = (iota(shape, 0) == entry).astype(F32).astype(BF16)
    high, low = two_parts(padded[...])
    vector = nn(high, spread[...]) + nn(low, spread[...])
    cells = GRID_ROWS * GRID_COLS
    for head in range(heads):
        line = jnp.broadcast_to(vector[head : head + 1, :], (GRID_COLS, WIDE))
        line = pltpu.roll(line, 0, 1, stride=1, stride_axis=0)
        for low_row in range(4):
            turned = line if low_row == 0 else pltpu.roll(line, low_row * PITCH, 1)
            for high_row in range(GRID_ROWS // 4):
                if high_row == 0:
                    part = turned[:, 0:HALF]
                else:
                    part = jnp.concatenate(
                        [turned[:, WIDE - 4 * PITCH : WIDE], turned[:, 0 : HALF - 4 * PITCH]], axis=1
                    )
                top = (high_row * 4 + low_row) * GRID_COLS
                part_high, part_low = two_parts(part)
                wide_table[top : top + GRID_COLS, head * HALF : (head + 1) * HALF] = part_high
                wide_table[
                    cells + top : cells + top + GRID_COLS, head * HALF : (head + 1) * HALF
                ] = part_low


def fold_table(head_grad):
    total = None
    for low_row in range(4):
        near = head_grad[low_row * GRID_COLS : (low_row + 1) * GRID_COLS, :]
        far = head_grad[(low_row + 4) * GRID_COLS : (low_row + 5) * GRID_COLS, :]
        step = 4 * PITCH
        laid = jnp.concatenate(
            [
                near[:, 0:step] + far[:, step : 2 * step],
                near[:, step : 2 * step],
                jnp.zeros((GRID_COLS, step), F32),
                far[:, 0:step],
            ],
            axis=1,
        )
        if low_row > 0:
            laid = pltpu.roll(laid, WIDE - low_row * PITCH, 1)
        total = laid if total is None else total + laid
    total = pltpu.roll(total, WIDE - (GRID_COLS - 1), 1, stride=1, stride_axis=0)
    return col_sum(total)


def block_body(
    hooks,
    b_at,
    inputs,
    cotangent,
    seg,
    wid,
    wqkv_in,
    wout_in,
    wfc1_in,
    wfc2_in,
    gains,
    biases,
    fc1_bias,
    table,
    activation,
    grad_in,
    small,
    wqkv,
    wout,
    wfc1,
    wfc2,
    arrived,
    leaving,
    stream,
    hat_one,
    hat_two,
    att_out,
    branch,
    d_middle,
    d_wide,
    normed,
    qkv,
    probs,
    bias,
    mixed,
    d_mixed,
    second,
    active,
    slope,
    same,
    pick_q,
    pick_k,
    pick_kt,
    pick_qt,
    padded,
    spread,
    wide_table,
    folded,
    scale_one,
    scale_two,
    weight_sem,
    send_sem,
    recv_sem,
):
    section = lax.axis_index("section")
    place = lax.axis_index("batch")
    other = (1 - section, place)
    width = inputs.shape[1]
    tokens = inputs.shape[0]
    ff = active.shape[1]
    heads = table.shape[0]
    pair = 2 * (width // heads)
    pairs = heads // 2
    parts = ff // width
    per_part = width // COLS

    loads = [
        pltpu.make_async_copy(source.at[0], target, weight_sem.at[index])
        for index, (source, target) in enumerate(
            [(wqkv_in, wqkv), (wout_in, wout), (wfc1_in, wfc1), (wfc2_in, wfc2)]
        )
    ]
    for load in loads:
        load.start()

    hooks.greet(other)

    geometry(seg, wid, same, pick_q, pick_k, pick_kt, pick_qt)
    spread_table(table, padded, spread, wide_table)
    cells = GRID_ROWS * GRID_COLS

    def bias_of(head):
        where = cols_of(head, HALF)
        high = nn(pick_q[...], wide_table[0:cells, where]).astype(BF16)
        low = nn(pick_q[...], wide_table[cells : 2 * cells, where]).astype(BF16)
        bias[cols_of(head, tokens), :] = nn(high, pick_kt[...]) + nn(low, pick_kt[...])

    for index in range(heads):
        bias_of(index)

    hooks.met()

    def relay(source):
        return pltpu.make_async_remote_copy(
            src_ref=source,
            dst_ref=arrived,
            send_sem=send_sem,
            recv_sem=recv_sem,
            device_id=other,
            device_id_type=MESH,
        )

    @pl.when(section == 0)
    def _():
        stream[...] = inputs[...].astype(F32)

    @pl.when(section == 1)
    def _():
        relay(activation).wait_recv()
        stream[...] = arrived[...].astype(F32)

    def turn_small(number, source):
        hooks.turned(number, source[...].T)

    hat, inv_scale = norm_parts(stream[...])
    hat_one[...] = hat
    scale_one[...] = inv_scale
    normed[...] = (hat * gains[0, 0:1, :] + biases[0, 0:1, :]).astype(BF16)
    turn_small(1, normed)
    loads[0].wait()
    for third in range(3):

        def project(index):
            out = nn(normed[...], wqkv[:, cols_of(third * per_part + index)])
            if third != 1:
                row = 1 if third == 0 else 2
                out = out + biases[row, 0:1, cols_of(index)]
            qkv[third, :, cols_of(index)] = out.astype(BF16)

        for index in range(per_part):
            project(index)

    lane = iota((1, pair), 1)
    low_lanes = (lane < pair // 2).astype(F32).astype(BF16)
    high_lanes = (lane >= pair // 2).astype(F32).astype(BF16)

    def stacked(value):
        return jnp.concatenate([value * low_lanes, value * high_lanes], axis=0)

    def side_by_side(value):
        return jnp.concatenate([value[0:tokens, :], value[tokens : 2 * tokens, :]], axis=1)

    for index in range(pairs):
        at = slice(index * pair, (index + 1) * pair)
        rows = slice(index * 2 * tokens, (index + 1) * 2 * tokens)
        raw = nt(stacked(qkv[0, :, at]), qkv[1, :, at])
        mask = jnp.concatenate([same[...], same[...]], axis=0) > 0.5
        scores = jnp.where(mask, raw * 0.125 + bias[rows, :], -1e30)
        exped = jnp.exp(scores - jnp.max(scores, axis=-1, keepdims=True))
        prob = exped / jnp.sum(exped, axis=-1, keepdims=True)
        probs[rows, :] = prob
        mixed[:, at] = nn(side_by_side(prob.astype(BF16)), stacked(qkv[2, :, at])).astype(BF16)

    turn_small(2, mixed)
    loads[1].wait()

    def attend_out(index):
        at = cols_of(index)
        out = nn(mixed[...], wout[:, at]) + biases[3, 0:1, at]
        att_out[:, at] = out
        stream[:, at] = stream[:, at] + gains[0, 1:2, at] * out

    for index in range(per_part):
        attend_out(index)
    hat, inv_scale = norm_parts(stream[...])
    hat_two[...] = hat
    scale_two[...] = inv_scale
    second[...] = (hat * gains[0, 2:3, :] + biases[4, 0:1, :]).astype(BF16)
    turn_small(0, second)
    loads[2].wait()

    def feed(index):
        at = cols_of(index)
        hidden = nn(second[...], wfc1[:, at]) + fc1_bias[0:1, at]
        cumul = 0.5 * (1.0 + lax.erf(hidden * ROOT_HALF))
        density = jnp.exp(-0.5 * hidden * hidden) * INV_ROOT_TWO_PI
        active[:, at] = (hidden * cumul).astype(BF16)
        slope[:, at] = cumul + hidden * density
        if (index + 1) % per_part == 0:
            part = index // per_part
            hooks.active_turned(part, active[:, cols_of(part, width)].T)

    for index in range(ff // COLS):
        feed(index)
    loads[3].wait()

    def feed_out(index):
        at = cols_of(index)
        out = nn(active[...], wfc2[:, at]) + biases[5, 0:1, at]
        branch[:, at] = out
        activation[:, at] = (stream[:, at] + gains[0, 3:4, at] * out).astype(BF16)

    for index in range(per_part):
        feed_out(index)

    @pl.when(section == 0)
    def _():
        relay(activation).start()

    hooks.forward_done()

    @pl.when(section == 0)
    def _():
        relay(activation).wait_send()
        relay(activation).wait_recv()
        stream[...] = arrived[...].astype(F32)

    @pl.when(section == 1)
    def _():
        stream[...] = cotangent[...].astype(F32)

    small[...] = jnp.zeros_like(small)
    upstream = stream[...]
    small[3:4, :] = col_sum(upstream * branch[...])
    d_branch = (gains[0, 3:4, :] * upstream).astype(BF16)
    b_at(parts + 4)[...] = d_branch
    small[9:10, :] = col_sum(d_branch.astype(F32))
    hooks.branch_done()

    def feed_back(index):
        at = cols_of(index)
        out = nt(b_at(parts + 4)[...], wfc2[at, :])
        d_hidden = (out * slope[:, at]).astype(BF16)
        part = index // per_part
        inner = cols_of(index % per_part)
        b_at(part)[:, inner] = d_hidden
        small[10 + part : 11 + part, inner] = col_sum(d_hidden.astype(F32))
        if (index + 1) % per_part == 0:
            hooks.hidden_done(part)

    for index in range(ff // COLS):
        feed_back(index)

    def second_back(index):
        at = cols_of(index)
        out = nt(b_at(0)[...], wfc1[at, 0:width])
        for part in range(1, parts):
            out = out + nt(b_at(part)[...], wfc1[at, part * width : (part + 1) * width])
        d_wide[:, at] = out

    for index in range(per_part):
        second_back(index)
    d_second = d_wide[...]
    small[2:3, :] = col_sum(d_second * hat_two[...])
    small[8:9, :] = col_sum(d_second)
    d_mid = stream[...] + norm_back(d_second * gains[0, 2:3, :], hat_two[...], scale_two[...])
    d_middle[...] = d_mid
    small[1:2, :] = col_sum(d_mid * att_out[...])
    d_att = (gains[0, 1:2, :] * d_mid).astype(BF16)
    b_at(parts + 3)[...] = d_att
    small[7:8, :] = col_sum(d_att.astype(F32))
    hooks.attention_out_done()

    def out_back(index):
        at = cols_of(index)
        d_mixed[:, at] = nt(b_at(parts + 3)[...], wout[at, :]).astype(BF16)

    for index in range(per_part):
        out_back(index)

    hooks.attention_next()
    folded[...] = jnp.zeros_like(folded)
    for index in range(pairs):
        at = slice(index * pair, (index + 1) * pair)
        rows = slice(index * 2 * tokens, (index + 1) * 2 * tokens)
        prob = probs[rows, :]
        d_mix = stacked(d_mixed[:, at])
        d_prob = nt(d_mix, qkv[2, :, at])
        b_at(parts + 2)[:, at] = tn(prob.astype(BF16), d_mix).astype(BF16)
        d_scores = prob * (d_prob - jnp.sum(prob * d_prob, axis=-1, keepdims=True))
        d_raw = (0.125 * d_scores).astype(BF16)
        b_at(parts)[:, at] = nn(side_by_side(d_raw), stacked(qkv[1, :, at])).astype(BF16)
        b_at(parts + 1)[:, at] = tn(d_raw, stacked(qkv[0, :, at])).astype(BF16)
        high, low = two_parts(d_scores)
        high = nn(high, pick_k[...]).astype(BF16)
        low = nn(low, pick_k[...]).astype(BF16)
        for side in range(2):
            own = slice(side * tokens, (side + 1) * tokens)
            head_grad = nn(pick_qt[...], high[own, :]) + nn(pick_qt[...], low[own, :])
            folded[2 * index + side : 2 * index + side + 1, :] = fold_table(head_grad)

    hooks.qkv_done()
    small[5:6, :] = col_sum(b_at(parts)[...].astype(F32))
    small[6:7, :] = col_sum(b_at(parts + 2)[...].astype(F32))

    def normed_back(index):
        at = cols_of(index)
        out = nt(b_at(parts)[...], wqkv[at, 0:width])
        for third in range(1, 3):
            out = out + nt(b_at(parts + third)[...], wqkv[at, third * width : (third + 1) * width])
        d_wide[:, at] = out

    for index in range(per_part):
        normed_back(index)
    d_normed = d_wide[...]
    small[0:1, :] = col_sum(d_normed * hat_one[...])
    small[4:5, :] = col_sum(d_normed)
    d_in = d_middle[...] + norm_back(d_normed * gains[0, 0:1, :], hat_one[...], scale_one[...])
    grad_in[...] = d_in
    leaving[...] = d_in.astype(BF16)

    @pl.when(section == 1)
    def _():
        relay(leaving).start()

    high, low = two_parts(folded[...])
    small[16:32, :] = nt(high, spread[...]) + nt(low, spread[...])
    hooks.small_done()

    @pl.when(section == 1)
    def _():
        relay(leaving).wait_send()


class Alone:
    def __init__(self, at_small, at_active):
        self.at_small, self.at_active = at_small, at_active

    def turned(self, number, value):
        self.at_small[number] = value

    def active_turned(self, part, value):
        self.at_active[part] = value

    def greet(self, other):
        pl.semaphore_signal(
            pltpu.get_barrier_semaphore(), inc=1, device_id=other, device_id_type=MESH
        )

    def met(self):
        pl.semaphore_wait(pltpu.get_barrier_semaphore(), 1)

    def nothing(self, *_):
        pass

    forward_done = branch_done = hidden_done = attention_out_done = nothing
    attention_next = qkv_done = small_done = nothing


def block_kernel(*refs):
    given, (activation, grad_in, at_small, at_active, b_all, small), rest = (
        refs[:12],
        refs[12:18],
        refs[18:],
    )
    block_body(
        Alone(at_small, at_active),
        lambda k: b_all.at[k],
        *given,
        activation,
        grad_in,
        small,
        *rest,
    )


def block_specs():
    whole = pl.BlockSpec(memory_space=pltpu.VMEM)
    return (
        [whole, whole, whole, pl.BlockSpec(memory_space=pltpu.SMEM)]
        + [pl.BlockSpec(memory_space=pl.ANY)] * 4
        + [whole] * 4
    )


def block_scratch(tokens, width, ff, heads, rels):
    cells = GRID_ROWS * GRID_COLS
    padded_rels = -(-rels // 256) * 256
    vm = pltpu.VMEM
    return (
        [
            vm((width, 3 * width), BF16),
            vm((width, width), BF16),
            vm((width, ff), BF16),
            vm((ff, width), BF16),
            vm((tokens, width), BF16),
            vm((tokens, width), BF16),
        ]
        + [vm((tokens, width), F32)] * 7
        + [
            vm((tokens, width), BF16),
            vm((3, tokens, width), BF16),
            vm((heads * tokens, tokens), F32),
            vm((heads * tokens, tokens), F32),
            vm((tokens, width), BF16),
            vm((tokens, width), BF16),
            vm((tokens, width), BF16),
            vm((tokens, ff), BF16),
            vm((tokens, ff), F32),
            vm((tokens, tokens), F32),
            vm((tokens, cells), BF16),
            vm((tokens, HALF), BF16),
            vm((HALF, tokens), BF16),
            vm((cells, tokens), BF16),
            vm((16, padded_rels), F32),
            vm((padded_rels, WIDE), BF16),
            vm((2 * cells, heads * HALF), BF16),
            vm((16, WIDE), F32),
            vm((tokens, 1), F32),
            vm((tokens, 1), F32),
            pltpu.SemaphoreType.DMA((4,)),
            pltpu.SemaphoreType.DMA,
            pltpu.SemaphoreType.DMA,
        ]
    )


N_BLOCK_SCRATCH = 36
UNIT_LEFT = (0, 0, 0, 0, 1, 1, 1, 2)
UNITS = len(UNIT_LEFT)
FOUR_UNITS = 4
SWAPPED = (1,)
AHEAD = 8
FOUR_AT = 0


def schedule(firsts, seconds, depths, small_at, started=0):
    ops = []
    for turn in range(started, len(seconds) + depths[2]):
        if turn - started < len(firsts):
            ops.append(f"x{firsts[turn - started]}")
        for name, depth in zip("yzwe", (0,) + depths):
            if max(0, started if depth == 0 else 0) <= turn - depth < len(seconds):
                ops.append(f"{name}{seconds[turn - depth]}")
        if turn == small_at:
            ops.append("s")
    for unit in seconds[: max(0, started - depths[0])]:
        ops.insert(0, f"z{unit}")
    return " ".join(ops + ["t"])


OPS = (
    "",
    "y8 y9",
    schedule((0, 1, 2, 4, 3, 5, 7, 6), (8, 9, 10, 11, 0, 1, 2, 4, 3, 5, 7, 6), (2, 3, 5), 12, 2),
)


def whole_kernel(*refs):
    given, (activation, grad_in, g_all, small_sum), rest = refs[:12], refs[12:16], refs[16:]
    block_scratches = rest[:N_BLOCK_SCRATCH]
    (
        at_small,
        at_active,
        left,
        right,
        left_four,
        right_four,
        y_send,
        y_recv,
        totals,
        passing,
        inward,
        small,
        small_parts,
        small_in,
        small_all,
        x_send_sem,
        x_recv_sem,
        y_send_sem,
        y_recv_sem,
        four_send_sem,
        four_recv_sem,
        z_send_sem,
        z_recv_sem,
        small_sem,
    ) = rest[N_BLOCK_SCRATCH:]
    section = lax.axis_index("section")
    place = lax.axis_index("batch")
    z = place // 4
    y = (place // 2) % 2
    x = place % 2
    x_peer = z * 4 + y * 2 + (1 - x)
    y_peer = z * 4 + (1 - y) * 2 + x
    xy_peer = z * 4 + (1 - y) * 2 + (1 - x)
    at_end = (z == 0) | (z == 3)
    between = jnp.logical_not(at_end)
    lower = z < 2
    in_peer = jnp.where(lower, place + 4, place - 4)
    out_peer = jnp.where(at_end, place, jnp.where(z == 1, place - 4, place + 4))
    tokens = given[0].shape[0]
    rows = left.shape[3]
    width = right.shape[2]
    barrier = pltpu.get_barrier_semaphore()

    def remote(source, target, send, recv, peer):
        return pltpu.make_async_remote_copy(
            src_ref=source,
            dst_ref=target,
            send_sem=send,
            recv_sem=recv,
            device_id=(section, peer),
            device_id_type=MESH,
        )

    others = ((1, y, 1 - x, x_peer), (2, 1 - y, x, y_peer), (3, 1 - y, 1 - x, xy_peer))
    four_left = [
        remote(
            at_active.at[peer_y, peer_x],
            left_four.at[slot - 1],
            four_send_sem.at[0, slot],
            four_recv_sem.at[0, slot],
            peer,
        )
        for slot, peer_y, peer_x, peer in others
    ]
    four_right = [
        remote(
            right_four.at[0:tokens, :],
            right_four.at[slot * tokens : (slot + 1) * tokens, :],
            four_send_sem.at[1, slot],
            four_recv_sem.at[1, slot],
            peer,
        )
        for slot, _, _, peer in others
    ]
    x_left = [
        remote(
            at_small.at[number, 1 - (y if number in SWAPPED else x)],
            left.at[number],
            x_send_sem.at[UNITS + number],
            x_recv_sem.at[UNITS + number],
            y_peer if number in SWAPPED else x_peer,
        )
        for number in range(3)
    ]
    x_right = [
        remote(
            right.at[unit, 0:tokens, :],
            right.at[unit, tokens : 2 * tokens, :],
            x_send_sem.at[unit],
            x_recv_sem.at[unit],
            y_peer if UNIT_LEFT[unit] in SWAPPED else x_peer,
        )
        for unit in range(UNITS)
    ]
    y_copy = [
        remote(
            y_send.at[unit],
            y_recv.at[unit],
            y_send_sem.at[unit],
            y_recv_sem.at[unit],
            x_peer if UNIT_LEFT[unit] in SWAPPED else y_peer,
        )
        for unit in range(UNITS)
    ]
    small_out = [
        remote(
            small_parts.at[place ^ step],
            small_in.at[place],
            small_sem.at[0, step],
            small_sem.at[1, step],
            place ^ step,
        )
        for step in range(1, 16)
    ]
    small_back = [
        remote(
            small_all.at[place],
            small_all.at[place],
            small_sem.at[2, step],
            small_sem.at[3, step],
            place ^ step,
        )
        for step in range(1, 16)
    ]

    def start(copies):
        for copy in copies:
            copy.start()

    waited = set()

    def once(name, copies):
        if name not in waited:
            waited.add(name)
            for copy in copies:
                copy.wait_recv()

    def product(unit, own):
        number = UNIT_LEFT[unit]
        held, side = (y, x) if number in SWAPPED else (x, y)
        if not own:
            side = 1 - side
        lhs = jnp.concatenate([at_small[number, held, :, side], left[number, :, side]], axis=2)
        return nn(lhs.reshape(4 * rows, 2 * tokens), right[unit])

    ready, sent, used = [], [], []

    def issue(units):
        ready.extend(units)
        while len(sent) < len(ready) and len(sent) - len(used) < AHEAD:
            x_right[ready[len(sent)]].start()
            sent.append(ready[len(sent)])

    def first(unit):
        number = UNIT_LEFT[unit]
        once(("left", number), [x_left[number]])
        once(("right", unit), [x_right[unit]])
        used.append(unit)
        issue([])
        y_send[unit] = product(unit, False).astype(BF16).reshape(4, rows, width)
        y_copy[unit].start()

    far_end = jnp.where(lower, 3, 0)
    far_mid = jnp.where(lower, 2, 1)
    near_mid = jnp.where(lower, 1, 2)
    near_end = jnp.where(lower, 0, 3)

    def z_copy(unit, dest, peer, final_inside):
        target = inward.at[unit] if final_inside else passing.at[unit, dest]
        slot = 4 if final_inside else dest
        return remote(
            totals.at[unit, dest],
            target,
            z_send_sem.at[unit, dest],
            z_recv_sem.at[unit, slot],
            peer,
        )

    def add_passing(unit, dest):
        totals[unit, dest] = (
            totals[unit, dest].astype(F32) + passing[unit, dest].astype(F32)
        ).astype(BF16)

    def second(unit):
        if unit >= UNITS:
            once("four", four_left + four_right)
            piece = slice((unit - UNITS) * rows, (unit - UNITS + 1) * rows)
            lhs = jnp.concatenate(
                [at_active[y, x, :, piece, :]] + [left_four[slot, :, piece, :] for slot in range(3)],
                axis=2,
            )
            out = nn(lhs.reshape(4 * rows, 4 * tokens), right_four[...])
        else:
            out = product(unit, True)
            y_copy[unit].wait_recv()
            out = out + y_recv[unit].reshape(4 * rows, width).astype(F32)
        totals[unit] = out.astype(BF16).reshape(4, rows, width)

        @pl.when(at_end)
        def _():
            z_copy(unit, far_end, in_peer, False).start()
            z_copy(unit, far_mid, in_peer, False).start()
            z_copy(unit, near_mid, in_peer, False).start()

    def third(unit):
        @pl.when(between)
        def _():
            z_copy(unit, far_end, in_peer, False).wait_recv()
            add_passing(unit, far_end)
            z_copy(unit, far_end, in_peer, False).start()
            z_copy(unit, far_mid, in_peer, False).wait_recv()
            add_passing(unit, far_mid)
            z_copy(unit, far_mid, in_peer, True).start()

    def fourth(unit):
        @pl.when(between)
        def _():
            z_copy(unit, near_end, out_peer, False).wait_recv()
            add_passing(unit, near_end)
            z_copy(unit, near_end, out_peer, True).start()

    def fifth(unit):
        z_copy(unit, z, in_peer, True).wait_recv()
        value = totals[unit, z].astype(F32) + inward[unit].astype(F32)

        @pl.when(at_end)
        def _():
            g_all[unit] = value

        @pl.when(between)
        def _():
            z_copy(unit, z, in_peer, False).wait_recv()
            g_all[unit] = value + passing[unit, z].astype(F32)

    def small_first():
        for index in range(16):
            small_parts[index] = small[2 * index : 2 * index + 2, :]
        start(small_out)

    def small_second():
        total = small_parts[place]
        for step, copy in enumerate(small_out, 1):
            copy.wait_recv()
            total = total + small_in[place ^ step]
        small_all[place] = total
        start(small_back)

    def small_third():
        for copy in small_back:
            copy.wait_recv()
        for index in range(16):
            small_sum[2 * index : 2 * index + 2, :] = small_all[index]

    stages = {"x": first, "y": second, "z": third, "w": fourth, "e": fifth}

    def run_ops(ops):
        for op in ops.split():
            if op == "s":
                small_second()
            elif op == "t":
                small_third()
            else:
                stages[op[0]](int(op[1:]))

    class Sending:
        def greet(self, other):
            pl.semaphore_signal(barrier, inc=1, device_id=other, device_id_type=MESH)
            for step in range(1, 16):
                pl.semaphore_signal(
                    barrier, inc=1, device_id=(section, place ^ step), device_id_type=MESH
                )

        def met(self):
            pl.semaphore_wait(barrier, 16)

        def turned(self, number, value):
            shares = value.reshape(4, 2, 2, rows, tokens)
            for side in range(2):
                at_small[number, side] = (
                    shares[:, side] if number in SWAPPED else shares[:, :, side]
                )
            x_left[number].start()

        def active_turned(self, part, value):
            shares = value.reshape(2, 2, left_four.shape[2], tokens)
            for high in range(2):
                for side in range(2):
                    at_active[high, side, part] = shares[high, side]

        def forward_done(self):
            start([four_left[1], four_left[0], four_left[2]])

        def branch_done(self):
            start([four_right[1]])
            if FOUR_AT == 0:
                start([four_right[0], four_right[2]])

        def hidden_done(self, part):
            issue([part])
            if part == 1 and FOUR_AT == 1:
                start([four_right[0], four_right[2]])

        def attention_out_done(self):
            issue([7])

        def attention_next(self):
            run_ops(OPS[0])

        def qkv_done(self):
            issue([4, 5, 6])
            run_ops(OPS[1])

        def small_done(self):
            small_first()

    block_body(
        Sending(),
        lambda k: right.at[k, 0:tokens] if k < UNITS else right_four.at[0:tokens],
        *given,
        activation,
        grad_in,
        small,
        *block_scratches,
    )

    run_ops(OPS[2])

    for copy in four_left + four_right + x_left + x_right + y_copy + small_out + small_back:
        copy.wait_send()

    @pl.when(at_end)
    def _():
        for unit in range(UNITS + FOUR_UNITS):
            z_copy(unit, far_end, in_peer, False).wait_send()
            z_copy(unit, far_mid, in_peer, False).wait_send()
            z_copy(unit, near_mid, in_peer, False).wait_send()

    @pl.when(between)
    def _():
        for unit in range(UNITS + FOUR_UNITS):
            z_copy(unit, far_end, in_peer, False).wait_send()
            z_copy(unit, far_mid, in_peer, True).wait_send()
            z_copy(unit, near_end, out_peer, True).wait_send()


def finish_kernel(
    activation,
    grad_in,
    g_all,
    small,
    activation_out,
    grad_in_out,
    g_qkv,
    g_out,
    g_fc1,
    g_fc2,
    g_gains,
    g_biases,
    g_fc1_bias,
    g_table,
    small_here,
    sems,
):
    rows, width = g_all.shape[1:]
    pairs = [(small, small_here), (activation, activation_out), (grad_in, grad_in_out)]
    for unit in range(UNITS + FOUR_UNITS):
        if unit < 4:
            target = g_fc1.at[:, unit * width : (unit + 1) * width]
        elif unit < 7:
            target = g_qkv.at[:, (unit - 4) * width : (unit - 3) * width]
        elif unit == 7:
            target = g_out
        else:
            target = g_fc2.at[(unit - UNITS) * rows : (unit - UNITS + 1) * rows, :]
        pairs.append((g_all.at[unit], target))
    copies = [
        pltpu.make_async_copy(source, target, sems.at[index])
        for index, (source, target) in enumerate(pairs)
    ]
    for copy in copies:
        copy.start()
    copies[0].wait()
    g_gains[...] = small_here[0:4, :]
    for row in range(g_biases.shape[0]):
        g_biases[row] = small_here[4 + row : 5 + row, :]
    for part in range(4):
        g_fc1_bias[0:1, part * width : (part + 1) * width] = small_here[10 + part : 11 + part, :]
    for head in range(g_table.shape[0]):
        g_table[head] = small_here[16 + head : 17 + head, 0 : g_table.shape[2]]
    for copy in copies[1:]:
        copy.wait()


def run_whole(inputs, cotangent, seg, wid, weights):
    w_qkv, w_out, w_fc1, w_fc2, gains, biases, fc1_bias, table = weights
    tokens, width = inputs.shape
    ff = w_fc1.shape[2]
    heads, rels = table.shape[1:]
    rows = width // 16
    all_units = UNITS + FOUR_UNITS
    whole = pl.BlockSpec(memory_space=pltpu.VMEM)
    anywhere = pl.BlockSpec(memory_space=pl.ANY)
    vm = pltpu.VMEM
    dma = pltpu.SemaphoreType.DMA
    activation, grad_in, g_all, small = pl.pallas_call(
        whole_kernel,
        out_shape=(
            jax.ShapeDtypeStruct((tokens, width), BF16),
            jax.ShapeDtypeStruct((tokens, width), F32),
            jax.ShapeDtypeStruct((all_units, rows, width), F32),
            jax.ShapeDtypeStruct((32, width), F32),
        ),
        in_specs=block_specs(),
        out_specs=(whole,) * 4,
        scratch_shapes=block_scratch(tokens, width, ff, heads, rels)
        + [
            vm((3, 2, 4, 2, rows, tokens), BF16),
            vm((2, 2, 4, ff // 16, tokens), BF16),
            vm((3, 4, 2, rows, tokens), BF16),
            vm((UNITS, 2 * tokens, width), BF16),
            vm((3, 4, ff // 16, tokens), BF16),
            vm((4 * tokens, width), BF16),
            vm((UNITS, 4, rows, width), BF16),
            vm((UNITS, 4, rows, width), BF16),
            vm((all_units, 4, rows, width), BF16),
            vm((all_units, 4, rows, width), BF16),
            vm((all_units, rows, width), BF16),
            vm((32, width), F32),
            vm((16, 2, width), F32),
            vm((16, 2, width), F32),
            vm((16, 2, width), F32),
            dma((UNITS + 3,)),
            dma((UNITS + 3,)),
            dma((UNITS,)),
            dma((UNITS,)),
            dma((2, 4)),
            dma((2, 4)),
            dma((all_units, 4)),
            dma((all_units, 5)),
            dma((4, 16)),
        ],
        compiler_params=pltpu.CompilerParams(
            collective_id=0, has_side_effects=True, vmem_limit_bytes=60 * 2**20
        ),
        name="whole",
    )(
        inputs,
        cotangent,
        seg,
        wid,
        w_qkv,
        w_out,
        w_fc1,
        w_fc2,
        gains,
        jnp.swapaxes(biases, 0, 1),
        fc1_bias,
        jnp.swapaxes(table, 0, 1),
    )
    activation, grad_in, g_qkv, g_out, g_fc1, g_fc2, g_gains, g_biases, g_fc1_bias, g_table = (
        pl.pallas_call(
            finish_kernel,
            out_shape=(
                jax.ShapeDtypeStruct((tokens, width), BF16),
                jax.ShapeDtypeStruct((tokens, width), F32),
                jax.ShapeDtypeStruct((rows, 3 * width), F32),
                jax.ShapeDtypeStruct((rows, width), F32),
                jax.ShapeDtypeStruct((rows, ff), F32),
                jax.ShapeDtypeStruct((ff // 16, width), F32),
                jax.ShapeDtypeStruct((4, width), F32),
                jax.ShapeDtypeStruct((6, 1, width), F32),
                jax.ShapeDtypeStruct((1, ff), F32),
                jax.ShapeDtypeStruct((heads, 1, rels), F32),
            ),
            in_specs=[anywhere] * 4,
            out_specs=(whole,) * 10,
            scratch_shapes=[vm((32, width), F32), dma((all_units + 3,))],
            compiler_params=pltpu.CompilerParams(vmem_limit_bytes=60 * 2**20),
            name="finish",
        )(activation, grad_in, g_all, small)
    )
    return (
        activation,
        grad_in,
        g_qkv[None],
        g_out[None],
        g_fc1[None],
        g_fc2[None],
        g_gains[None],
        jnp.swapaxes(g_biases, 0, 1),
        g_fc1_bias,
        jnp.swapaxes(g_table, 0, 1),
    )


def run_plain(inputs, cotangent, seg, wid, weights):
    w_qkv, w_out, w_fc1, w_fc2, gains, biases, fc1_bias, table = weights
    tokens, width = inputs.shape
    ff = w_fc1.shape[2]
    heads, rels = table.shape[1:]
    parts = ff // width
    whole = pl.BlockSpec(memory_space=pltpu.VMEM)
    activation, grad_in, at_small, at_active, b_all, small = pl.pallas_call(
        block_kernel,
        out_shape=(
            jax.ShapeDtypeStruct((tokens, width), BF16),
            jax.ShapeDtypeStruct((tokens, width), F32),
            jax.ShapeDtypeStruct((3, width, tokens), BF16),
            jax.ShapeDtypeStruct((parts, width, tokens), BF16),
            jax.ShapeDtypeStruct((parts + 5, tokens, width), BF16),
            jax.ShapeDtypeStruct((32, width), F32),
        ),
        in_specs=block_specs(),
        out_specs=(whole,) * 6,
        scratch_shapes=block_scratch(tokens, width, ff, heads, rels),
        compiler_params=pltpu.CompilerParams(
            collective_id=1, has_side_effects=True, vmem_limit_bytes=56 * 2**20
        ),
        name="block",
    )(
        inputs,
        cotangent,
        seg,
        wid,
        w_qkv,
        w_out,
        w_fc1,
        w_fc2,
        gains,
        jnp.swapaxes(biases, 0, 1),
        fc1_bias,
        jnp.swapaxes(table, 0, 1),
    )

    def scattered(left, right):
        grad = jnp.dot(left, right, preferred_element_type=F32)
        return lax.psum_scatter(grad, "batch", scatter_dimension=0, tiled=True)[None]

    def joined(first, count):
        return jnp.concatenate([b_all[first + number] for number in range(count)], axis=1)

    g_fc1 = scattered(at_small[0], joined(0, parts))
    g_qkv = scattered(at_small[1], joined(parts, 3))
    g_out = scattered(at_small[2], b_all[parts + 3])
    g_fc2 = scattered(at_active.reshape(ff, tokens), b_all[parts + 4])
    small = lax.psum(small, "batch")
    return (
        activation,
        grad_in,
        g_qkv,
        g_out,
        g_fc1,
        g_fc2,
        small[None, 0:4],
        small[None, 4:10],
        small[10:14].reshape(1, ff),
        small[None, 16 : 16 + heads, :rels],
    )


def per_device(
    inputs,
    cotangent,
    segments,
    row_widths,
    w_qkv,
    w_out,
    w_fc1,
    w_fc2,
    norm_gains,
    bias_rows,
    fc1_bias,
    rel_table,
):
    micro, _, slots, width = inputs.shape
    weights = (w_qkv, w_out, w_fc1, w_fc2, norm_gains, bias_rows, fc1_bias, rel_table)
    run = run_whole if lax.axis_size("batch") == 16 else run_plain
    activation, grad_in, *grads = run(
        inputs.reshape(micro * slots, width),
        cotangent.reshape(micro * slots, width),
        segments.reshape(micro, slots),
        row_widths.reshape(micro, row_widths.shape[2]),
        weights,
    )
    shape = (1, micro, 1, slots, width)
    return (activation.reshape(shape), grad_in.reshape(shape), *grads)


def solution(mesh):
    return jax.shard_map(
        per_device,
        mesh=mesh,
        in_specs=(
            P(None, "batch", None, None),
            P(None, "batch", None, None),
            P(None, "batch", None),
            P(None, "batch", None),
            P("section", None, None),
            P("section", None, None),
            P("section", None, None),
            P("section", None, None),
            P("section", None, None),
            P("section", None, None),
            P("section", None),
            P("section", None, None),
        ),
        out_specs=(
            P("section", None, "batch", None, None),
            P("section", None, "batch", None, None),
            P("section", "batch", None),
            P("section", "batch", None),
            P("section", "batch", None),
            P("section", "batch", None),
            P("section", None, None),
            P("section", None, None),
            P("section", None),
            P("section", None, None),
        ),
        check_vma=False,
    )
```
